128 devices in a mesh: gx: 4 (over x_lo, core), gy: 4 (over z), gz: 8 (over y, x_hi).
Axes of the slice: x: 4 (x_hi: 2, x_lo: 2; x = x_hi * 2 + x_lo), y: 4, z: 4, core: 2. Of those that a mesh axis runs over, the one named last changes fastest.
Arguments:
- basis_vectors: float32 [8, 64, 64, 1024], P(None, 'gx', 'gy', 'gz'), may hold values from -30 to 30
- diffusion: float32 [64, 64, 1024], P('gx', 'gy', 'gz'), may hold values from 0.1 to 1
- reaction: float32 [64, 64, 1024], P('gx', 'gy', 'gz'), may hold values from 0.002 to 0.02
Outputs:
- next_vector: float32 [64, 64, 1024], P('gx', 'gy', 'gz')
- coefficients: float32 [9], replicated
The draws below stay inside these ranges and needn't reach their ends.
All inputs are finite; a program needn't handle non-finite values.
Results may differ from the reference program's by a relative error of at most 0.00027.
Values sent between devices are 32-bit elements; how exact they have to be, the bound alone decides.
No kernel may reach another device: no remote copies, remote signals or barrier semaphores. Data moves between devices by JAX's collectives and lax.ppermute only.
A program may use at most 256 MiB of HBM per device.

```python
import math
import jax
import jax.numpy as jnp
from jax import lax

BASIS = 8
LEVELS = 4
DEGREE = 4
COARSE_DEGREE = 8
CYCLES = 2
NX = 64
NY = 64
NZ = 1024


def draw_basis_vectors(key, part):
    key = jax.random.fold_in(key, 7)
    subkeys = jax.random.split(key, 4)
    cell_scale = jnp.exp(jax.random.uniform(subkeys[2], (NX, NY, NZ), jnp.float32, math.log(0.3), math.log(3.0)))
    mixing = jax.random.uniform(subkeys[3], (BASIS, 1, 1, 1), jnp.float32, -0.6, 0.6)
    common = jax.random.truncated_normal(subkeys[0], -4.0, 4.0, (NX, NY, NZ), jnp.float32)
    rough_part = jax.random.truncated_normal(subkeys[1], -4.0, 4.0, (BASIS, NX, NY, NZ), jnp.float32)
    return (mixing * common * cell_scale + 0.8 * rough_part).astype(jnp.float32)


def steps_of(rng, dims, cuts, smallest, high):
    gain, own = 1.0, jax.random.fold_in(rng, 6)
    for axis_at, shards_of in cuts:
        heights = jnp.exp(jax.random.uniform(jax.random.fold_in(own, axis_at), (shards_of,), jnp.float32, smallest / len(cuts), high / len(cuts)))
        gain = gain * jnp.repeat(heights, dims[axis_at] // shards_of).reshape([-1 if axis == axis_at else 1 for axis in range(len(dims))])
    return gain


def setup_inputs(seed: int = 0) -> dict:
    seeds = jax.random.split(jax.random.key(seed), 4)
    return {
        "basis_vectors": draw_basis_vectors(jax.random.fold_in(seeds[3], 71), 0),
        "diffusion": jnp.clip(jnp.exp(math.log(1.0) - 2.3025851 * jax.random.uniform(seeds[1], (NX, NY, NZ), jnp.float32) ** steps_of(seeds[1], (NX, NY, NZ), ((0, 4), (1, 4), (2, 8)), -0.2, 0.2)), 0.1, 1.0),
        "reaction": jnp.clip(jnp.exp(math.log(0.02) - 2.30258502 * jax.random.uniform(seeds[2], (NX, NY, NZ), jnp.float32) ** steps_of(seeds[2], (NX, NY, NZ), ((0, 4), (1, 4), (2, 8)), -0.2, 0.2)), 0.002, 0.02),
    }


UPPER_BOUND = 2.0
SMOOTH_LOW = 0.25
COARSE_LOW = 0.05
AXIS_PULL = (1.0, 0.5, 2.0)
HIGHEST = lax.Precision.HIGHEST

def stencil_table():
    entries = []
    for shift_x in (-1, 0, 1):
        for shift_y in (-1, 0, 1):
            for shift_z in (-1, 0, 1):
                picked = [AXIS_PULL[axis_index] for axis_index, offset in enumerate((shift_x, shift_y, shift_z)) if offset != 0]
                if len(picked) == 1:
                    weight = picked[0]
                elif len(picked) == 2:
                    weight = (picked[0] + picked[1]) / 8.0
                elif len(picked) == 3:
                    weight = (picked[0] + picked[1] + picked[2]) / 24.0
                else:
                    continue
                entries.append((shift_x, shift_y, shift_z, weight))
    return entries

def window(padded, shift_x, shift_y, shift_z, extent):
    return padded[1 + shift_x:1 + shift_x + extent[0], 1 + shift_y:1 + shift_y + extent[1], 1 + shift_z:1 + shift_z + extent[2]]

def diagonal_of(reaction, padded_diff):
    extent = reaction.shape
    center = padded_diff[1:-1, 1:-1, 1:-1]
    summed = reaction
    for shift_x, shift_y, shift_z, weight in stencil_table():
        summed = summed + 0.5 * weight * (center + window(padded_diff, shift_x, shift_y, shift_z, extent))
    return summed

def apply_operator(padded_field, padded_diff, diagonal):
    extent = diagonal.shape
    center = padded_diff[1:-1, 1:-1, 1:-1]
    summed = diagonal * padded_field[1:-1, 1:-1, 1:-1]
    for shift_x, shift_y, shift_z, weight in stencil_table():
        beside = window(padded_diff, shift_x, shift_y, shift_z, extent)
        summed = summed - 0.5 * weight * (center + beside) * window(padded_field, shift_x, shift_y, shift_z, extent)
    return summed

def chebyshev(right_side, start, operate, diagonal, degree, lower):
    middle = 0.5 * (UPPER_BOUND + lower)
    radius = 0.5 * (UPPER_BOUND - lower)
    spread_ratio = middle / radius
    inverse = 1.0 / diagonal
    if start is None:
        solved = jnp.zeros_like(right_side)
        residual_now = right_side
    else:
        solved = start
        residual_now = right_side - operate(start)
    direction = inverse * residual_now / middle
    rho_now = 1.0 / spread_ratio
    for turn_index in range(degree):
        solved = solved + direction
        if turn_index + 1 < degree:
            residual_now = residual_now - operate(direction)
            rho_next = 1.0 / (2.0 * spread_ratio - rho_now)
            direction = rho_next * rho_now * direction + 2.0 * rho_next / radius * inverse * residual_now
            rho_now = rho_next
    return solved

def restrict(grid_field):
    extent = grid_field.shape
    return grid_field.reshape(extent[0] // 2, 2, extent[1] // 2, 2, extent[2] // 2, 2).sum(axis=(1, 3, 5))

def prolong(grid_field):
    extent = grid_field.shape
    expanded = jnp.broadcast_to(grid_field[:, None, :, None, :, None], (extent[0], 2, extent[1], 2, extent[2], 2))
    return expanded.reshape(2 * extent[0], 2 * extent[1], 2 * extent[2])

def build_levels(reaction, diffusion):
    levels = []
    for level_index in range(LEVELS):
        padded = jnp.pad(diffusion, 1)
        levels.append((padded, diagonal_of(reaction, padded)))
        if level_index + 1 < LEVELS:
            reaction = restrict(reaction)
            diffusion = 0.25 * restrict(diffusion)
    return levels

def vcycle(level_index, right_side, levels):
    padded_diff, diagonal = levels[level_index]

    def operate(grid_field):
        return apply_operator(jnp.pad(grid_field, 1), padded_diff, diagonal)
    if level_index == LEVELS - 1:
        return chebyshev(right_side, None, operate, diagonal, COARSE_DEGREE, COARSE_LOW)
    smoothed = chebyshev(right_side, None, operate, diagonal, DEGREE, SMOOTH_LOW)
    coarse = vcycle(level_index + 1, restrict(right_side - operate(smoothed)), levels)
    return chebyshev(right_side, smoothed + prolong(coarse), operate, diagonal, DEGREE, SMOOTH_LOW)

def reference(basis_vectors, diffusion, reaction):
    levels = build_levels(reaction, diffusion)
    source = basis_vectors[BASIS - 1]
    padded_diff, diagonal = levels[0]
    applied = vcycle(0, source, levels)
    for repeat_index in range(CYCLES - 1):
        remainder = source - apply_operator(jnp.pad(applied, 1), padded_diff, diagonal)
        applied = applied + vcycle(0, remainder, levels)
    cell_count = float(NX * NY * NZ)
    gram_sums = jnp.tensordot(basis_vectors, basis_vectors, axes=((1, 2, 3), (1, 2, 3)), precision=HIGHEST)
    coeff_one = jnp.tensordot(basis_vectors, applied, axes=3, precision=HIGHEST) / cell_count
    first_pass = applied - jnp.tensordot(coeff_one, basis_vectors, axes=1, precision=HIGHEST)
    proj_two = jnp.tensordot(basis_vectors, first_pass, axes=3, precision=HIGHEST)
    squares = jnp.sum(first_pass * first_pass)
    coeff_two = proj_two / cell_count
    second_pass = first_pass - jnp.tensordot(coeff_two, basis_vectors, axes=1, precision=HIGHEST)
    quadratic = jnp.dot(coeff_two, jnp.dot(gram_sums, coeff_two, precision=HIGHEST), precision=HIGHEST)
    mean_square = (squares - 2.0 * jnp.dot(coeff_two, proj_two, precision=HIGHEST) + quadratic) / cell_count
    length = jnp.sqrt(mean_square + 1e-06)
    return (second_pass / length, jnp.concatenate([coeff_one + coeff_two, length[None]]))
```

```python
import numpy as np
import jax
import jax.numpy as jnp
from jax import lax
from jax.experimental import pallas as pl
from jax.experimental.pallas import tpu as pltpu
from jax.sharding import PartitionSpec as P

AXES = ("gx", "gy", "gz")
DEGREE = 4
COARSE_DEGREE = 8
UPPER_BOUND = 2.0
SMOOTH_LOW = 0.25
COARSE_LOW = 0.05
PULL = (1.0, 0.5, 2.0)
WX, WY, WZ = PULL
WXY = (WX + WY) / 8.0
WXZ = (WX + WZ) / 8.0
WYZ = (WY + WZ) / 8.0
WXYZ = (WX + WY + WZ) / 24.0
WEIGHT_SUM = 2.0 * (WX + WY + WZ) + 4.0 * (WXY + WXZ + WYZ) + 8.0 * WXYZ
LANES = 128
SLABS = 128
CELLS = 64.0 * 64.0 * 1024.0
F32 = jnp.float32
BF16 = jnp.bfloat16
VMEM_LIMIT = 56 * 1024 * 1024

WIDTHS = (64, 32, 16, 8)


def slab_in_group(x_lo, z, odd):
    turned = z + odd * (3 - 2 * z)
    return 2 * turned + (x_lo + z + 1) % 2


def device_order():
    order = [0] * SLABS
    for gx in range(4):
        for gy in range(4):
            for gz in range(8):
                slab = 16 * gz + 2 * slab_in_group(gx // 2, gy, gz % 2) + gx % 2
                order[slab] = (gx * 4 + gy) * 8 + gz
    return order


ORDER = device_order()
CORE_SWAP = [(ORDER[s], ORDER[s ^ 1]) for s in range(SLABS)]
CHIP_SWAP = [(ORDER[s], ORDER[(s + 1 if s % 2 else s - 1) % SLABS]) for s in range(SLABS)]


def fine_to_coarse(level):
    width = WIDTHS[level]
    planes = LANES // width
    table = np.zeros((4, LANES, LANES), np.float32)
    for pack in range(4):
        for lane in range(LANES):
            z, y = divmod(lane, width)
            table[pack, lane, ((pack * planes + z) // 2) * (width // 2) + y // 2] = 1.0
    return table.reshape(4 * LANES, LANES)


def block_to_slab():
    table = np.zeros((512, 512), np.float32)
    for gy in range(4):
        for z in range(8):
            for y in range(16):
                table[gy * 128 + z * 16 + y, (z // 2) * 128 + (z % 2) * 64 + gy * 16 + y] = 1.0
    return table


RESTRICT = [fine_to_coarse(level) for level in range(3)]
TO_SLAB = block_to_slab()


def exact_dot(a, table):
    total = None
    rest = a
    for _ in range(3):
        part = rest.astype(BF16)
        rest = rest - part.astype(F32)
        term = jnp.dot(part, table, preferred_element_type=F32)
        total = term if total is None else total + term
    return total


def masks(rows, width):
    lane = lax.broadcasted_iota(jnp.int32, (rows, LANES), 1)
    row = lax.broadcasted_iota(jnp.int32, (rows, LANES), 0)
    y = lane % width
    seg = lane // width
    return (
        y == 0,
        y == width - 1,
        seg == 0,
        seg == LANES // width - 1,
        row == 0,
        row == rows - 1,
    )


def spread(before, here, after, width, mask):
    y_first, y_last, z_first, z_last, x_first, x_last = mask
    zero = jnp.zeros_like(here)
    if width == 64:
        zs = pltpu.roll(here + jnp.where(z_first, after, before), 64, 1)
    else:
        zs = pltpu.roll(jnp.where(z_first, after, here), LANES - width, 1) + pltpu.roll(
            jnp.where(z_last, before, here), width, 1
        )

    def ysum(a):
        return jnp.where(y_last, zero, pltpu.roll(a, LANES - 1, 1)) + jnp.where(
            y_first, zero, pltpu.roll(a, 1, 1)
        )

    ys = ysum(here)
    yz = ysum(zs)
    middle = WY * ys + WZ * zs + WYZ * yz
    side = WX * here + WXY * ys + WXZ * zs + WXYZ * yz
    rows = here.shape[0]
    return (
        middle
        + jnp.where(x_last, zero, pltpu.roll(side, rows - 1, 0))
        + jnp.where(x_first, zero, pltpu.roll(side, 1, 0))
    )


def operate(k, u, du, diff, diag, width, mask):
    s_u = spread(u[k - 1], u[k], u[k + 1], width, mask)
    s_du = spread(du[k - 1], du[k], du[k + 1], width, mask)
    return diag[k] * u[k] - 0.5 * (diff[k] * s_u + s_du)


def over(lo, hi, body):
    def step(k, carry):
        body(k)
        return carry

    lax.fori_loop(lo, hi, step, 0)


class Level:
    def __init__(self, index, diff, diag, inv, side, x, r, q, dq):
        self.width = WIDTHS[index]
        self.rows = WIDTHS[index]
        self.diff, self.diag, self.inv, self.side = diff, diag, inv, side
        self.x, self.r, self.q, self.dq = x, r, q, dq
        self.mask = masks(self.rows, self.width)

    def set_diagonal(self, lo, hi, reaction):
        def body(k):
            d = self.diff[k]
            s = spread(self.diff[k - 1], d, self.diff[k + 1], self.width, self.mask)
            diag = reaction[k] + 0.5 * (WEIGHT_SUM * d + s)
            self.diag[k] = diag
            self.inv[k] = jnp.where(d > 0.0, 1.0 / diag, 0.0)

        over(lo, hi, body)

    def residual(self, lo, hi, out, u, du):
        def body(k):
            out[k] = self.side[k] - operate(k, u, du, self.diff, self.diag, self.width, self.mask)

        over(lo, hi, body)

    def smooth(self, ranges, degree, lower, fresh, keep):
        middle = 0.5 * (UPPER_BOUND + lower)
        radius = 0.5 * (UPPER_BOUND - lower)
        ratio = middle / radius
        rho = 1.0 / ratio

        def first(k):
            r = self.side[k] if fresh else self.r[k]
            if fresh:
                self.r[k] = r
            q = self.inv[k] * r * (1.0 / middle)
            self.q[0][k] = q
            self.dq[0][k] = self.diff[k] * q
            self.x[k] = q if fresh else self.x[k] + q

        over(ranges[0][0], ranges[0][1], first)
        now = 0
        for turn in range(1, degree):
            rho_next = 1.0 / (2.0 * ratio - rho)
            a, b = rho_next * rho, 2.0 * rho_next / radius
            rho = rho_next
            last = turn == degree - 1
            u, du, v, dv = self.q[now], self.dq[now], self.q[1 - now], self.dq[1 - now]

            def body(k, u=u, du=du, v=v, dv=dv, a=a, b=b, last=last):
                r = self.r[k] - operate(k, u, du, self.diff, self.diag, self.width, self.mask)
                q = a * u[k] + b * (self.inv[k] * r)
                x = self.x[k] + q
                self.x[k] = x
                if last:
                    if keep:
                        dv[k] = self.diff[k] * x
                else:
                    self.r[k] = r
                    v[k] = q
                    dv[k] = self.diff[k] * q

            over(ranges[turn][0], ranges[turn][1], body)
            now = 1 - now
        return self.dq[now]


def paired_rows(ref, k, rows):
    return ref[k, pl.ds(0, rows // 2, 2), :] + ref[k, pl.ds(1, rows // 2, 2), :]


def restricted(ref, k, rows, table):
    wide = jnp.concatenate([paired_rows(ref, k + j, rows) for j in range(4)], axis=1)
    return exact_dot(wide, table[...])


def add_prolonged(level, k, coarse, table_t, j, dx):
    rows = level.rows
    fine = exact_dot(coarse, table_t[j * LANES : (j + 1) * LANES].T)
    for half in range(2):
        at = pl.ds(half, rows // 2, 2)
        x = level.x[k, at, :] + fine
        level.x[k, at, :] = x
        dx[k, at, :] = level.diff[k, at, :] * x


W0 = 30
W1 = 9
W2 = 34
W3 = 10
C0 = 10
SMEM = pl.BlockSpec(memory_space=pltpu.SMEM)
VM = pl.BlockSpec(memory_space=pltpu.VMEM)


def call(kernel, outs, scratch, *args, scalars=0):
    return pl.pallas_call(
        kernel,
        out_shape=[jax.ShapeDtypeStruct(s, F32) for s in outs],
        in_specs=[SMEM] * scalars + [VM] * (len(args) - scalars),
        out_specs=[VM] * len(outs),
        scratch_shapes=[pltpu.VMEM(s, F32) for s in scratch],
        compiler_params=pltpu.CompilerParams(vmem_limit_bytes=VMEM_LIMIT),
    )(*args)


def unpack_kernel(received, table, own):
    fields = own.shape[0]
    for f in range(fields):
        rows = []
        for gx in range(4):
            rows.append(jnp.concatenate([received[gx * 4 + gy, f] for gy in range(4)], axis=1))
        wide = exact_dot(jnp.concatenate(rows, axis=0), table[...])
        for k in range(4):
            own[f, k] = wide[:, k * LANES : (k + 1) * LANES]


def assemble(place, pieces, field, window):
    slab, core = place[0], place[1]
    sign = 1 - 2 * core
    zero = jnp.zeros((64, LANES), F32)
    window[0] = zero
    window[W0 - 1] = zero
    for side, distance, ref, base in pieces:
        slot = 3 + side * sign * distance
        inside = jnp.logical_and(slab + slot - 3 >= 0, slab + slot - 3 < SLABS)
        for k in range(4):
            value = ref[base + field, k]
            window[1 + 4 * slot + k] = jnp.where(inside, value, 0.0)


def down_level0(level, level1, table0):
    dx = level.smooth([(1, 29), (2, 28), (2, 28), (3, 27)], DEGREE, SMOOTH_LOW, True, True)
    level.residual(4, 26, level.r, level.x, dx)
    zero = jnp.zeros((32, LANES), F32)
    level1.side[0] = zero
    level1.side[8] = zero
    for t in range(7):
        level1.side[1 + t] = restricted(level.r, 1 + 4 * t, 64, table0)


def down_level1(level, table1):
    for ref in level.q + level.dq:
        ref[...] = jnp.zeros_like(ref)
    dx = level.smooth([(1, 8), (2, 7), (2, 7), (2, 7)], DEGREE, SMOOTH_LOW, True, True)
    level.residual(4, 5, level.r, level.x, dx)
    own = paired_rows(level.r, 4, 32)
    return exact_dot(own, table1[0:LANES])


def keep_centre(level, level1, centre, kept1):
    for i, ref in enumerate((level.x, level.side, level.diff, level.diag, level.inv)):
        for k in range(8):
            centre[i, 1 + k] = ref[11 + k]
        centre[i, 0] = jnp.zeros((64, LANES), F32)
        centre[i, 9] = jnp.zeros((64, LANES), F32)
    for i, ref in enumerate((level1.x, level1.side, level1.diff, level1.diag, level1.inv)):
        kept1[i] = ref[...]


def clear(*refs):
    for ref in refs:
        ref[...] = jnp.zeros_like(ref)


def down_first_kernel(
    place, own, mate, near, far, near3, table0, table1,
    full, full1, centre, kept1, packet,
    react, react1, x, r, qa, qb, da, db, side1, x1, r1, q1a, q1b, d1a, d1b,
):
    clear(full.at[2], full.at[3], x, r, qa, qb, da, db, x1, r1, full1, react1)
    pieces = [
        (-1, 0, own, 0), (-1, 1, near, 0), (-1, 2, near, 3), (-1, 3, near3, 0),
        (1, 1, mate, 0), (1, 2, far, 0), (1, 3, far, 3),
    ]
    assemble(place, pieces, 0, full.at[0])
    assemble(place, pieces, 1, full.at[1])
    assemble(place, pieces, 2, react)
    level = Level(0, full.at[1], full.at[2], full.at[3], full.at[0], x, r, [qa, qb], [da, db])
    level1 = Level(
        1, full1.at[0], full1.at[1], full1.at[2], side1, x1, r1, [q1a, q1b], [d1a, d1b]
    )
    level.set_diagonal(1, 29, react)
    for t in range(7):
        level1.diff[1 + t] = 0.25 * restricted(level.diff, 1 + 4 * t, 64, table0)
        react1[1 + t] = restricted(react, 1 + 4 * t, 64, table0)
    level1.set_diagonal(1, 8, react1)
    down_level0(level, level1, table0)
    rhs2 = down_level1(level1, table1)
    diff2 = 0.25 * exact_dot(paired_rows(level1.diff, 4, 32), table1[0:LANES])
    react2 = exact_dot(paired_rows(react1, 4, 32), table1[0:LANES])
    packet[...] = rhs2 + pltpu.roll(diff2, 32, 1) + pltpu.roll(react2, 64, 1)
    keep_centre(level, level1, centre, kept1)


def down_second_kernel(
    place, own, mate, near, far, near3, full, full1, table0, table1,
    centre, kept1, packet,
    window, dwin, side, x, r, qa, qb, da, db, side1, x1, r1, q1a, q1b, d1a, d1b,
):
    clear(side, x, r, qa, qb, da, db, x1, r1)
    pieces = [
        (-1, 0, own, 0), (-1, 1, near, 0), (-1, 2, near, 1), (-1, 3, near3, 0),
        (1, 1, mate, 0), (1, 2, far, 0), (1, 3, far, 1),
    ]
    assemble(place, pieces, 0, window)
    dwin[...] = window[...] * full[1]
    source = Level(0, full.at[1], full.at[2], full.at[3], full.at[0], x, r, [qa, qb], [da, db])
    source.residual(1, 29, side, window, dwin)
    level = Level(0, full.at[1], full.at[2], full.at[3], side, x, r, [qa, qb], [da, db])
    level1 = Level(
        1, full1.at[0], full1.at[1], full1.at[2], side1, x1, r1, [q1a, q1b], [d1a, d1b]
    )
    down_level0(level, level1, table0)
    packet[...] = down_level1(level1, table1)
    keep_centre(level, level1, centre, kept1)


def gather_level2(packets, at, target):
    lane = lax.broadcasted_iota(jnp.int32, (16, LANES), 1) // 32
    zero = jnp.zeros((16, LANES), F32)
    target[0] = zero
    target[W2 - 1] = zero
    for pack in range(32):
        total = zero
        for j in range(4):
            piece = packets[ORDER[4 * pack + j]]
            shift = (32 * j - at) % LANES
            if shift:
                piece = pltpu.roll(piece, shift, 1)
            total = jnp.where(lane == j, piece, total)
        target[1 + pack] = total


def coarse_part(first, packets, lv2, lv3, f2, f3, react2, react3, work2, work3, table1, table2):
    x2, r2, q2a, q2b, d2a, d2b = work2
    x3, r3, q3a, q3b, d3a, d3b = work3
    clear(*work2)
    clear(*work3)
    gather_level2(packets, 0, f2)
    level2 = Level(2, lv2.at[0], lv2.at[1], lv2.at[2], f2, x2, r2, [q2a, q2b], [d2a, d2b])
    level3 = Level(3, lv3.at[0], lv3.at[1], lv3.at[2], f3, x3, r3, [q3a, q3b], [d3a, d3b])
    clear(f3)
    if first:
        clear(lv2.at[1], lv2.at[2], lv3, react3)
        gather_level2(packets, 32, lv2.at[0])
        gather_level2(packets, 64, react2)
        level2.set_diagonal(1, 33, react2)
        for t in range(8):
            level3.diff[1 + t] = 0.25 * restricted(level2.diff, 1 + 4 * t, 16, table2)
            react3[1 + t] = restricted(react2, 1 + 4 * t, 16, table2)
        level3.set_diagonal(1, 9, react3)
    whole2 = [(1, 33)] * 4
    dx = level2.smooth(whole2, DEGREE, SMOOTH_LOW, True, True)
    level2.residual(1, 33, r2, x2, dx)
    for t in range(8):
        f3[1 + t] = restricted(r2, 1 + 4 * t, 16, table2)
    level3.smooth([(1, 9)] * 8, COARSE_DEGREE, COARSE_LOW, True, False)
    for t in range(8):
        for j in range(4):
            add_prolonged(level2, 1 + 4 * t + j, x3[1 + t], table2, j, dx)
    level2.residual(1, 33, r2, x2, dx)
    level2.smooth(whole2, DEGREE, SMOOTH_LOW, False, False)
    return x2


def up_part(place, x2, spaced, centre, kept1, work0, work1, table0, table1):
    r, qa, qb, da, db = work0
    r1, q1a, q1b, d1a, d1b = work1
    clear(*work0)
    clear(*work1)
    slab = place[0]
    spaced[0:3] = jnp.zeros((3, 16, LANES), F32)
    spaced[SLABS + 3 : SLABS + 6] = jnp.zeros((3, 16, LANES), F32)
    for pack in range(32):
        value = x2[1 + pack]
        for j in range(4):
            spaced[3 + 4 * pack + j] = pltpu.roll(value, (LANES - 32 * j) % LANES, 1) if j else value
    level1 = Level(
        1, kept1.at[2], kept1.at[3], kept1.at[4], kept1.at[1], kept1.at[0], r1,
        [q1a, q1b], [d1a, d1b],
    )
    level = Level(
        0, centre.at[2], centre.at[3], centre.at[4], centre.at[1], centre.at[0], r,
        [qa, qb], [da, db],
    )
    for t in range(1, 6):
        add_prolonged(level1, 1 + t, spaced[slab + t], table1, 0, d1b)
    level1.residual(2, 7, r1, level1.x, d1b)
    level1.smooth([(2, 7), (3, 6), (3, 6), (3, 6)], DEGREE, SMOOTH_LOW, False, False)
    for k in range(8):
        t, j = divmod(10 + k, 4)
        add_prolonged(level, 1 + k, level1.x[1 + t], table0, j, db)
    level.residual(1, 9, r, level.x, db)
    level.smooth([(1, 9), (2, 8), (2, 8), (3, 7)], DEGREE, SMOOTH_LOW, False, False)


def up_first_kernel(place, packets, centre_in, kept1_in, table0, table1, table2, applied, lv2, lv3, *scratch):
    f2, f3, react2, react3 = scratch[0:4]
    work2, work3 = scratch[4:10], scratch[10:16]
    work0, work1 = scratch[16:21], scratch[21:26]
    spaced, centre, kept1 = scratch[26:29]
    centre[...] = centre_in[...]
    kept1[...] = kept1_in[...]
    x2 = coarse_part(
        True, packets, lv2, lv3, f2, f3, react2, react3, work2, work3, table1, table2
    )
    up_part(place, x2, spaced, centre, kept1, work0, work1, table0, table1)
    for k in range(4):
        applied[0, k] = centre[0, 3 + k]


def up_second_kernel(
    place, packets, centre_in, kept1_in, lv2, lv3, before, table0, table1, table2, to_block, out, *scratch
):
    f2, f3, react2, react3 = scratch[0:4]
    work2, work3 = scratch[4:10], scratch[10:16]
    work0, work1 = scratch[16:21], scratch[21:26]
    spaced, centre, kept1 = scratch[26:29]
    centre[...] = centre_in[...]
    kept1[...] = kept1_in[...]
    x2 = coarse_part(
        False, packets, lv2, lv3, f2, f3, react2, react3, work2, work3, table1, table2
    )
    up_part(place, x2, spaced, centre, kept1, work0, work1, table0, table1)
    wide = jnp.concatenate([before[0, k] + centre[0, 3 + k] for k in range(4)], axis=1)
    pieces = exact_dot(wide, to_block[...])
    for gx in range(4):
        for gy in range(4):
            out[gx * 4 + gy] = pieces[gx * 16 : (gx + 1) * 16, gy * LANES : (gy + 1) * LANES]


def row_of_sums(rows):
    stacked = jnp.concatenate(
        [jnp.sum(jnp.sum(a, axis=0), axis=0, keepdims=True) for a in rows], axis=0
    )
    totals = jnp.sum(stacked, axis=1, keepdims=True)
    n = len(rows)
    lane = lax.broadcasted_iota(jnp.int32, (n, LANES), 1)
    row = lax.broadcasted_iota(jnp.int32, (n, LANES), 0)
    return jnp.sum(jnp.where(lane == row, totals, 0.0), axis=0, keepdims=True)


def sums_one_kernel(basis, applied, out):
    rows = [basis[k] * applied[...] for k in range(8)]
    rows += [basis[j] * basis[k] for j in range(8) for k in range(j, 8)]
    out[...] = row_of_sums(rows)


def sums_two_kernel(coeff, basis, applied, first, out):
    value = applied[...]
    for k in range(8):
        value = value - coeff[k] * basis[k]
    first[...] = value
    out[...] = row_of_sums([basis[k] * value for k in range(8)] + [value * value])


def finish_kernel(coeff, basis, first, out):
    value = first[...] * coeff[8]
    for k in range(8):
        value = value - coeff[k] * basis[k]
    out[...] = value


def everywhere(x):
    return lax.all_to_all(jnp.broadcast_to(x[None], (SLABS,) + x.shape), AXES, 0, 0, tiled=True)


def halo(own):
    mate = lax.ppermute(own, AXES, CORE_SWAP)
    near = lax.ppermute(jnp.concatenate([own, mate], axis=0), AXES, CHIP_SWAP)
    far = lax.ppermute(near, AXES, CORE_SWAP)
    near3 = lax.ppermute(far[: own.shape[0]], AXES, CHIP_SWAP)
    return mate, near, far, near3


def local(basis, diffusion, reaction):
    gx, gy, gz = (lax.axis_index(a) for a in AXES)
    odd = gz % 2
    core = gx % 2
    slab = 16 * gz + 2 * slab_in_group(gx // 2, gy, odd) + core
    place = jnp.stack([slab, core]).astype(jnp.int32)
    table0, table1, table2 = (jnp.asarray(t, BF16) for t in RESTRICT)
    to_slab = jnp.asarray(TO_SLAB, BF16)
    to_block = jnp.asarray(TO_SLAB.T, BF16)
    takes = [
        [2 * slab_in_group(a // 2, b, parity) + a % 2 for a in range(4) for b in range(4)]
        for parity in (0, 1)
    ]

    fields = jnp.stack([basis[7], diffusion, reaction])
    parts = fields.reshape(3, 16, 16, 16, 8).transpose(3, 0, 1, 4, 2).reshape(16, 3, 16, LANES)
    parts = jnp.where(
        odd == 1,
        jnp.stack([parts[i] for i in takes[1]]),
        jnp.stack([parts[i] for i in takes[0]]),
    )
    received = lax.all_to_all(parts, ("gx", "gy"), 0, 0, tiled=True)
    (own,) = call(unpack_kernel, [(3, 4, 64, LANES)], [], received, to_slab)

    big = (W0, 64, LANES)
    small = (W1, 32, LANES)
    two = (W2, 16, LANES)
    three = (W3, 8, LANES)
    mid = (10, 64, LANES)
    full, full1, centre, kept1, packet = call(
        down_first_kernel,
        [(4,) + big, (3,) + small, (5,) + mid, (5,) + small, (16, LANES)],
        [big, small] + [big] * 6 + [small] * 7,
        place, own, *halo(own), table0, table1, scalars=1,
    )
    coarse_scratch = (
        [two, three, two, three]
        + [two] * 6
        + [three] * 6
        + [mid] * 5
        + [small] * 5
        + [(SLABS + 6, 16, LANES), (5,) + mid, (5,) + small]
    )
    applied, lv2, lv3 = call(
        up_first_kernel,
        [(1, 4, 64, LANES), (3,) + two, (3,) + three],
        coarse_scratch,
        place, everywhere(packet), centre, kept1, table0, table1, table2, scalars=1,
    )
    centre, kept1, packet = call(
        down_second_kernel,
        [(5,) + mid, (5,) + small, (16, LANES)],
        [big] * 9 + [small] * 7,
        place, applied, *halo(applied), full, full1, table0, table1, scalars=1,
    )
    (out,) = call(
        up_second_kernel,
        [(16, 16, LANES)],
        coarse_scratch,
        place, everywhere(packet), centre, kept1, lv2, lv3, applied,
        table0, table1, table2, to_block, scalars=1,
    )
    back = lax.all_to_all(out, ("gx", "gy"), 0, 0, tiled=True)
    inverse = [[t.index(p) for p in range(16)] for t in takes]
    back = jnp.where(
        odd == 1,
        jnp.stack([back[i] for i in inverse[1]]),
        jnp.stack([back[i] for i in inverse[0]]),
    )
    applied = back.reshape(16, 16, 8, 16).transpose(1, 3, 0, 2).reshape(16, 16, LANES)

    (part,) = call(sums_one_kernel, [(1, LANES)], [], basis, applied)
    sums = everywhere(part).sum(axis=(0, 1))
    coeff_one = sums[0:8] / CELLS
    upper = {}
    at = 8
    for j in range(8):
        for k in range(j, 8):
            upper[j, k] = upper[k, j] = at
            at += 1
    gram = jnp.stack([jnp.stack([sums[upper[j, k]] for k in range(8)]) for j in range(8)])
    first, part = call(
        sums_two_kernel, [(16, 16, LANES), (1, LANES)], [], coeff_one, basis, applied, scalars=1
    )
    sums = everywhere(part).sum(axis=(0, 1))
    proj_two, squares = sums[0:8], sums[8]
    coeff_two = proj_two / CELLS
    quadratic = jnp.sum(coeff_two * jnp.sum(gram * coeff_two[None, :], axis=1))
    mean_square = (squares - 2.0 * jnp.sum(coeff_two * proj_two) + quadratic) / CELLS
    length = jnp.sqrt(mean_square + 1e-06)
    (next_vector,) = call(
        finish_kernel,
        [(16, 16, LANES)],
        [],
        jnp.concatenate([coeff_two / length, (1.0 / length)[None]]),
        basis,
        first,
        scalars=1,
    )
    return next_vector, jnp.concatenate([coeff_one + coeff_two, length[None]])


def solution(mesh):
    placed = (P(None, "gx", "gy", "gz"), P("gx", "gy", "gz"), P("gx", "gy", "gz"))
    return jax.shard_map(
        local, mesh=mesh, in_specs=placed, out_specs=(P("gx", "gy", "gz"), P()), check_vma=False
    )
```

```python
import numpy as np
import jax
import jax.numpy as jnp
from jax import lax
from jax.experimental import pallas as pl
from jax.experimental.pallas import tpu as pltpu
from jax.sharding import PartitionSpec as P

AXES = ("gx", "gy", "gz")
DEGREE = 4
COARSE_DEGREE = 8
UPPER_BOUND = 2.0
SMOOTH_LOW = 0.25
COARSE_LOW = 0.05
PULL = (1.0, 0.5, 2.0)
WX, WY, WZ = PULL
WXY = (WX + WY) / 8.0
WXZ = (WX + WZ) / 8.0
WYZ = (WY + WZ) / 8.0
WXYZ = (WX + WY + WZ) / 24.0
WEIGHT_SUM = 2.0 * (WX + WY + WZ) + 4.0 * (WXY + WXZ + WYZ) + 8.0 * WXYZ
LANES = 128
SLABS = 128
CELLS = 64.0 * 64.0 * 1024.0
F32 = jnp.float32
BF16 = jnp.bfloat16
VMEM_LIMIT = 56 * 1024 * 1024

WIDTHS = (64, 32, 16, 8)


def slab_in_group(x_lo, z, odd):
    turned = z + odd * (3 - 2 * z)
    return 2 * turned + (x_lo + z + 1) % 2


def device_order():
    order = [0] * SLABS
    for gx in range(4):
        for gy in range(4):
            for gz in range(8):
                slab = 16 * gz + 2 * slab_in_group(gx // 2, gy, gz % 2) + gx % 2
                order[slab] = (gx * 4 + gy) * 8 + gz
    return order


ORDER = device_order()
CORE_SWAP = [(ORDER[s], ORDER[s ^ 1]) for s in range(SLABS)]
CHIP_SWAP = [(ORDER[s], ORDER[(s + 1 if s % 2 else s - 1) % SLABS]) for s in range(SLABS)]


def fine_to_coarse(level):
    width = WIDTHS[level]
    planes = LANES // width
    table = np.zeros((4, LANES, LANES), np.float32)
    for pack in range(4):
        for lane in range(LANES):
            z, y = divmod(lane, width)
            table[pack, lane, ((pack * planes + z) // 2) * (width // 2) + y // 2] = 1.0
    return table.reshape(4 * LANES, LANES)


def block_to_slab():
    table = np.zeros((512, 512), np.float32)
    for gy in range(4):
        for z in range(8):
            for y in range(16):
                table[gy * 128 + z * 16 + y, (z // 2) * 128 + (z % 2) * 64 + gy * 16 + y] = 1.0
    return table


def stencil_table(level):
    width = WIDTHS[level]
    planes = LANES // width
    weights = {
        (0, 1, 0): WY, (0, 0, 1): WZ, (0, 1, 1): WYZ,
        (1, 0, 0): WX, (1, 1, 0): WXY, (1, 0, 1): WXZ, (1, 1, 1): WXYZ,
    }
    table = np.zeros((2 * LANES, 2 * LANES), np.float32)
    for lane in range(LANES):
        z, y = divmod(lane, width)
        for dz in (-1, 0, 1):
            for dy in (-1, 0, 1):
                if not 0 <= y + dy < width:
                    continue
                outside = not 0 <= z + dz < planes
                source = outside * LANES + (z + dz) % planes * width + y + dy
                for dx in (0, 1):
                    if (dx, abs(dy), abs(dz)) in weights:
                        weight = round(48.0 * weights[dx, abs(dy), abs(dz)]) / 2.0
                        table[source, dx * LANES + lane] += weight
    return table


RESTRICT = [fine_to_coarse(level) for level in range(3)]
TO_SLAB = block_to_slab()
STENCIL = [stencil_table(level) for level in range(4)]


def table_dot(a, table, parts=2):
    total = None
    rest = a
    for part_number in range(parts):
        part = rest.astype(BF16)
        if part_number + 1 < parts:
            rest = rest - part.astype(F32)
        term = jnp.dot(part, table, preferred_element_type=F32)
        total = term if total is None else total + term
    return total


class Level:
    def __init__(self, index, table, diff, diag, inv, side, x, r, q, dq):
        self.width = self.rows = WIDTHS[index]
        self.table = table
        self.diff, self.diag, self.inv, self.side = diff, diag, inv, side
        self.x, self.r, self.q, self.dq = x, r, q, dq

    def get(self, ref, lo, hi):
        return ref[lo:hi].reshape((hi - lo) * self.rows, LANES)

    def put(self, ref, lo, hi, value):
        ref[lo:hi] = value.reshape(hi - lo, self.rows, LANES)

    def spread(self, ref, lo, hi):
        n = (hi - lo) * self.rows
        lane = lax.broadcasted_iota(jnp.int32, (n, LANES), 1)
        row = lax.broadcasted_iota(jnp.int32, (n, LANES), 0) % self.rows
        here = self.get(ref, lo, hi)
        beside = jnp.where(
            lane < self.width, self.get(ref, lo + 1, hi + 1), self.get(ref, lo - 1, hi - 1)
        )
        out = table_dot(jnp.concatenate([here, beside], axis=1), self.table[...])
        next_x = out[:, LANES:]
        return (
            out[:, :LANES]
            + jnp.where(row == self.rows - 1, 0.0, pltpu.roll(next_x, n - 1, 0))
            + jnp.where(row == 0, 0.0, pltpu.roll(next_x, 1, 0))
        )

    def operate(self, lo, hi, u, du):
        both = self.get(self.diff, lo, hi) * self.spread(u, lo, hi) + self.spread(du, lo, hi)
        return self.get(self.diag, lo, hi) * self.get(u, lo, hi) - (1.0 / 48.0) * both

    def set_diagonal(self, lo, hi, reaction):
        d = self.get(self.diff, lo, hi)
        diag = self.get(reaction, lo, hi) + (
            (0.5 * WEIGHT_SUM) * d + (1.0 / 48.0) * self.spread(self.diff, lo, hi)
        )
        self.put(self.diag, lo, hi, diag)
        self.put(self.inv, lo, hi, jnp.where(d > 0.0, 1.0 / diag, 0.0))

    def residual(self, lo, hi, out, u, du):
        self.put(out, lo, hi, self.get(self.side, lo, hi) - self.operate(lo, hi, u, du))

    def scale_x(self, lo, hi, out):
        self.put(out, lo, hi, self.get(self.diff, lo, hi) * self.get(self.x, lo, hi))

    def smooth(self, ranges, degree, lower, fresh, keep):
        middle = 0.5 * (UPPER_BOUND + lower)
        radius = 0.5 * (UPPER_BOUND - lower)
        ratio = middle / radius
        rho = 1.0 / ratio

        lo, hi = ranges[0]
        if fresh:
            r = self.get(self.side, lo, hi)
            self.put(self.r, lo, hi, r)
        else:
            r = self.get(self.r, lo, hi)
        q = self.get(self.inv, lo, hi) * r * (1.0 / middle)
        self.put(self.q[0], lo, hi, q)
        self.put(self.dq[0], lo, hi, self.get(self.diff, lo, hi) * q)
        self.put(self.x, lo, hi, q if fresh else self.get(self.x, lo, hi) + q)
        now = 0
        for turn in range(1, degree):
            rho_next = 1.0 / (2.0 * ratio - rho)
            a, b = rho_next * rho, 2.0 * rho_next / radius
            rho = rho_next
            u, du, v, dv = self.q[now], self.dq[now], self.q[1 - now], self.dq[1 - now]
            lo, hi = ranges[turn]
            r = self.get(self.r, lo, hi) - self.operate(lo, hi, u, du)
            q = a * self.get(u, lo, hi) + b * (self.get(self.inv, lo, hi) * r)
            x = self.get(self.x, lo, hi) + q
            self.put(self.x, lo, hi, x)
            if turn + 1 < degree:
                self.put(self.r, lo, hi, r)
                self.put(v, lo, hi, q)
                self.put(dv, lo, hi, self.get(self.diff, lo, hi) * q)
            elif keep:
                self.put(dv, lo, hi, self.get(self.diff, lo, hi) * x)
            now = 1 - now
        return self.dq[now]

    def row_pairs(self, ref, lo, hi):
        half = self.rows // 2
        return ref[lo:hi, pl.ds(0, half, 2), :] + ref[lo:hi, pl.ds(1, half, 2), :]

    def restricted(self, ref, lo, count, table):
        half = self.rows // 2
        pairs = self.row_pairs(ref, lo, lo + 4 * count).reshape(count, 4, half, LANES)
        wide = jnp.concatenate(
            [pairs[:, j].reshape(count * half, LANES) for j in range(4)], axis=1
        )
        return table_dot(wide, table[...]).reshape(count, half, LANES)

    def add_rows(self, k, fine):
        half = self.rows // 2
        for place in range(2):
            at = pl.ds(place, half, 2)
            self.x[k, at, :] = self.x[k, at, :] + fine


W0 = 30
W1 = 9
W2 = 34
W3 = 10
SMEM = pl.BlockSpec(memory_space=pltpu.SMEM)
VM = pl.BlockSpec(memory_space=pltpu.VMEM)


def call(kernel, outs, scratch, *args, scalars=0):
    return pl.pallas_call(
        kernel,
        out_shape=[jax.ShapeDtypeStruct(s, F32) for s in outs],
        in_specs=[SMEM] * scalars + [VM] * (len(args) - scalars),
        out_specs=[VM] * len(outs),
        scratch_shapes=[pltpu.VMEM(s, F32) for s in scratch],
        compiler_params=pltpu.CompilerParams(vmem_limit_bytes=VMEM_LIMIT),
    )(*args)


def unpack_kernel(received, table, own):
    fields = own.shape[0]
    for f in range(fields):
        rows = []
        for gx in range(4):
            rows.append(jnp.concatenate([received[gx * 4 + gy, f] for gy in range(4)], axis=1))
        wide = table_dot(jnp.concatenate(rows, axis=0), table[...], 3)
        for k in range(4):
            own[f, k] = wide[:, k * LANES : (k + 1) * LANES]


def assemble(place, pieces, field, window):
    slab, core = place[0], place[1]
    sign = 1 - 2 * core
    clear(window.at[0], window.at[W0 - 1])
    for side, distance, ref, base in pieces:
        slot = 3 + side * sign * distance
        inside = jnp.logical_and(slab + slot - 3 >= 0, slab + slot - 3 < SLABS)
        window[pl.ds(1 + 4 * slot, 4)] = jnp.where(inside, ref[base + field], 0.0)


def clear(*refs):
    for ref in refs:
        ref[...] = jnp.zeros_like(ref)


def clear_ends(count, *refs):
    for ref in refs:
        size = ref.shape[0]
        clear(ref.at[0:count], ref.at[size - count : size])


def down_level0(level, level1, table):
    clear_ends(2, *level.q, *level.dq)
    dx = level.smooth([(1, 29), (2, 28), (2, 28), (3, 27)], DEGREE, SMOOTH_LOW, True, True)
    level.residual(4, 26, level.r, level.x, dx)
    clear_ends(1, level1.side)
    level1.side[1:8] = level.restricted(level.r, 1, 7, table)


def down_level1(level, table):
    clear(*level.q, *level.dq)
    dx = level.smooth([(1, 8), (2, 7), (2, 7), (2, 7)], DEGREE, SMOOTH_LOW, True, True)
    level.residual(4, 5, level.r, level.x, dx)
    return own_quarter(level, level.r, table)


def own_quarter(level, ref, table):
    return table_dot(level.row_pairs(ref, 4, 5)[0], table[0:LANES])


def turn_quarters(x):
    group = lax.broadcasted_iota(jnp.int32, (16, LANES), 0) // 4
    lane = lax.broadcasted_iota(jnp.int32, (16, LANES), 1) // 32
    total = jnp.where(lane == group, x, 0.0)
    for step in range(1, 4):
        moved = pltpu.roll(pltpu.roll(x, 32 * step, 1), 16 - 4 * step, 0)
        total = jnp.where((lane - group) % 4 == step, moved, total)
    return total


def keep_centre(level, level1, centre, kept1):
    for i, ref in enumerate((level.x, level.side, level.diff, level.diag, level.inv)):
        centre[i, 1:9] = ref[11:19]
        clear(centre.at[i, 0], centre.at[i, 9])
    for i, ref in enumerate((level1.x, level1.side, level1.diff, level1.diag, level1.inv)):
        kept1[i] = ref[...]


def make_levels(tables, full, side, work0, full1, work1):
    x, r, qa, qb, da, db = work0
    side1, x1, r1, q1a, q1b, d1a, d1b = work1
    level = Level(0, tables[0], full.at[1], full.at[2], full.at[3], side, x, r, [qa, qb], [da, db])
    level1 = Level(
        1, tables[1], full1.at[0], full1.at[1], full1.at[2], side1, x1, r1, [q1a, q1b], [d1a, d1b]
    )
    return level, level1


def down_first_kernel(
    place, own, mate, near, far, near3, *refs
):
    tables, (coarse0, coarse1) = refs[0:2], refs[2:4]
    full, full1, centre, kept1, packet = refs[4:9]
    react, react1 = refs[9:11]
    work0, work1 = refs[11:17], refs[17:24]
    for i in (2, 3):
        clear_ends(1, full.at[i])
    clear(full1, work1[1], work1[2])
    pieces = [
        (-1, 0, own, 0), (-1, 1, near, 0), (-1, 2, near, 3), (-1, 3, near3, 0),
        (1, 1, mate, 0), (1, 2, far, 0), (1, 3, far, 3),
    ]
    assemble(place, pieces, 0, full.at[0])
    assemble(place, pieces, 1, full.at[1])
    assemble(place, pieces, 2, react)
    level, level1 = make_levels(tables, full, full.at[0], work0, full1, work1)
    level.set_diagonal(1, 29, react)
    level1.diff[1:8] = 0.25 * level.restricted(level.diff, 1, 7, coarse0)
    react1[1:8] = level.restricted(react, 1, 7, coarse0)
    level1.set_diagonal(1, 8, react1)
    down_level0(level, level1, coarse0)
    packet[0:4] = turn_quarters(down_level1(level1, coarse1))[0:4]
    packet[4:8] = turn_quarters(0.25 * own_quarter(level1, level1.diff, coarse1))[0:4]
    packet[8:12] = turn_quarters(own_quarter(level1, react1, coarse1))[0:4]
    keep_centre(level, level1, centre, kept1)


def down_second_kernel(place, own, mate, near, far, near3, full, full1, *refs):
    tables, (coarse0, coarse1) = refs[0:2], refs[2:4]
    centre, kept1, packet = refs[4:7]
    window, dwin, side = refs[7:10]
    work0, work1 = refs[10:16], refs[16:23]
    clear(work1[1], work1[2])
    clear_ends(1, side)
    pieces = [
        (-1, 0, own, 0), (-1, 1, near, 0), (-1, 2, near, 1), (-1, 3, near3, 0),
        (1, 1, mate, 0), (1, 2, far, 0), (1, 3, far, 1),
    ]
    assemble(place, pieces, 0, window)
    dwin[...] = window[...] * full[1]
    source, _ = make_levels(tables, full, full.at[0], work0, full1, work1)
    source.residual(1, 29, side, window, dwin)
    level, level1 = make_levels(tables, full, side, work0, full1, work1)
    down_level0(level, level1, coarse0)
    packet[...] = turn_quarters(down_level1(level1, coarse1))[0:4]
    keep_centre(level, level1, centre, kept1)


def gather_level2(packets, at, target):
    clear_ends(1, target)
    for pack in range(32):
        pieces = [packets[ORDER[4 * pack + j], at : at + 4] for j in range(4)]
        target[1 + pack] = turn_quarters(jnp.concatenate(pieces, axis=0))


def coarse_part(first, packets, tables, lv2, lv3, f2, f3, react2, react3, work2, work3, coarse2, back2):
    x2, r2, q2a, q2b, d2a, d2b = work2
    x3, r3, q3a, q3b, d3a, d3b = work3
    clear(*work2[2:])
    clear(*work3[2:])
    clear_ends(1, x2)
    level2 = Level(2, tables[2], lv2.at[0], lv2.at[1], lv2.at[2], f2, x2, r2, [q2a, q2b], [d2a, d2b])
    level3 = Level(3, tables[3], lv3.at[0], lv3.at[1], lv3.at[2], f3, x3, r3, [q3a, q3b], [d3a, d3b])
    gather_level2(packets, 0, f2)
    clear_ends(1, f3)
    if first:
        clear_ends(1, lv2.at[1], lv2.at[2], lv3.at[0], lv3.at[1], lv3.at[2], react3)
        gather_level2(packets, 4, lv2.at[0])
        gather_level2(packets, 8, react2)
        level2.set_diagonal(1, 33, react2)
        level3.diff[1:9] = 0.25 * level2.restricted(level2.diff, 1, 8, coarse2)
        react3[1:9] = level2.restricted(react2, 1, 8, coarse2)
        level3.set_diagonal(1, 9, react3)
    whole2 = [(1, 33)] * 4
    dx = level2.smooth(whole2, DEGREE, SMOOTH_LOW, True, True)
    level2.residual(1, 33, r2, x2, dx)
    f3[1:9] = level2.restricted(r2, 1, 8, coarse2)
    level3.smooth([(1, 9)] * 8, COARSE_DEGREE, COARSE_LOW, True, False)
    fine = table_dot(level3.get(x3, 1, 9), back2[...])
    for t in range(8):
        for j in range(4):
            level2.add_rows(1 + 4 * t + j, fine[t * 8 : t * 8 + 8, j * LANES : (j + 1) * LANES])
    level2.scale_x(1, 33, dx)
    level2.residual(1, 33, r2, x2, dx)
    level2.smooth(whole2, DEGREE, SMOOTH_LOW, False, False)
    return x2


def up_part(place, x2, spaced, tables, centre, kept1, work0, work1, back0, back1):
    x, r, qa, qb, da, db = work0
    x1, r1, q1a, q1b, d1a, d1b = work1
    clear(*work0[2:])
    clear(*work1[2:])
    slab = place[0]
    clear_ends(3, spaced)
    for pack in range(32):
        value = x2[1 + pack]
        for j in range(4):
            spaced[3 + 4 * pack + j] = pltpu.roll(value, LANES - 32 * j, 1) if j else value
    level1 = Level(
        1, tables[1], kept1.at[2], kept1.at[3], kept1.at[4], kept1.at[1], x1, r1,
        [q1a, q1b], [d1a, d1b],
    )
    level = Level(
        0, tables[0], centre.at[2], centre.at[3], centre.at[4], centre.at[1], x, r,
        [qa, qb], [da, db],
    )
    x1[...] = kept1[0]
    x[...] = centre[0]
    fine = table_dot(spaced[pl.ds(slab + 1, 5)].reshape(5 * 16, LANES), back1[:, 0:LANES])
    for t in range(5):
        level1.add_rows(2 + t, fine[t * 16 : t * 16 + 16])
    level1.scale_x(2, 7, d1b)
    level1.residual(2, 7, r1, x1, d1b)
    level1.smooth([(2, 7), (3, 6), (3, 6), (3, 6)], DEGREE, SMOOTH_LOW, False, False)
    fine = table_dot(level1.get(x1, 3, 6), back0[...])
    for k in range(8):
        t, j = divmod(2 + k, 4)
        level.add_rows(1 + k, fine[t * 32 : t * 32 + 32, j * LANES : (j + 1) * LANES])
    level.scale_x(1, 9, db)
    level.residual(1, 9, r, x, db)
    level.smooth([(1, 9), (2, 8), (2, 8), (3, 7)], DEGREE, SMOOTH_LOW, False, False)
    return x


def up_kernel(first, place, packets, centre, kept1, *refs):
    if first:
        lv2, lv3, before = None, None, None
    else:
        (lv2, lv3, before), refs = refs[0:3], refs[3:]
    tables, (coarse2, back0, back1, back2) = refs[0:4], refs[4:8]
    refs = refs[8:]
    if first:
        (applied, lv2, lv3), refs = refs[0:3], refs[3:]
    else:
        (to_block, out), refs = refs[0:2], refs[2:]
    f2, f3, react2, react3 = refs[0:4]
    work2, work3, work0, work1, spaced = refs[4:10], refs[10:16], refs[16:22], refs[22:28], refs[28]
    x2 = coarse_part(
        first, packets, tables, lv2, lv3, f2, f3, react2, react3, work2, work3, coarse2, back2
    )
    x = up_part(place, x2, spaced, tables, centre, kept1, work0, work1, back0, back1)
    if first:
        applied[0] = x[3:7]
    else:
        wide = jnp.concatenate([before[0, k] + x[3 + k] for k in range(4)], axis=1)
        pieces = table_dot(wide, to_block[...], 3)
        for gx in range(4):
            for gy in range(4):
                out[gx * 4 + gy] = pieces[gx * 16 : (gx + 1) * 16, gy * LANES : (gy + 1) * LANES]


def up_first_kernel(*refs):
    up_kernel(True, *refs)


def up_second_kernel(*refs):
    up_kernel(False, *refs)


def row_of_sums(rows):
    stacked = jnp.concatenate(
        [jnp.sum(jnp.sum(a, axis=0), axis=0, keepdims=True) for _, a in rows], axis=0
    )
    totals = jnp.sum(stacked, axis=1, keepdims=True)
    lane = lax.broadcasted_iota(jnp.int32, (1, LANES), 1)
    out = jnp.zeros((1, LANES), F32)
    for i, (lanes, _) in enumerate(rows):
        for at in lanes:
            out = jnp.where(lane == at, totals[i : i + 1], out)
    return out


def sums_one_kernel(basis, applied, out):
    rows = [([8 * j + k, 8 * k + j], basis[j] * basis[k]) for j in range(8) for k in range(j, 8)]
    rows += [([64 + k], basis[k] * applied[...]) for k in range(8)]
    rows += [([72], applied[...] * applied[...])]
    out[...] = row_of_sums(rows)


def read_sums(gathered):
    totals = jnp.sum(gathered[...], axis=0)
    row = lax.broadcasted_iota(jnp.int32, (8, LANES), 0)
    lane = lax.broadcasted_iota(jnp.int32, (8, LANES), 1)
    gram = jnp.zeros((8, LANES), F32)
    wide = jnp.broadcast_to(totals, (8, LANES))
    for j in range(8):
        gram = jnp.where(row == j, pltpu.roll(wide, (LANES - 8 * j) % LANES, 1), gram)
    gram = jnp.where(lane < 8, gram, 0.0)
    proj = jnp.where(lane < 8, pltpu.roll(wide, LANES - 64, 1), 0.0)[0:1]
    return gram, proj, totals[:, 72:73]


def column(row_vector):
    row = lax.broadcasted_iota(jnp.int32, (8, LANES), 0)
    lane = lax.broadcasted_iota(jnp.int32, (8, LANES), 1)
    return jnp.sum(jnp.where(row == lane, row_vector, 0.0), axis=1, keepdims=True)


def as_row(column_vector):
    row = lax.broadcasted_iota(jnp.int32, (8, LANES), 0)
    lane = lax.broadcasted_iota(jnp.int32, (8, LANES), 1)
    return jnp.sum(jnp.where(row == lane, column_vector, 0.0), axis=0, keepdims=True)


def times(gram, row_vector):
    return jnp.sum(gram * row_vector, axis=1, keepdims=True)


def dot8(a, b):
    return jnp.sum(a * b, axis=0, keepdims=True)


def finish(gram, proj_two, squares, coeff_one, base, basis, weights_of, out, coefficients, near):
    coeff_two = proj_two * (1.0 / CELLS)
    quadratic = dot8(coeff_two, times(gram, as_row(coeff_two)))
    mean_square = (squares - 2.0 * dot8(coeff_two, proj_two) + quadratic) * (1.0 / CELLS)
    length = jnp.sqrt(mean_square + 1e-06)
    value = base[...]
    subtract = weights_of(coeff_two)
    for k in range(8):
        value = value - subtract[k : k + 1].reshape(1, 1, 1) * basis[k]
    out[...] = value * (1.0 / length).reshape(1, 1, 1)
    lane = lax.broadcasted_iota(jnp.int32, (1, LANES), 1)
    row = as_row(coeff_one + coeff_two)
    coefficients[...] = jnp.where(lane == 8, length, jnp.where(lane == 9, near, row))


def finish_one_kernel(gathered, basis, applied, out, coefficients):
    gram, proj, square = read_sums(gathered)
    one_row = proj * (1.0 / CELLS)
    one, proj = column(one_row), column(proj)
    image = times(gram, one_row)
    proj_two = proj - image
    squares = square - 2.0 * dot8(one, proj) + dot8(one, image)
    near = jnp.where(squares > 0.02 * square, 0.0, 1.0)
    finish(
        gram, proj_two, squares, one, applied, basis, lambda two: one + two, out, coefficients, near
    )


def sums_two_kernel(gathered, basis, applied, first, out):
    _, proj, _ = read_sums(gathered)
    one = column(proj * (1.0 / CELLS))
    value = applied[...]
    for k in range(8):
        value = value - one[k : k + 1].reshape(1, 1, 1) * basis[k]
    first[...] = value
    out[...] = row_of_sums([([64 + k], basis[k] * value) for k in range(8)] + [([72], value * value)])


def finish_two_kernel(gathered, gathered_two, basis, first, out, coefficients):
    gram, proj, _ = read_sums(gathered)
    _, proj_two, squares = read_sums(gathered_two)
    one = column(proj * (1.0 / CELLS))
    near = jnp.zeros((1, 1), F32)
    finish(
        gram, column(proj_two), squares, one, first, basis, lambda two: two, out, coefficients, near
    )


def everywhere(x):
    return lax.all_to_all(jnp.broadcast_to(x[None], (SLABS,) + x.shape), AXES, 0, 0, tiled=True)


def halo(own):
    mate = lax.ppermute(own, AXES, CORE_SWAP)
    near = lax.ppermute(jnp.concatenate([own, mate], axis=0), AXES, CHIP_SWAP)
    far = lax.ppermute(near, AXES, CORE_SWAP)
    near3 = lax.ppermute(far[: own.shape[0]], AXES, CHIP_SWAP)
    return mate, near, far, near3


def local(basis, diffusion, reaction):
    gx, gy, gz = (lax.axis_index(a) for a in AXES)
    odd = gz % 2
    core = gx % 2
    slab = 16 * gz + 2 * slab_in_group(gx // 2, gy, odd) + core
    place = jnp.stack([slab, core]).astype(jnp.int32)
    tables = [jnp.asarray(t, BF16) for t in STENCIL]
    coarse = [jnp.asarray(t, BF16) for t in RESTRICT]
    back = [jnp.asarray(t.T, BF16) for t in RESTRICT]
    to_slab = jnp.asarray(TO_SLAB, BF16)
    to_block = jnp.asarray(TO_SLAB.T, BF16)
    takes = [
        [2 * slab_in_group(a // 2, b, parity) + a % 2 for a in range(4) for b in range(4)]
        for parity in (0, 1)
    ]

    fields = jnp.stack([basis[7], diffusion, reaction])
    parts = fields.reshape(3, 16, 16, 16, 8).transpose(3, 0, 1, 4, 2).reshape(16, 3, 16, LANES)
    parts = jnp.where(
        odd == 1,
        jnp.stack([parts[i] for i in takes[1]]),
        jnp.stack([parts[i] for i in takes[0]]),
    )
    received = lax.all_to_all(parts, ("gx", "gy"), 0, 0, tiled=True)
    (own,) = call(unpack_kernel, [(3, 4, 64, LANES)], [], received, to_slab)

    big = (W0, 64, LANES)
    small = (W1, 32, LANES)
    two = (W2, 16, LANES)
    three = (W3, 8, LANES)
    mid = (10, 64, LANES)
    full, full1, centre, kept1, packet = call(
        down_first_kernel,
        [(4,) + big, (3,) + small, (5,) + mid, (5,) + small, (12, LANES)],
        [big, small] + [big] * 6 + [small] * 7,
        place, own, *halo(own), *tables[0:2], *coarse[0:2], scalars=1,
    )
    up_scratch = (
        [two, three, two, three]
        + [two] * 6
        + [three] * 6
        + [mid] * 6
        + [small] * 6
        + [(SLABS + 6, 16, LANES)]
    )
    applied, lv2, lv3 = call(
        up_first_kernel,
        [(1, 4, 64, LANES), (3,) + two, (3,) + three],
        up_scratch,
        place, everywhere(packet), centre, kept1, *tables, coarse[2], *back, scalars=1,
    )
    centre, kept1, packet = call(
        down_second_kernel,
        [(5,) + mid, (5,) + small, (4, LANES)],
        [big] * 9 + [small] * 7,
        place, applied, *halo(applied), full, full1, *tables[0:2], *coarse[0:2], scalars=1,
    )
    (out,) = call(
        up_second_kernel,
        [(16, 16, LANES)],
        up_scratch,
        place, everywhere(packet), centre, kept1, lv2, lv3, applied,
        *tables, coarse[2], *back, to_block, scalars=1,
    )
    back = lax.all_to_all(out, ("gx", "gy"), 0, 0, tiled=True)
    inverse = [[t.index(p) for p in range(16)] for t in takes]
    back = jnp.where(
        odd == 1,
        jnp.stack([back[i] for i in inverse[1]]),
        jnp.stack([back[i] for i in inverse[0]]),
    )
    applied = back.reshape(16, 16, 8, 16).transpose(1, 3, 0, 2).reshape(16, 16, LANES)

    (part,) = call(sums_one_kernel, [(1, LANES)], [], basis, applied)
    gathered = everywhere(part)
    block = (16, 16, LANES)
    row = (1, LANES)
    next_vector, coefficients = call(
        finish_one_kernel, [block, row], [], gathered, basis, applied
    )

    def second_sum():
        first, part = call(sums_two_kernel, [block, row], [], gathered, basis, applied)
        return tuple(
            call(finish_two_kernel, [block, row], [], gathered, everywhere(part), basis, first)
        )

    next_vector, coefficients = lax.cond(
        coefficients[0, 9] > 0.5, second_sum, lambda: (next_vector, coefficients)
    )
    return next_vector, coefficients[0, 0:9]


def solution(mesh):
    placed = (P(None, "gx", "gy", "gz"), P("gx", "gy", "gz"), P("gx", "gy", "gz"))
    return jax.shard_map(
        local, mesh=mesh, in_specs=placed, out_specs=(P("gx", "gy", "gz"), P()), check_vma=False
    )
```

```python
import numpy as np
import jax
import jax.numpy as jnp
from jax import lax
from jax.experimental import pallas as pl
from jax.experimental.pallas import tpu as pltpu
from jax.sharding import PartitionSpec as P

AXES = ("gx", "gy", "gz")
DEGREE = 4
COARSE_DEGREE = 8
UPPER_BOUND = 2.0
SMOOTH_LOW = 0.25
COARSE_LOW = 0.05
PULL = (1.0, 0.5, 2.0)
WX, WY, WZ = PULL
WXY = (WX + WY) / 8.0
WXZ = (WX + WZ) / 8.0
WYZ = (WY + WZ) / 8.0
WXYZ = (WX + WY + WZ) / 24.0
WEIGHT_SUM = 2.0 * (WX + WY + WZ) + 4.0 * (WXY + WXZ + WYZ) + 8.0 * WXYZ
LANES = 128
SLABS = 128
CELLS = 64.0 * 64.0 * 1024.0
F32 = jnp.float32
BF16 = jnp.bfloat16
VMEM_LIMIT = 56 * 1024 * 1024

WIDTHS = (64, 32, 16, 8)


def slab_in_group(x_lo, z, odd):
    turned = z + odd * (3 - 2 * z)
    return 2 * turned + (x_lo + z + 1) % 2


def device_order():
    order = [0] * SLABS
    for gx in range(4):
        for gy in range(4):
            for gz in range(8):
                slab = 16 * gz + 2 * slab_in_group(gx // 2, gy, gz % 2) + gx % 2
                order[slab] = (gx * 4 + gy) * 8 + gz
    return order


ORDER = device_order()
CORE_SWAP = [(ORDER[s], ORDER[s ^ 1]) for s in range(SLABS)]
CHIP_SWAP = [(ORDER[s], ORDER[(s + 1 if s % 2 else s - 1) % SLABS]) for s in range(SLABS)]


def fine_to_coarse(level):
    width = WIDTHS[level]
    planes = LANES // width
    table = np.zeros((4, LANES, LANES), np.float32)
    for pack in range(4):
        for lane in range(LANES):
            z, y = divmod(lane, width)
            table[pack, lane, ((pack * planes + z) // 2) * (width // 2) + y // 2] = 1.0
    return table.reshape(4 * LANES, LANES)


def block_to_slab():
    table = np.zeros((512, 512), np.float32)
    for gy in range(4):
        for z in range(8):
            for y in range(16):
                table[gy * 128 + z * 16 + y, (z // 2) * 128 + (z % 2) * 64 + gy * 16 + y] = 1.0
    return table


def stencil_table(level):
    width = WIDTHS[level]
    planes = LANES // width
    weights = {
        (0, 1, 0): WY, (0, 0, 1): WZ, (0, 1, 1): WYZ,
        (1, 0, 0): WX, (1, 1, 0): WXY, (1, 0, 1): WXZ, (1, 1, 1): WXYZ,
    }
    table = np.zeros((2 * LANES, 2 * LANES), np.float32)
    for lane in range(LANES):
        z, y = divmod(lane, width)
        for dz in (-1, 0, 1):
            for dy in (-1, 0, 1):
                if not 0 <= y + dy < width:
                    continue
                outside = not 0 <= z + dz < planes
                source = outside * LANES + (z + dz) % planes * width + y + dy
                for dx in (0, 1):
                    if (dx, abs(dy), abs(dz)) in weights:
                        weight = round(48.0 * weights[dx, abs(dy), abs(dz)]) / 2.0
                        table[source, dx * LANES + lane] += weight
    return table


RESTRICT = [fine_to_coarse(level) for level in range(3)]
TO_SLAB = block_to_slab()
STENCIL = [stencil_table(level) for level in range(4)]


def table_dot(a, table, parts=2):
    total = None
    rest = a
    for part_number in range(parts):
        part = rest.astype(BF16)
        if part_number + 1 < parts:
            rest = rest - part.astype(F32)
        term = jnp.dot(part, table, preferred_element_type=F32)
        total = term if total is None else total + term
    return total


class Level:
    def __init__(self, index, table, diff, diag, inv, side, x, r, q, dq):
        self.width = self.rows = WIDTHS[index]
        self.table = table
        self.diff, self.diag, self.inv, self.side = diff, diag, inv, side
        self.x, self.r, self.q, self.dq = x, r, q, dq

    def get(self, ref, lo, hi):
        return ref[lo:hi].reshape((hi - lo) * self.rows, LANES)

    def put(self, ref, lo, hi, value):
        ref[lo:hi] = value.reshape(hi - lo, self.rows, LANES)

    def spread(self, ref, lo, hi):
        n = (hi - lo) * self.rows
        lane = lax.broadcasted_iota(jnp.int32, (n, LANES), 1)
        row = lax.broadcasted_iota(jnp.int32, (n, LANES), 0) % self.rows
        here = self.get(ref, lo, hi)
        beside = jnp.where(
            lane < self.width, self.get(ref, lo + 1, hi + 1), self.get(ref, lo - 1, hi - 1)
        )
        out = table_dot(jnp.concatenate([here, beside], axis=1), self.table[...])
        next_x = out[:, LANES:]
        return (
            out[:, :LANES]
            + jnp.where(row == self.rows - 1, 0.0, pltpu.roll(next_x, n - 1, 0))
            + jnp.where(row == 0, 0.0, pltpu.roll(next_x, 1, 0))
        )

    def operate(self, lo, hi, u, du):
        both = self.get(self.diff, lo, hi) * self.spread(u, lo, hi) + self.spread(du, lo, hi)
        return self.get(self.diag, lo, hi) * self.get(u, lo, hi) - (1.0 / 48.0) * both

    def set_diagonal(self, lo, hi, reaction):
        d = self.get(self.diff, lo, hi)
        diag = self.get(reaction, lo, hi) + (
            (0.5 * WEIGHT_SUM) * d + (1.0 / 48.0) * self.spread(self.diff, lo, hi)
        )
        self.put(self.diag, lo, hi, diag)
        self.put(self.inv, lo, hi, jnp.where(d > 0.0, 1.0 / diag, 0.0))

    def residual(self, lo, hi, out, u, du):
        self.put(out, lo, hi, self.get(self.side, lo, hi) - self.operate(lo, hi, u, du))

    def scale_x(self, lo, hi, out):
        self.put(out, lo, hi, self.get(self.diff, lo, hi) * self.get(self.x, lo, hi))

    def smooth(self, ranges, degree, lower, fresh, keep):
        middle = 0.5 * (UPPER_BOUND + lower)
        radius = 0.5 * (UPPER_BOUND - lower)
        ratio = middle / radius
        rho = 1.0 / ratio

        lo, hi = ranges[0]
        if fresh:
            r = self.get(self.side, lo, hi)
            self.put(self.r, lo, hi, r)
        else:
            r = self.get(self.r, lo, hi)
        q = self.get(self.inv, lo, hi) * r * (1.0 / middle)
        self.put(self.q[0], lo, hi, q)
        self.put(self.dq[0], lo, hi, self.get(self.diff, lo, hi) * q)
        self.put(self.x, lo, hi, q if fresh else self.get(self.x, lo, hi) + q)
        now = 0
        for turn in range(1, degree):
            rho_next = 1.0 / (2.0 * ratio - rho)
            a, b = rho_next * rho, 2.0 * rho_next / radius
            rho = rho_next
            u, du, v, dv = self.q[now], self.dq[now], self.q[1 - now], self.dq[1 - now]
            lo, hi = ranges[turn]
            r = self.get(self.r, lo, hi) - self.operate(lo, hi, u, du)
            q = a * self.get(u, lo, hi) + b * (self.get(self.inv, lo, hi) * r)
            x = self.get(self.x, lo, hi) + q
            self.put(self.x, lo, hi, x)
            if turn + 1 < degree:
                self.put(self.r, lo, hi, r)
                self.put(v, lo, hi, q)
                self.put(dv, lo, hi, self.get(self.diff, lo, hi) * q)
            elif keep:
                self.put(dv, lo, hi, self.get(self.diff, lo, hi) * x)
            now = 1 - now
        return self.dq[now]

    def row_pairs(self, ref, lo, hi):
        half = self.rows // 2
        return ref[lo:hi, pl.ds(0, half, 2), :] + ref[lo:hi, pl.ds(1, half, 2), :]

    def restricted(self, ref, lo, count, table):
        half = self.rows // 2
        pairs = self.row_pairs(ref, lo, lo + 4 * count).reshape(count, 4, half, LANES)
        wide = jnp.concatenate(
            [pairs[:, j].reshape(count * half, LANES) for j in range(4)], axis=1
        )
        return table_dot(wide, table[...]).reshape(count, half, LANES)

    def add_rows(self, k, fine):
        half = self.rows // 2
        for place in range(2):
            at = pl.ds(place, half, 2)
            self.x[k, at, :] = self.x[k, at, :] + fine


W0 = 22
W1 = 7
W2 = 14
W3 = 5
SMEM = pl.BlockSpec(memory_space=pltpu.SMEM)
VM = pl.BlockSpec(memory_space=pltpu.VMEM)


def call(kernel, outs, scratch, *args, scalars=0):
    return pl.pallas_call(
        kernel,
        out_shape=[jax.ShapeDtypeStruct(s, F32) for s in outs],
        in_specs=[SMEM] * scalars + [VM] * (len(args) - scalars),
        out_specs=[VM] * len(outs),
        scratch_shapes=[pltpu.VMEM(s, F32) for s in scratch],
        compiler_params=pltpu.CompilerParams(vmem_limit_bytes=VMEM_LIMIT),
    )(*args)


def unpack_kernel(received, table, own):
    fields = own.shape[0]
    for f in range(fields):
        rows = []
        for gx in range(4):
            rows.append(jnp.concatenate([received[gx * 4 + gy, f] for gy in range(4)], axis=1))
        wide = table_dot(jnp.concatenate(rows, axis=0), table[...], 3)
        for k in range(4):
            own[f, k] = wide[:, k * LANES : (k + 1) * LANES]


def assemble(place, pieces, field, window):
    slab, core = place[0], place[1]
    sign = 1 - 2 * core
    clear(window.at[0], window.at[W0 - 1])
    for side, distance, ref, base in pieces:
        slot = 2 + side * sign * distance
        inside = jnp.logical_and(slab + slot - 2 >= 0, slab + slot - 2 < SLABS)
        window[pl.ds(1 + 4 * slot, 4)] = jnp.where(inside, ref[base + field], 0.0)


def clear(*refs):
    for ref in refs:
        ref[...] = jnp.zeros_like(ref)


def clear_ends(count, *refs):
    for ref in refs:
        size = ref.shape[0]
        clear(ref.at[0:count], ref.at[size - count : size])


def down_level0(level, level1, table):
    clear_ends(2, *level.q, *level.dq)
    dx = level.smooth([(1, 21), (2, 20), (2, 20), (3, 19)], DEGREE, SMOOTH_LOW, True, True)
    level.residual(4, 18, level.r, level.x, dx)
    clear_ends(1, level1.side)
    level1.side[1:6] = level.restricted(level.r, 1, 5, table)


def down_level1(level, table):
    clear(*level.q, *level.dq)
    dx = level.smooth([(1, 6), (2, 5), (2, 5), (2, 5)], DEGREE, SMOOTH_LOW, True, True)
    level.residual(3, 4, level.r, level.x, dx)
    return own_quarter(level, level.r, table)


def own_quarter(level, ref, table):
    return table_dot(level.row_pairs(ref, 3, 4)[0], table[0:LANES])


def turn_quarters(x):
    group = lax.broadcasted_iota(jnp.int32, (16, LANES), 0) // 4
    lane = lax.broadcasted_iota(jnp.int32, (16, LANES), 1) // 32
    total = jnp.where(lane == group, x, 0.0)
    for step in range(1, 4):
        moved = pltpu.roll(pltpu.roll(x, 32 * step, 1), 16 - 4 * step, 0)
        total = jnp.where((lane - group) % 4 == step, moved, total)
    return total


def keep_centre(level, level1, centre, kept1, lent):
    lent[...] = level1.x[2:5]
    for i, ref in enumerate((level.x, level.side, level.diff, level.diag, level.inv)):
        centre[i, 1:9] = ref[7:15]
        clear(centre.at[i, 0], centre.at[i, 9])
    for i, ref in enumerate((level1.x, level1.side, level1.diff, level1.diag, level1.inv)):
        kept1[i] = ref[...]


def make_levels(tables, full, side, work0, full1, work1):
    x, r, qa, qb, da, db = work0
    side1, x1, r1, q1a, q1b, d1a, d1b = work1
    level = Level(0, tables[0], full.at[1], full.at[2], full.at[3], side, x, r, [qa, qb], [da, db])
    level1 = Level(
        1, tables[1], full1.at[0], full1.at[1], full1.at[2], side1, x1, r1, [q1a, q1b], [d1a, d1b]
    )
    return level, level1


def down_first_kernel(
    place, own, mate, near, far, *refs
):
    tables, (coarse0, coarse1) = refs[0:2], refs[2:4]
    full, full1, centre, kept1, lent, packet = refs[4:10]
    react, react1 = refs[10:12]
    work0, work1 = refs[12:18], refs[18:25]
    for i in (2, 3):
        clear_ends(1, full.at[i])
    clear(full1, work1[1], work1[2])
    pieces = [
        (-1, 0, own, 0), (-1, 1, near, 0), (-1, 2, near, 3), (1, 1, mate, 0), (1, 2, far, 0)
    ]
    assemble(place, pieces, 0, full.at[0])
    assemble(place, pieces, 1, full.at[1])
    assemble(place, pieces, 2, react)
    level, level1 = make_levels(tables, full, full.at[0], work0, full1, work1)
    level.set_diagonal(1, 21, react)
    level1.diff[1:6] = 0.25 * level.restricted(level.diff, 1, 5, coarse0)
    react1[1:6] = level.restricted(react, 1, 5, coarse0)
    level1.set_diagonal(1, 6, react1)
    down_level0(level, level1, coarse0)
    packet[0] = turn_quarters(down_level1(level1, coarse1))[0:4]
    packet[1] = turn_quarters(0.25 * own_quarter(level1, level1.diff, coarse1))[0:4]
    packet[2] = turn_quarters(own_quarter(level1, react1, coarse1))[0:4]
    keep_centre(level, level1, centre, kept1, lent)


def down_second_kernel(place, own, mate, near, far, full, full1, *refs):
    tables, (coarse0, coarse1) = refs[0:2], refs[2:4]
    centre, kept1, lent, packet = refs[4:8]
    window, dwin, side = refs[8:11]
    work0, work1 = refs[11:17], refs[17:24]
    clear(work1[1], work1[2])
    clear_ends(1, side)
    pieces = [
        (-1, 0, own, 0), (-1, 1, near, 0), (-1, 2, near, 1), (1, 1, mate, 0), (1, 2, far, 0)
    ]
    assemble(place, pieces, 0, window)
    dwin[...] = window[...] * full[1]
    source, _ = make_levels(tables, full, full.at[0], work0, full1, work1)
    source.residual(1, 21, side, window, dwin)
    level, level1 = make_levels(tables, full, side, work0, full1, work1)
    down_level0(level, level1, coarse0)
    packet[0] = turn_quarters(down_level1(level1, coarse1))[0:4]
    keep_centre(level, level1, centre, kept1, lent)


def gather_level2(place, order, packets, field, target):
    clear_ends(1, target)
    start = place[0] - place[0] % 16 - 16
    for pack in range(12):
        slab = start + 4 * pack
        inside = jnp.logical_and(slab >= 0, slab < SLABS)
        pieces = [packets[order[jnp.clip(slab + j, 0, SLABS - 1)], field] for j in range(4)]
        value = turn_quarters(jnp.concatenate(pieces, axis=0))
        target[1 + pack] = jnp.where(inside, value, 0.0)


def coarse_part(first, place, order, packets, tables, lv2, lv3, f2, f3, react2, react3, work2, work3, coarse2, back2):
    x2, r2, q2a, q2b, d2a, d2b = work2
    x3, r3, q3a, q3b, d3a, d3b = work3
    clear(*work2[2:])
    clear(*work3[2:])
    clear_ends(1, x2)
    level2 = Level(2, tables[2], lv2.at[0], lv2.at[1], lv2.at[2], f2, x2, r2, [q2a, q2b], [d2a, d2b])
    level3 = Level(3, tables[3], lv3.at[0], lv3.at[1], lv3.at[2], f3, x3, r3, [q3a, q3b], [d3a, d3b])
    gather_level2(place, order, packets, 0, f2)
    clear_ends(1, f3)
    if first:
        clear_ends(1, lv2.at[1], lv2.at[2], lv3.at[0], lv3.at[1], lv3.at[2], react3)
        gather_level2(place, order, packets, 1, lv2.at[0])
        gather_level2(place, order, packets, 2, react2)
        level2.set_diagonal(1, 13, react2)
        level3.diff[1:4] = 0.25 * level2.restricted(level2.diff, 1, 3, coarse2)
        react3[1:4] = level2.restricted(react2, 1, 3, coarse2)
        level3.set_diagonal(1, 4, react3)
    whole2 = [(1, 13)] * 4
    dx = level2.smooth(whole2, DEGREE, SMOOTH_LOW, True, True)
    level2.residual(1, 13, r2, x2, dx)
    f3[1:4] = level2.restricted(r2, 1, 3, coarse2)
    level3.smooth([(1, 4)] * 8, COARSE_DEGREE, COARSE_LOW, True, False)
    fine = table_dot(level3.get(x3, 1, 4), back2[...])
    for t in range(3):
        for j in range(4):
            level2.add_rows(1 + 4 * t + j, fine[t * 8 : t * 8 + 8, j * LANES : (j + 1) * LANES])
    level2.scale_x(1, 13, dx)
    level2.residual(1, 13, r2, x2, dx)
    level2.smooth(whole2, DEGREE, SMOOTH_LOW, False, False)
    return x2


def up_part(place, x2, spaced, tables, centre, kept1, swapped, mate, work0, work1, back0, back1):
    x, r, qa, qb, da, db = work0
    x1, r1, q1a, q1b, d1a, d1b = work1
    clear(*work0[2:])
    clear(*work1[2:])
    slab, core = place[0], place[1]
    for pack in range(3, 9):
        value = x2[1 + pack]
        for j in range(4):
            spaced[4 * pack + j - 12] = pltpu.roll(value, LANES - 32 * j, 1) if j else value
    level1 = Level(
        1, tables[1], kept1.at[2], kept1.at[3], kept1.at[4], kept1.at[1], x1, r1,
        [q1a, q1b], [d1a, d1b],
    )
    level = Level(
        0, tables[0], centre.at[2], centre.at[3], centre.at[4], centre.at[1], x, r,
        [qa, qb], [da, db],
    )
    x1[...] = kept1[0]
    x[...] = centre[0]
    half = lax.broadcasted_iota(jnp.int32, (32, LANES), 1) < 64
    below, above = slab > 0, slab < SLABS - 1
    first_core = core == 0

    def beside(pack, is_below):
        mine, others = (swapped, mate) if is_below else (mate, swapped)
        value = jnp.where(first_core, mine[pack], others[pack])
        return jnp.where(below if is_below else above, value, 0.0)

    x1[1] = beside(0, True)
    x1[2] = jnp.where(half, beside(1, True), x1[2])
    x1[4] = jnp.where(half, x1[4], beside(1, False))
    x1[5] = beside(2, False)
    start = slab % 16 + 2
    fine = table_dot(spaced[pl.ds(start, 5)].reshape(5 * 16, LANES), back1[:, 0:LANES])
    for t in range(5):
        level1.add_rows(1 + t, fine[t * 16 : t * 16 + 16])
    level1.scale_x(1, 6, d1b)
    level1.residual(1, 6, r1, x1, d1b)
    level1.smooth([(1, 6), (2, 5), (2, 5), (2, 5)], DEGREE, SMOOTH_LOW, False, False)
    fine = table_dot(level1.get(x1, 2, 5), back0[...])
    for k in range(8):
        t, j = divmod(2 + k, 4)
        level.add_rows(1 + k, fine[t * 32 : t * 32 + 32, j * LANES : (j + 1) * LANES])
    level.scale_x(1, 9, db)
    level.residual(1, 9, r, x, db)
    level.smooth([(1, 9), (2, 8), (2, 8), (3, 7)], DEGREE, SMOOTH_LOW, False, False)
    return x


def up_kernel(first, place, order, packets, centre, kept1, swapped, mate, *refs):
    if first:
        lv2, lv3, before = None, None, None
    else:
        (lv2, lv3, before), refs = refs[0:3], refs[3:]
    tables, (coarse2, back0, back1, back2) = refs[0:4], refs[4:8]
    refs = refs[8:]
    if first:
        (applied, lv2, lv3), refs = refs[0:3], refs[3:]
    else:
        (to_block, out), refs = refs[0:2], refs[2:]
    f2, f3, react2, react3 = refs[0:4]
    work2, work3, work0, work1, spaced = refs[4:10], refs[10:16], refs[16:22], refs[22:28], refs[28]
    x2 = coarse_part(
        first, place, order, packets, tables, lv2, lv3, f2, f3, react2, react3, work2, work3, coarse2, back2
    )
    x = up_part(
        place, x2, spaced, tables, centre, kept1, swapped, mate, work0, work1, back0, back1
    )
    if first:
        applied[0] = x[3:7]
    else:
        wide = jnp.concatenate([before[0, k] + x[3 + k] for k in range(4)], axis=1)
        pieces = table_dot(wide, to_block[...], 3)
        for gx in range(4):
            for gy in range(4):
                out[gx * 4 + gy] = pieces[gx * 16 : (gx + 1) * 16, gy * LANES : (gy + 1) * LANES]


def up_first_kernel(*refs):
    up_kernel(True, *refs)


def up_second_kernel(*refs):
    up_kernel(False, *refs)


def row_of_sums(rows):
    stacked = jnp.concatenate(
        [jnp.sum(jnp.sum(a, axis=0), axis=0, keepdims=True) for _, a in rows], axis=0
    )
    totals = jnp.sum(stacked, axis=1, keepdims=True)
    lane = lax.broadcasted_iota(jnp.int32, (1, LANES), 1)
    out = jnp.zeros((1, LANES), F32)
    for i, (lanes, _) in enumerate(rows):
        for at in lanes:
            out = jnp.where(lane == at, totals[i : i + 1], out)
    return out


def sums_one_kernel(basis, applied, out):
    rows = [([8 * j + k, 8 * k + j], basis[j] * basis[k]) for j in range(8) for k in range(j, 8)]
    rows += [([64 + k], basis[k] * applied[...]) for k in range(8)]
    rows += [([72], applied[...] * applied[...])]
    out[...] = row_of_sums(rows)


def read_sums(gathered):
    totals = jnp.sum(gathered[...], axis=0)
    row = lax.broadcasted_iota(jnp.int32, (8, LANES), 0)
    lane = lax.broadcasted_iota(jnp.int32, (8, LANES), 1)
    gram = jnp.zeros((8, LANES), F32)
    wide = jnp.broadcast_to(totals, (8, LANES))
    for j in range(8):
        gram = jnp.where(row == j, pltpu.roll(wide, (LANES - 8 * j) % LANES, 1), gram)
    gram = jnp.where(lane < 8, gram, 0.0)
    proj = jnp.where(lane < 8, pltpu.roll(wide, LANES - 64, 1), 0.0)[0:1]
    return gram, proj, totals[:, 72:73]


def column(row_vector):
    row = lax.broadcasted_iota(jnp.int32, (8, LANES), 0)
    lane = lax.broadcasted_iota(jnp.int32, (8, LANES), 1)
    return jnp.sum(jnp.where(row == lane, row_vector, 0.0), axis=1, keepdims=True)


def as_row(column_vector):
    row = lax.broadcasted_iota(jnp.int32, (8, LANES), 0)
    lane = lax.broadcasted_iota(jnp.int32, (8, LANES), 1)
    return jnp.sum(jnp.where(row == lane, column_vector, 0.0), axis=0, keepdims=True)


def times(gram, row_vector):
    return jnp.sum(gram * row_vector, axis=1, keepdims=True)


def dot8(a, b):
    return jnp.sum(a * b, axis=0, keepdims=True)


def finish(gram, proj_two, squares, coeff_one, base, basis, weights_of, out, coefficients, near):
    coeff_two = proj_two * (1.0 / CELLS)
    quadratic = dot8(coeff_two, times(gram, as_row(coeff_two)))
    mean_square = (squares - 2.0 * dot8(coeff_two, proj_two) + quadratic) * (1.0 / CELLS)
    length = jnp.sqrt(mean_square + 1e-06)
    value = base[...]
    subtract = weights_of(coeff_two)
    for k in range(8):
        value = value - subtract[k : k + 1].reshape(1, 1, 1) * basis[k]
    out[...] = value * (1.0 / length).reshape(1, 1, 1)
    lane = lax.broadcasted_iota(jnp.int32, (1, LANES), 1)
    row = as_row(coeff_one + coeff_two)
    coefficients[...] = jnp.where(lane == 8, length, jnp.where(lane == 9, near, row))


def finish_one_kernel(gathered, basis, applied, out, coefficients):
    gram, proj, square = read_sums(gathered)
    one_row = proj * (1.0 / CELLS)
    one, proj = column(one_row), column(proj)
    image = times(gram, one_row)
    proj_two = proj - image
    squares = square - 2.0 * dot8(one, proj) + dot8(one, image)
    near = jnp.where(squares > 0.02 * square, 0.0, 1.0)
    finish(
        gram, proj_two, squares, one, applied, basis, lambda two: one + two, out, coefficients, near
    )


def sums_two_kernel(gathered, basis, applied, first, out):
    _, proj, _ = read_sums(gathered)
    one = column(proj * (1.0 / CELLS))
    value = applied[...]
    for k in range(8):
        value = value - one[k : k + 1].reshape(1, 1, 1) * basis[k]
    first[...] = value
    out[...] = row_of_sums([([64 + k], basis[k] * value) for k in range(8)] + [([72], value * value)])


def finish_two_kernel(gathered, gathered_two, basis, first, out, coefficients):
    gram, proj, _ = read_sums(gathered)
    _, proj_two, squares = read_sums(gathered_two)
    one = column(proj * (1.0 / CELLS))
    near = jnp.zeros((1, 1), F32)
    finish(
        gram, column(proj_two), squares, one, first, basis, lambda two: two, out, coefficients, near
    )


def everywhere(x):
    return lax.all_to_all(jnp.broadcast_to(x[None], (SLABS,) + x.shape), AXES, 0, 0, tiled=True)


def halo(own):
    mate = lax.ppermute(own, AXES, CORE_SWAP)
    near = lax.ppermute(jnp.concatenate([own, mate], axis=0), AXES, CHIP_SWAP)
    far = lax.ppermute(near[: own.shape[0]], AXES, CORE_SWAP)
    return mate, near, far


def beside(lent):
    return lax.ppermute(lent, AXES, CHIP_SWAP), lax.ppermute(lent, AXES, CORE_SWAP)


def local(basis, diffusion, reaction):
    gx, gy, gz = (lax.axis_index(a) for a in AXES)
    odd = gz % 2
    core = gx % 2
    slab = 16 * gz + 2 * slab_in_group(gx // 2, gy, odd) + core
    place = jnp.stack([slab, core]).astype(jnp.int32)
    order = jnp.asarray(ORDER, jnp.int32)
    tables = [jnp.asarray(t, BF16) for t in STENCIL]
    coarse = [jnp.asarray(t, BF16) for t in RESTRICT]
    back = [jnp.asarray(t.T, BF16) for t in RESTRICT]
    to_slab = jnp.asarray(TO_SLAB, BF16)
    to_block = jnp.asarray(TO_SLAB.T, BF16)
    takes = [
        [2 * slab_in_group(a // 2, b, parity) + a % 2 for a in range(4) for b in range(4)]
        for parity in (0, 1)
    ]

    fields = jnp.stack([basis[7], diffusion, reaction])
    parts = fields.reshape(3, 16, 16, 16, 8).transpose(3, 0, 1, 4, 2).reshape(16, 3, 16, LANES)
    parts = jnp.where(
        odd == 1,
        jnp.stack([parts[i] for i in takes[1]]),
        jnp.stack([parts[i] for i in takes[0]]),
    )
    received = lax.all_to_all(parts, ("gx", "gy"), 0, 0, tiled=True)
    (own,) = call(unpack_kernel, [(3, 4, 64, LANES)], [], received, to_slab)

    big = (W0, 64, LANES)
    small = (W1, 32, LANES)
    two = (W2, 16, LANES)
    three = (W3, 8, LANES)
    mid = (10, 64, LANES)
    full, full1, centre, kept1, lent, packet = call(
        down_first_kernel,
        [(4,) + big, (3,) + small, (5,) + mid, (5,) + small, (3, 32, LANES), (3, 4, LANES)],
        [big, small] + [big] * 6 + [small] * 7,
        place, own, *halo(own), *tables[0:2], *coarse[0:2], scalars=1,
    )
    up_scratch = (
        [two, three, two, three]
        + [two] * 6
        + [three] * 6
        + [mid] * 6
        + [small] * 6
        + [(24, 16, LANES)]
    )
    applied, lv2, lv3 = call(
        up_first_kernel,
        [(1, 4, 64, LANES), (3,) + two, (3,) + three],
        up_scratch,
        place, order, everywhere(packet), centre, kept1, *beside(lent), *tables, coarse[2], *back, scalars=2,
    )
    centre, kept1, lent, packet = call(
        down_second_kernel,
        [(5,) + mid, (5,) + small, (3, 32, LANES), (1, 4, LANES)],
        [big] * 9 + [small] * 7,
        place, applied, *halo(applied), full, full1, *tables[0:2], *coarse[0:2], scalars=1,
    )
    (out,) = call(
        up_second_kernel,
        [(16, 16, LANES)],
        up_scratch,
        place, order, everywhere(packet), centre, kept1, *beside(lent), lv2, lv3, applied,
        *tables, coarse[2], *back, to_block, scalars=2,
    )
    back = lax.all_to_all(out, ("gx", "gy"), 0, 0, tiled=True)
    inverse = [[t.index(p) for p in range(16)] for t in takes]
    back = jnp.where(
        odd == 1,
        jnp.stack([back[i] for i in inverse[1]]),
        jnp.stack([back[i] for i in inverse[0]]),
    )
    applied = back.reshape(16, 16, 8, 16).transpose(1, 3, 0, 2).reshape(16, 16, LANES)

    (part,) = call(sums_one_kernel, [(1, LANES)], [], basis, applied)
    gathered = everywhere(part)
    block = (16, 16, LANES)
    row = (1, LANES)
    next_vector, coefficients = call(
        finish_one_kernel, [block, row], [], gathered, basis, applied
    )

    def second_sum():
        first, part = call(sums_two_kernel, [block, row], [], gathered, basis, applied)
        return tuple(
            call(finish_two_kernel, [block, row], [], gathered, everywhere(part), basis, first)
        )

    next_vector, coefficients = lax.cond(
        coefficients[0, 9] > 0.5, second_sum, lambda: (next_vector, coefficients)
    )
    return next_vector, coefficients[0, 0:9]


def solution(mesh):
    placed = (P(None, "gx", "gy", "gz"), P("gx", "gy", "gz"), P("gx", "gy", "gz"))
    return jax.shard_map(
        local, mesh=mesh, in_specs=placed, out_specs=(P("gx", "gy", "gz"), P()), check_vma=False
    )
```

```python
import numpy as np
import jax
import jax.numpy as jnp
from jax import lax
from jax.experimental import pallas as pl
from jax.experimental.pallas import tpu as pltpu
from jax.sharding import PartitionSpec as P

AXES = ("gx", "gy", "gz")
DEGREE = 4
COARSE_DEGREE = 8
UPPER_BOUND = 2.0
SMOOTH_LOW = 0.25
COARSE_LOW = 0.05
PULL = (1.0, 0.5, 2.0)
WX, WY, WZ = PULL
WXY = (WX + WY) / 8.0
WXZ = (WX + WZ) / 8.0
WYZ = (WY + WZ) / 8.0
WXYZ = (WX + WY + WZ) / 24.0
WEIGHT_SUM = 2.0 * (WX + WY + WZ) + 4.0 * (WXY + WXZ + WYZ) + 8.0 * WXYZ
LANES = 128
SLABS = 128
CELLS = 64.0 * 64.0 * 1024.0
F32 = jnp.float32
BF16 = jnp.bfloat16
VMEM_LIMIT = 56 * 1024 * 1024

WIDTHS = (64, 32, 16, 8)


def slab_in_group(x_lo, z, odd):
    turned = z + odd * (3 - 2 * z)
    return 2 * turned + (x_lo + z + 1) % 2


def device_order():
    order = [0] * SLABS
    for gx in range(4):
        for gy in range(4):
            for gz in range(8):
                slab = 16 * gz + 2 * slab_in_group(gx // 2, gy, gz % 2) + gx % 2
                order[slab] = (gx * 4 + gy) * 8 + gz
    return order


ORDER = device_order()
HOLDERS = [[0] * 16, [0] * 16]
for _a in range(4):
    for _b in range(4):
        for _odd in (0, 1):
            HOLDERS[_odd][2 * slab_in_group(_a // 2, _b, _odd) + _a % 2] = 4 * _a + _b
CORE_SWAP = [(ORDER[s], ORDER[s ^ 1]) for s in range(SLABS)]
CHIP_SWAP = [(ORDER[s], ORDER[(s + 1 if s % 2 else s - 1) % SLABS]) for s in range(SLABS)]


def fine_to_coarse(level):
    width = WIDTHS[level]
    planes = LANES // width
    table = np.zeros((4, LANES, LANES), np.float32)
    for pack in range(4):
        for lane in range(LANES):
            z, y = divmod(lane, width)
            table[pack, lane, ((pack * planes + z) // 2) * (width // 2) + y // 2] = 1.0
    return table.reshape(4 * LANES, LANES)


def block_to_slab():
    table = np.zeros((512, 512), np.float32)
    for gy in range(4):
        for z in range(8):
            for y in range(16):
                table[gy * 128 + z * 16 + y, (z // 2) * 128 + (z % 2) * 64 + gy * 16 + y] = 1.0
    return table


def stencil_table(level):
    width = WIDTHS[level]
    planes = LANES // width
    weights = {
        (0, 1, 0): WY, (0, 0, 1): WZ, (0, 1, 1): WYZ,
        (1, 0, 0): WX, (1, 1, 0): WXY, (1, 0, 1): WXZ, (1, 1, 1): WXYZ,
    }
    table = np.zeros((2 * LANES, 2 * LANES), np.float32)
    for lane in range(LANES):
        z, y = divmod(lane, width)
        for dz in (-1, 0, 1):
            for dy in (-1, 0, 1):
                if not 0 <= y + dy < width:
                    continue
                outside = not 0 <= z + dz < planes
                source = outside * LANES + (z + dz) % planes * width + y + dy
                for dx in (0, 1):
                    if (dx, abs(dy), abs(dz)) in weights:
                        weight = round(48.0 * weights[dx, abs(dy), abs(dz)]) / 2.0
                        table[source, dx * LANES + lane] += weight
    return table


RESTRICT = [fine_to_coarse(level) for level in range(3)]
TO_SLAB = block_to_slab()
STENCIL = [stencil_table(level) for level in range(4)]


def table_dot(a, table, parts=2):
    total = None
    rest = a
    for part_number in range(parts):
        part = rest.astype(BF16)
        if part_number + 1 < parts:
            rest = rest - part.astype(F32)
        term = jnp.dot(part, table, preferred_element_type=F32)
        total = term if total is None else total + term
    return total


class Level:
    def __init__(self, index, table, diff, diag, inv, side, x, r, q, dq):
        self.width = self.rows = WIDTHS[index]
        self.table = table
        self.diff, self.diag, self.inv, self.side = diff, diag, inv, side
        self.x, self.r, self.q, self.dq = x, r, q, dq

    def get(self, ref, lo, hi):
        return ref[lo:hi].reshape((hi - lo) * self.rows, LANES)

    def put(self, ref, lo, hi, value):
        ref[lo:hi] = value.reshape(hi - lo, self.rows, LANES)

    def spread(self, ref, lo, hi):
        n = (hi - lo) * self.rows
        lane = lax.broadcasted_iota(jnp.int32, (n, LANES), 1)
        row = lax.broadcasted_iota(jnp.int32, (n, LANES), 0) % self.rows
        here = self.get(ref, lo, hi)
        beside = jnp.where(
            lane < self.width, self.get(ref, lo + 1, hi + 1), self.get(ref, lo - 1, hi - 1)
        )
        out = table_dot(jnp.concatenate([here, beside], axis=1), self.table[...])
        next_x = out[:, LANES:]
        return (
            out[:, :LANES]
            + jnp.where(row == self.rows - 1, 0.0, pltpu.roll(next_x, n - 1, 0))
            + jnp.where(row == 0, 0.0, pltpu.roll(next_x, 1, 0))
        )

    def operate(self, lo, hi, u, du):
        both = self.get(self.diff, lo, hi) * self.spread(u, lo, hi) + self.spread(du, lo, hi)
        return self.get(self.diag, lo, hi) * self.get(u, lo, hi) - (1.0 / 48.0) * both

    def set_diagonal(self, lo, hi, reaction):
        d = self.get(self.diff, lo, hi)
        diag = self.get(reaction, lo, hi) + (
            (0.5 * WEIGHT_SUM) * d + (1.0 / 48.0) * self.spread(self.diff, lo, hi)
        )
        self.put(self.diag, lo, hi, diag)
        self.put(self.inv, lo, hi, jnp.where(d > 0.0, 1.0 / diag, 0.0))

    def residual(self, lo, hi, out, u, du):
        self.put(out, lo, hi, self.get(self.side, lo, hi) - self.operate(lo, hi, u, du))

    def scale_x(self, lo, hi, out):
        self.put(out, lo, hi, self.get(self.diff, lo, hi) * self.get(self.x, lo, hi))

    def smooth(self, ranges, degree, lower, fresh, keep):
        middle = 0.5 * (UPPER_BOUND + lower)
        radius = 0.5 * (UPPER_BOUND - lower)
        ratio = middle / radius
        rho = 1.0 / ratio

        lo, hi = ranges[0]
        if fresh:
            r = self.get(self.side, lo, hi)
            self.put(self.r, lo, hi, r)
        else:
            r = self.get(self.r, lo, hi)
        q = self.get(self.inv, lo, hi) * r * (1.0 / middle)
        self.put(self.q[0], lo, hi, q)
        self.put(self.dq[0], lo, hi, self.get(self.diff, lo, hi) * q)
        self.put(self.x, lo, hi, q if fresh else self.get(self.x, lo, hi) + q)
        now = 0
        for turn in range(1, degree):
            rho_next = 1.0 / (2.0 * ratio - rho)
            a, b = rho_next * rho, 2.0 * rho_next / radius
            rho = rho_next
            u, du, v, dv = self.q[now], self.dq[now], self.q[1 - now], self.dq[1 - now]
            lo, hi = ranges[turn]
            r = self.get(self.r, lo, hi) - self.operate(lo, hi, u, du)
            q = a * self.get(u, lo, hi) + b * (self.get(self.inv, lo, hi) * r)
            x = self.get(self.x, lo, hi) + q
            self.put(self.x, lo, hi, x)
            if turn + 1 < degree:
                self.put(self.r, lo, hi, r)
                self.put(v, lo, hi, q)
                self.put(dv, lo, hi, self.get(self.diff, lo, hi) * q)
            elif keep:
                self.put(dv, lo, hi, self.get(self.diff, lo, hi) * x)
            now = 1 - now
        return self.dq[now]

    def row_pairs(self, ref, lo, hi):
        half = self.rows // 2
        return ref[lo:hi, pl.ds(0, half, 2), :] + ref[lo:hi, pl.ds(1, half, 2), :]

    def restricted(self, ref, lo, count, table):
        half = self.rows // 2
        pairs = self.row_pairs(ref, lo, lo + 4 * count).reshape(count, 4, half, LANES)
        wide = jnp.concatenate(
            [pairs[:, j].reshape(count * half, LANES) for j in range(4)], axis=1
        )
        return table_dot(wide, table[...]).reshape(count, half, LANES)

    def add_rows(self, k, fine):
        half = self.rows // 2
        for place in range(2):
            at = pl.ds(place, half, 2)
            self.x[k, at, :] = self.x[k, at, :] + fine


W0 = 22
W1 = 7
W2 = 14
W3 = 5
DMA = pltpu.SemaphoreType.DMA
STENCILS = pltpu.VMEM((4, 256, 256), BF16)
COARSE = pltpu.VMEM((3, 512, LANES), BF16)
BACK = pltpu.VMEM((3, LANES, 512), BF16)
SPACES = {"s": pltpu.SMEM, "v": pltpu.VMEM, "h": pltpu.HBM}


def call(kernel, outs, scratch, spaces, *args):
    made = []
    for space, shape in outs:
        if space == "v":
            made.append(pltpu.VMEM(shape, F32))
        else:
            made.append(jax.ShapeDtypeStruct(shape, F32))
    given = [
        pltpu.with_memory_space_constraint(a, pltpu.VMEM) if space == "v" else a
        for space, a in zip(spaces, args)
    ]
    return pl.pallas_call(
        kernel,
        out_shape=made,
        in_specs=[pl.BlockSpec(memory_space=SPACES[space]) for space in spaces],
        out_specs=[
            pl.BlockSpec(memory_space=pltpu.HBM if space == "h" else pltpu.VMEM) for space, _ in outs
        ],
        scratch_shapes=[pltpu.VMEM(s, F32) if isinstance(s, tuple) else s for s in scratch],
        compiler_params=pltpu.CompilerParams(vmem_limit_bytes=VMEM_LIMIT),
    )(*given)


def bring(sems, *pairs):
    copies = [pltpu.make_async_copy(a, b, sems.at[i]) for i, (a, b) in enumerate(pairs)]
    for copy in copies:
        copy.start()
    return copies


def wait(copies):
    for copy in copies:
        copy.wait()


def turn_eighths(x):
    row = lax.broadcasted_iota(jnp.int32, x.shape, 1)
    lane = lax.broadcasted_iota(jnp.int32, x.shape, 2) // 16
    total = jnp.where(lane == row, x, 0.0)
    for step in range(1, 8):
        moved = pltpu.roll(pltpu.roll(x, 16 * step, 2), 8 - step, 1)
        total = jnp.where((lane - row) % 8 == step, moved, total)
    return total


def holder(place, slab):
    odd = place[2]
    return jnp.where(odd == 1, HOLDERS[1][slab], HOLDERS[0][slab])


def pack_kernel(place, basis, diffusion, reaction, parts, fields, sems):
    copies = bring(
        sems, (basis.at[7], fields.at[0]), (diffusion, fields.at[1]), (reaction, fields.at[2])
    )
    for f in range(3):
        copies[f].wait()
        turned = fields[f].reshape(256, LANES).T
        for half in range(2):
            pieces = turn_eighths(
                turned[:, half * LANES : (half + 1) * LANES].reshape(16, 8, LANES)
            )
            for slab in range(16):
                parts[holder(place, slab), f, 8 * half : 8 * half + 8] = pieces[slab]


def to_blocks(place, received):
    wide = []
    for half in range(2):
        pieces = [
            received[holder(place, slab), 8 * half : 8 * half + 8][None] for slab in range(16)
        ]
        wide.append(turn_eighths(jnp.concatenate(pieces, axis=0)).reshape(LANES, LANES))
    return jnp.concatenate(wide, axis=1).T.reshape(16, 16, LANES)


def unpack_kernel(received, table, own):
    fields = own.shape[0]
    for f in range(fields):
        rows = []
        for gx in range(4):
            rows.append(jnp.concatenate([received[gx * 4 + gy, f] for gy in range(4)], axis=1))
        wide = table_dot(jnp.concatenate(rows, axis=0), table[...], 3)
        for k in range(4):
            own[f, k] = wide[:, k * LANES : (k + 1) * LANES]


def assemble(place, pieces, field, window):
    slab, core = place[0], place[1]
    sign = 1 - 2 * core
    clear(window.at[0], window.at[W0 - 1])
    for side, distance, ref, base in pieces:
        slot = 2 + side * sign * distance
        inside = jnp.logical_and(slab + slot - 2 >= 0, slab + slot - 2 < SLABS)
        window[pl.ds(1 + 4 * slot, 4)] = jnp.where(inside, ref[base + field], 0.0)


def clear(*refs):
    for ref in refs:
        ref[...] = jnp.zeros_like(ref)


def clear_ends(count, *refs):
    for ref in refs:
        size = ref.shape[0]
        clear(ref.at[0:count], ref.at[size - count : size])


def down_level0(level, level1, table):
    clear_ends(2, *level.q, *level.dq)
    dx = level.smooth([(1, 21), (2, 20), (2, 20), (3, 19)], DEGREE, SMOOTH_LOW, True, True)
    level.residual(4, 18, level.r, level.x, dx)
    clear_ends(1, level1.side)
    level1.side[1:6] = level.restricted(level.r, 1, 5, table)


def down_level1(level, table):
    clear(*level.q, *level.dq)
    dx = level.smooth([(1, 6), (2, 5), (2, 5), (2, 5)], DEGREE, SMOOTH_LOW, True, True)
    level.residual(3, 4, level.r, level.x, dx)
    return own_quarter(level, level.r, table)


def own_quarter(level, ref, table):
    return table_dot(level.row_pairs(ref, 3, 4)[0], table[0:LANES])


def turn_quarters(x):
    group = lax.broadcasted_iota(jnp.int32, (16, LANES), 0) // 4
    lane = lax.broadcasted_iota(jnp.int32, (16, LANES), 1) // 32
    total = jnp.where(lane == group, x, 0.0)
    for step in range(1, 4):
        moved = pltpu.roll(pltpu.roll(x, 32 * step, 1), 16 - 4 * step, 0)
        total = jnp.where((lane - group) % 4 == step, moved, total)
    return total


def to_all(packet, field, quarter):
    rows = turn_quarters(quarter)[0:4]
    packet[:, field] = jnp.broadcast_to(rows[None], (SLABS, 4, LANES))


def keep_early(sems, level, level1, centre, kept1):
    pairs = [
        (ref.at[7:15], centre.at[1 + i])
        for i, ref in enumerate((level.side, level.diff, level.diag, level.inv))
    ]
    pairs += [
        (ref, kept1.at[2 + i]) for i, ref in enumerate((level1.diff, level1.diag, level1.inv))
    ]
    return bring(sems, *pairs)


def keep_late(sems, level, level1, centre, kept1, lent):
    pairs = [
        (level1.x, kept1.at[0]),
        (level1.side, kept1.at[1]),
        (level1.x.at[2:5], lent),
        (level.x.at[7:15], centre.at[0]),
    ]
    return bring(sems, *pairs)


def make_levels(tables, full, side, work0, full1, work1):
    x, r, qa, qb, da, db = work0
    side1, x1, r1, q1a, q1b, d1a, d1b = work1
    level = Level(0, tables[0], full.at[1], full.at[2], full.at[3], side, x, r, [qa, qb], [da, db])
    level1 = Level(
        1, tables[1], full1.at[0], full1.at[1], full1.at[2], side1, x1, r1, [q1a, q1b], [d1a, d1b]
    )
    return level, level1


def down_first_kernel(
    place, own, mate, near, far, stencils_in, coarse_in,
    full_out, full1, centre, kept1, lent, packet,
    full, stencils, coarse, sems, react, react1, *work
):
    work0, work1 = work[0:6], work[6:13]
    tables, coarse0, coarse1 = [stencils.at[0], stencils.at[1]], coarse.at[0], coarse.at[1]
    arriving = bring(
        sems, (stencils_in.at[0:2], stencils.at[0:2]), (coarse_in.at[0:2], coarse.at[0:2])
    )
    for i in (2, 3):
        clear_ends(1, full.at[i])
    clear(full1, work1[1], work1[2])
    pieces = [
        (-1, 0, own, 0), (-1, 1, near, 0), (-1, 2, near, 3), (1, 1, mate, 0), (1, 2, far, 0)
    ]
    assemble(place, pieces, 0, full.at[0])
    assemble(place, pieces, 1, full.at[1])
    assemble(place, pieces, 2, react)
    level, level1 = make_levels(tables, full, full.at[0], work0, full1, work1)
    wait(arriving)
    level.set_diagonal(1, 21, react)
    leaving = bring(sems, (full, full_out))
    level1.diff[1:6] = 0.25 * level.restricted(level.diff, 1, 5, coarse0)
    react1[1:6] = level.restricted(react, 1, 5, coarse0)
    level1.set_diagonal(1, 6, react1)
    leaving += keep_early(sems.at[1:8], level, level1, centre, kept1)
    down_level0(level, level1, coarse0)
    to_all(packet, 0, down_level1(level1, coarse1))
    to_all(packet, 1, 0.25 * own_quarter(level1, level1.diff, coarse1))
    to_all(packet, 2, own_quarter(level1, react1, coarse1))
    wait(leaving + keep_late(sems.at[8:12], level, level1, centre, kept1, lent))


def down_second_kernel(
    place, own, mate, near, far, full_in, full1_in, stencils_in, coarse_in,
    centre, kept1, lent, before, packet,
    full, full1, stencils, coarse, sems, window, dwin, side, *work
):
    work0, work1 = work[0:6], work[6:13]
    tables, coarse0, coarse1 = [stencils.at[0], stencils.at[1]], coarse.at[0], coarse.at[1]
    arriving = bring(
        sems,
        (full_in, full),
        (stencils_in.at[0:2], stencils.at[0:2]),
        (coarse_in.at[0:2], coarse.at[0:2]),
        (full1_in, full1),
    )
    before[...] = own[0]
    clear(work1[1], work1[2])
    clear_ends(1, side)
    pieces = [
        (-1, 0, own, 0), (-1, 1, near, 0), (-1, 2, near, 1), (1, 1, mate, 0), (1, 2, far, 0)
    ]
    assemble(place, pieces, 0, window)
    wait(arriving)
    dwin[...] = window[...] * full[1]
    source, _ = make_levels(tables, full, full.at[0], work0, full1, work1)
    source.residual(1, 21, side, window, dwin)
    level, level1 = make_levels(tables, full, side, work0, full1, work1)
    leaving = keep_early(sems.at[0:7], level, level1, centre, kept1)
    down_level0(level, level1, coarse0)
    to_all(packet, 0, down_level1(level1, coarse1))
    wait(leaving + keep_late(sems.at[7:11], level, level1, centre, kept1, lent))


def gather_level2(place, order, packets, field, target):
    clear_ends(1, target)
    start = place[0] - place[0] % 16 - 16
    for pack in range(12):
        slab = start + 4 * pack
        inside = jnp.logical_and(slab >= 0, slab < SLABS)
        pieces = [packets[order[jnp.clip(slab + j, 0, SLABS - 1)], field] for j in range(4)]
        value = turn_quarters(jnp.concatenate(pieces, axis=0))
        target[1 + pack] = jnp.where(inside, value, 0.0)


def coarse_part(first, place, order, packets, tables, lv2, lv3, f2, f3, react2, react3, work2, work3, coarse2, back2):
    x2, r2, q2a, q2b, d2a, d2b = work2
    x3, r3, q3a, q3b, d3a, d3b = work3
    clear(*work2[2:])
    clear(*work3[2:])
    clear_ends(1, x2)
    level2 = Level(2, tables[2], lv2.at[0], lv2.at[1], lv2.at[2], f2, x2, r2, [q2a, q2b], [d2a, d2b])
    level3 = Level(3, tables[3], lv3.at[0], lv3.at[1], lv3.at[2], f3, x3, r3, [q3a, q3b], [d3a, d3b])
    gather_level2(place, order, packets, 0, f2)
    clear_ends(1, f3)
    if first:
        clear_ends(1, lv2.at[1], lv2.at[2], lv3.at[0], lv3.at[1], lv3.at[2], react3)
        gather_level2(place, order, packets, 1, lv2.at[0])
        gather_level2(place, order, packets, 2, react2)
        level2.set_diagonal(1, 13, react2)
        level3.diff[1:4] = 0.25 * level2.restricted(level2.diff, 1, 3, coarse2)
        react3[1:4] = level2.restricted(react2, 1, 3, coarse2)
        level3.set_diagonal(1, 4, react3)
    whole2 = [(1, 13)] * 4
    dx = level2.smooth(whole2, DEGREE, SMOOTH_LOW, True, True)
    level2.residual(1, 13, r2, x2, dx)
    f3[1:4] = level2.restricted(r2, 1, 3, coarse2)
    level3.smooth([(1, 4)] * 8, COARSE_DEGREE, COARSE_LOW, True, False)
    fine = table_dot(level3.get(x3, 1, 4), back2[...])
    for t in range(3):
        for j in range(4):
            level2.add_rows(1 + 4 * t + j, fine[t * 8 : t * 8 + 8, j * LANES : (j + 1) * LANES])
    level2.scale_x(1, 13, dx)
    level2.residual(1, 13, r2, x2, dx)
    level2.smooth(whole2, DEGREE, SMOOTH_LOW, False, False)
    return x2


def up_part(place, x2, spaced, tables, centre, kept1, swapped, mate, work0, work1, back0, back1):
    x, r, qa, qb, da, db = work0
    x1, r1, q1a, q1b, d1a, d1b = work1
    clear(*work0[2:])
    clear(*work1[2:])
    slab, core = place[0], place[1]
    for pack in range(3, 9):
        value = x2[1 + pack]
        for j in range(4):
            spaced[4 * pack + j - 12] = pltpu.roll(value, LANES - 32 * j, 1) if j else value
    level1 = Level(
        1, tables[1], kept1.at[2], kept1.at[3], kept1.at[4], kept1.at[1], x1, r1,
        [q1a, q1b], [d1a, d1b],
    )
    level = Level(
        0, tables[0], centre.at[2], centre.at[3], centre.at[4], centre.at[1], x, r,
        [qa, qb], [da, db],
    )
    x1[...] = kept1[0]
    x[...] = centre[0]
    half = lax.broadcasted_iota(jnp.int32, (32, LANES), 1) < 64
    below, above = slab > 0, slab < SLABS - 1
    first_core = core == 0

    def beside(pack, is_below):
        mine, others = (swapped, mate) if is_below else (mate, swapped)
        value = jnp.where(first_core, mine[pack], others[pack])
        return jnp.where(below if is_below else above, value, 0.0)

    x1[1] = beside(0, True)
    x1[2] = jnp.where(half, beside(1, True), x1[2])
    x1[4] = jnp.where(half, x1[4], beside(1, False))
    x1[5] = beside(2, False)
    start = slab % 16 + 2
    fine = table_dot(spaced[pl.ds(start, 5)].reshape(5 * 16, LANES), back1[:, 0:LANES])
    for t in range(5):
        level1.add_rows(1 + t, fine[t * 16 : t * 16 + 16])
    level1.scale_x(1, 6, d1b)
    level1.residual(1, 6, r1, x1, d1b)
    level1.smooth([(1, 6), (2, 5), (2, 5), (2, 5)], DEGREE, SMOOTH_LOW, False, False)
    fine = table_dot(level1.get(x1, 2, 5), back0[...])
    for k in range(8):
        t, j = divmod(2 + k, 4)
        level.add_rows(1 + k, fine[t * 32 : t * 32 + 32, j * LANES : (j + 1) * LANES])
    level.scale_x(1, 9, db)
    level.residual(1, 9, r, x, db)
    level.smooth([(1, 9), (2, 8), (2, 8), (3, 7)], DEGREE, SMOOTH_LOW, False, False)
    return x


def up_kernel(first, place, order, packets, centre_in, kept1_in, swapped_in, mate_in, *refs):
    if first:
        (stencils_in, coarse_in, back_in, applied, lv2, lv3), refs = refs[0:6], refs[6:]
        early, later = [], []
    else:
        (lv2_in, lv3_in, before_in, stencils_in, coarse_in, back_in), refs = refs[0:6], refs[6:]
        (to_block_in, out, lv2, lv3, before, to_block), refs = refs[0:6], refs[6:]
        early = [(lv2_in, lv2), (lv3_in, lv3)]
        later = [(before_in, before), (to_block_in, to_block)]
    (stencils, coarse, back, sems, centre, kept1, swapped, mate), refs = refs[0:8], refs[8:]
    early += [(stencils_in, stencils), (coarse_in.at[2], coarse.at[2]), (back_in, back)]
    later += [
        (kept1_in, kept1), (centre_in, centre.at[:, 1:9]), (swapped_in, swapped), (mate_in, mate)
    ]
    arriving = bring(sems.at[0:6], *early)
    arriving_later = bring(sems.at[6:12], *later)
    clear(centre.at[:, 0], centre.at[:, 9])
    tables = [stencils.at[i] for i in range(4)]
    coarse2, back0, back1, back2 = coarse.at[2], back.at[0], back.at[1], back.at[2]
    f2, f3, react2, react3 = refs[0:4]
    work2, work3, work0, work1, spaced = refs[4:10], refs[10:16], refs[16:22], refs[22:28], refs[28]
    wait(arriving)
    x2 = coarse_part(
        first, place, order, packets, tables, lv2, lv3, f2, f3, react2, react3, work2, work3, coarse2, back2
    )
    wait(arriving_later)
    x = up_part(
        place, x2, spaced, tables, centre, kept1, swapped, mate, work0, work1, back0, back1
    )
    if first:
        applied[0] = x[3:7]
    else:
        wide = jnp.concatenate([before[k] + x[3 + k] for k in range(4)], axis=1)
        pieces = table_dot(wide, to_block[...], 3)
        for gx in range(4):
            for gy in range(4):
                out[gx * 4 + gy] = pieces[gx * 16 : (gx + 1) * 16, gy * LANES : (gy + 1) * LANES]


def up_first_kernel(*refs):
    up_kernel(True, *refs)


def up_second_kernel(*refs):
    up_kernel(False, *refs)


def row_of_sums(rows):
    stacked = jnp.concatenate(
        [jnp.sum(jnp.sum(a, axis=0), axis=0, keepdims=True) for _, a in rows], axis=0
    )
    totals = jnp.sum(stacked, axis=1, keepdims=True)
    lane = lax.broadcasted_iota(jnp.int32, (1, LANES), 1)
    out = jnp.zeros((1, LANES), F32)
    for i, (lanes, _) in enumerate(rows):
        for at in lanes:
            out = jnp.where(lane == at, totals[i : i + 1], out)
    return out


def sums_one_kernel(place, received, basis, applied, out):
    applied[...] = to_blocks(place, received)
    rows = [([8 * j + k, 8 * k + j], basis[j] * basis[k]) for j in range(8) for k in range(j, 8)]
    rows += [([64 + k], basis[k] * applied[...]) for k in range(8)]
    rows += [([72], applied[...] * applied[...])]
    out[...] = jnp.broadcast_to(row_of_sums(rows)[None], (SLABS, 1, LANES))


def read_sums(gathered):
    totals = jnp.sum(gathered[...], axis=0)
    row = lax.broadcasted_iota(jnp.int32, (8, LANES), 0)
    lane = lax.broadcasted_iota(jnp.int32, (8, LANES), 1)
    gram = jnp.zeros((8, LANES), F32)
    wide = jnp.broadcast_to(totals, (8, LANES))
    for j in range(8):
        gram = jnp.where(row == j, pltpu.roll(wide, (LANES - 8 * j) % LANES, 1), gram)
    gram = jnp.where(lane < 8, gram, 0.0)
    proj = jnp.where(lane < 8, pltpu.roll(wide, LANES - 64, 1), 0.0)[0:1]
    return gram, proj, totals[:, 72:73]


def column(row_vector):
    row = lax.broadcasted_iota(jnp.int32, (8, LANES), 0)
    lane = lax.broadcasted_iota(jnp.int32, (8, LANES), 1)
    return jnp.sum(jnp.where(row == lane, row_vector, 0.0), axis=1, keepdims=True)


def as_row(column_vector):
    row = lax.broadcasted_iota(jnp.int32, (8, LANES), 0)
    lane = lax.broadcasted_iota(jnp.int32, (8, LANES), 1)
    return jnp.sum(jnp.where(row == lane, column_vector, 0.0), axis=0, keepdims=True)


def times(gram, row_vector):
    return jnp.sum(gram * row_vector, axis=1, keepdims=True)


def dot8(a, b):
    return jnp.sum(a * b, axis=0, keepdims=True)


def finish(gram, proj_two, squares, coeff_one, base, basis, weights_of, out, coefficients, near):
    coeff_two = proj_two * (1.0 / CELLS)
    quadratic = dot8(coeff_two, times(gram, as_row(coeff_two)))
    mean_square = (squares - 2.0 * dot8(coeff_two, proj_two) + quadratic) * (1.0 / CELLS)
    length = jnp.sqrt(mean_square + 1e-06)
    value = base[...]
    subtract = weights_of(coeff_two)
    for k in range(8):
        value = value - subtract[k : k + 1].reshape(1, 1, 1) * basis[k]
    out[...] = value * (1.0 / length).reshape(1, 1, 1)
    lane = lax.broadcasted_iota(jnp.int32, (1, LANES), 1)
    row = as_row(coeff_one + coeff_two)
    coefficients[...] = jnp.where(lane == 8, length, jnp.where(lane == 9, near, row))


def finish_one_kernel(gathered, basis, applied, out, coefficients):
    gram, proj, square = read_sums(gathered)
    one_row = proj * (1.0 / CELLS)
    one, proj = column(one_row), column(proj)
    image = times(gram, one_row)
    proj_two = proj - image
    squares = square - 2.0 * dot8(one, proj) + dot8(one, image)
    near = jnp.where(squares > 0.02 * square, 0.0, 1.0)
    finish(
        gram, proj_two, squares, one, applied, basis, lambda two: one + two, out, coefficients, near
    )


def sums_two_kernel(gathered, basis, applied, first, out):
    _, proj, _ = read_sums(gathered)
    one = column(proj * (1.0 / CELLS))
    value = applied[...]
    for k in range(8):
        value = value - one[k : k + 1].reshape(1, 1, 1) * basis[k]
    first[...] = value
    sums = row_of_sums([([64 + k], basis[k] * value) for k in range(8)] + [([72], value * value)])
    out[...] = jnp.broadcast_to(sums[None], (SLABS, 1, LANES))


def finish_two_kernel(gathered, gathered_two, basis, first, out, coefficients):
    gram, proj, _ = read_sums(gathered)
    _, proj_two, squares = read_sums(gathered_two)
    one = column(proj * (1.0 / CELLS))
    near = jnp.zeros((1, 1), F32)
    finish(
        gram, column(proj_two), squares, one, first, basis, lambda two: two, out, coefficients, near
    )


def swap_all(x):
    return lax.all_to_all(x, AXES, 0, 0, tiled=True)


def halo(own):
    mate = lax.ppermute(own, AXES, CORE_SWAP)
    near = lax.ppermute(jnp.concatenate([own, mate], axis=0), AXES, CHIP_SWAP)
    far = lax.ppermute(near[: own.shape[0]], AXES, CORE_SWAP)
    return mate, near, far


def beside(lent):
    return lax.ppermute(lent, AXES, CHIP_SWAP), lax.ppermute(lent, AXES, CORE_SWAP)


def local(basis, diffusion, reaction):
    gx, gy, gz = (lax.axis_index(a) for a in AXES)
    odd = gz % 2
    core = gx % 2
    slab = 16 * gz + 2 * slab_in_group(gx // 2, gy, odd) + core
    place = jnp.stack([slab, core, odd]).astype(jnp.int32)
    order = jnp.asarray(ORDER, jnp.int32)
    stencils = jnp.asarray(np.stack(STENCIL), BF16)
    coarse = jnp.asarray(np.stack(RESTRICT), BF16)
    back = jnp.asarray(np.stack([t.T for t in RESTRICT]), BF16)
    to_slab = jnp.asarray(TO_SLAB, BF16)
    to_block = jnp.asarray(TO_SLAB.T, BF16)
    block = (16, 16, LANES)
    (parts,) = call(
        pack_kernel,
        [("v", (16, 3, 16, LANES))],
        [(3,) + block, DMA((3,))],
        "shhh", place, basis, diffusion, reaction,
    )
    received = lax.all_to_all(parts, ("gx", "gy"), 0, 0, tiled=True)
    (own,) = call(unpack_kernel, [("v", (3, 4, 64, LANES))], [], "vv", received, to_slab)

    big = (W0, 64, LANES)
    small = (W1, 32, LANES)
    two = (W2, 16, LANES)
    three = (W3, 8, LANES)
    mid = (10, 64, LANES)
    lending = ("h", (3, 32, LANES))
    kept = [("h", (5, 8, 64, LANES)), ("h", (5,) + small), lending]
    slab_shape = (4, 64, LANES)
    full, full1, centre, kept1, lent, packet = call(
        down_first_kernel,
        [("h", (4,) + big), ("o", (3,) + small), *kept, ("o", (SLABS, 3, 4, LANES))],
        [(4,) + big, STENCILS, COARSE, DMA((12,)), big, small] + [big] * 6 + [small] * 7,
        "svvvvhh", place, own, *halo(own), stencils, coarse,
    )
    tables = [STENCILS, COARSE, BACK, DMA((12,))]
    tables += [pltpu.VMEM(s, F32) for s in ((5,) + mid, (5,) + small, (3, 32, LANES), (3, 32, LANES))]
    up_scratch = (
        [two, three, two, three]
        + [two] * 6
        + [three] * 6
        + [mid] * 6
        + [small] * 6
        + [(24, 16, LANES)]
    )
    applied, lv2, lv3 = call(
        up_first_kernel,
        [("v", (1,) + slab_shape), ("o", (3,) + two), ("o", (3,) + three)],
        tables + up_scratch,
        "ssvhhhhhhh",
        place, order, swap_all(packet), centre, kept1, *beside(lent), stencils, coarse, back,
    )
    centre, kept1, lent, before, packet = call(
        down_second_kernel,
        [*kept, ("o", slab_shape), ("o", (SLABS, 1, 4, LANES))],
        [(4,) + big, (3,) + small, STENCILS, COARSE, DMA((11,))] + [big] * 9 + [small] * 7,
        "svvvvhhhh", place, applied, *halo(applied), full, full1, stencils, coarse,
    )
    (out,) = call(
        up_second_kernel,
        [("v", (16, 16, LANES))],
        [(3,) + two, (3,) + three, slab_shape, pltpu.VMEM((512, 512), BF16)] + tables + up_scratch,
        "ssvhhhhhhhhhhh",
        place, order, swap_all(packet), centre, kept1, *beside(lent), lv2, lv3, before,
        stencils, coarse, back, to_block,
    )
    back = lax.all_to_all(out, ("gx", "gy"), 0, 0, tiled=True)
    row = (1, LANES)
    applied, part = call(
        sums_one_kernel,
        [("v", block), ("v", (SLABS, 1, LANES))],
        [],
        "svv", place, back, basis,
    )
    gathered = swap_all(part)
    next_vector, coefficients = call(
        finish_one_kernel, [("o", block), ("o", row)], [], "vvv", gathered, basis, applied
    )

    def second_sum():
        first, part = call(
            sums_two_kernel, [("o", block), ("o", (SLABS, 1, LANES))], [], "vvv", gathered, basis, applied
        )
        return tuple(
            call(
                finish_two_kernel, [("o", block), ("o", row)], [], "vvvv",
                gathered, swap_all(part), basis, first,
            )
        )

    next_vector, coefficients = lax.cond(
        coefficients[0, 9] > 0.5, second_sum, lambda: (next_vector, coefficients)
    )
    return next_vector, coefficients[0, 0:9]


def solution(mesh):
    placed = (P(None, "gx", "gy", "gz"), P("gx", "gy", "gz"), P("gx", "gy", "gz"))
    return jax.shard_map(
        local, mesh=mesh, in_specs=placed, out_specs=(P("gx", "gy", "gz"), P()), check_vma=False
    )
```

```python
import numpy as np
import jax
import jax.numpy as jnp
from jax import lax
from jax.experimental import pallas as pl
from jax.experimental.pallas import tpu as pltpu
from jax.sharding import PartitionSpec as P

AXES = ("gx", "gy", "gz")
DEGREE = 4
COARSE_DEGREE = 8
UPPER_BOUND = 2.0
SMOOTH_LOW = 0.25
COARSE_LOW = 0.05
PULL = (1.0, 0.5, 2.0)
WX, WY, WZ = PULL
WXY = (WX + WY) / 8.0
WXZ = (WX + WZ) / 8.0
WYZ = (WY + WZ) / 8.0
WXYZ = (WX + WY + WZ) / 24.0
WEIGHT_SUM = 2.0 * (WX + WY + WZ) + 4.0 * (WXY + WXZ + WYZ) + 8.0 * WXYZ
LANES = 128
SLABS = 128
CELLS = 64.0 * 64.0 * 1024.0
F32 = jnp.float32
BF16 = jnp.bfloat16
VMEM_LIMIT = 56 * 1024 * 1024

WIDTHS = (64, 32, 16, 8)


def slab_in_group(x_lo, z, odd):
    turned = z + odd * (3 - 2 * z)
    return 2 * turned + (x_lo + z + 1) % 2


def device_order():
    order = [0] * SLABS
    for gx in range(4):
        for gy in range(4):
            for gz in range(8):
                slab = 16 * gz + 2 * slab_in_group(gx // 2, gy, gz % 2) + gx % 2
                order[slab] = (gx * 4 + gy) * 8 + gz
    return order


ORDER = device_order()
HOLDERS = [[0] * 16, [0] * 16]
for _a in range(4):
    for _b in range(4):
        for _odd in (0, 1):
            HOLDERS[_odd][2 * slab_in_group(_a // 2, _b, _odd) + _a % 2] = 4 * _a + _b
CORE_SWAP = [(ORDER[s], ORDER[s ^ 1]) for s in range(SLABS)]
CHIP_SWAP = [(ORDER[s], ORDER[(s + 1 if s % 2 else s - 1) % SLABS]) for s in range(SLABS)]


def fine_to_coarse(level):
    width = WIDTHS[level]
    planes = LANES // width
    table = np.zeros((4, LANES, LANES), np.float32)
    for pack in range(4):
        for lane in range(LANES):
            z, y = divmod(lane, width)
            table[pack, lane, ((pack * planes + z) // 2) * (width // 2) + y // 2] = 1.0
    return table.reshape(4 * LANES, LANES)


def block_to_slab():
    table = np.zeros((512, 512), np.float32)
    for gy in range(4):
        for z in range(8):
            for y in range(16):
                table[gy * 128 + z * 16 + y, (z // 2) * 128 + (z % 2) * 64 + gy * 16 + y] = 1.0
    return table


def stencil_table(level):
    width = WIDTHS[level]
    planes = LANES // width
    weights = {
        (0, 1, 0): WY, (0, 0, 1): WZ, (0, 1, 1): WYZ,
        (1, 0, 0): WX, (1, 1, 0): WXY, (1, 0, 1): WXZ, (1, 1, 1): WXYZ,
    }
    table = np.zeros((2 * LANES, 2 * LANES), np.float32)
    for lane in range(LANES):
        z, y = divmod(lane, width)
        for dz in (-1, 0, 1):
            for dy in (-1, 0, 1):
                if not 0 <= y + dy < width:
                    continue
                outside = not 0 <= z + dz < planes
                source = outside * LANES + (z + dz) % planes * width + y + dy
                for dx in (0, 1):
                    if (dx, abs(dy), abs(dz)) in weights:
                        weight = round(48.0 * weights[dx, abs(dy), abs(dz)]) / 2.0
                        table[source, dx * LANES + lane] += weight
    return table


RESTRICT = [fine_to_coarse(level) for level in range(3)]
TO_SLAB = block_to_slab()
STENCIL = [stencil_table(level) for level in range(4)]


def table_dot(a, table, parts=2):
    total = None
    rest = a
    for part_number in range(parts):
        part = rest.astype(BF16)
        if part_number + 1 < parts:
            rest = rest - part.astype(F32)
        term = jnp.dot(part, table, preferred_element_type=F32)
        total = term if total is None else total + term
    return total


class Level:
    def __init__(self, index, table, diff, diag, inv, side, x, r, q, dq):
        self.width = self.rows = WIDTHS[index]
        self.table = table
        self.diff, self.diag, self.inv, self.side = diff, diag, inv, side
        self.x, self.r, self.q, self.dq = x, r, q, dq

    def get(self, ref, lo, hi):
        return ref[lo:hi].reshape((hi - lo) * self.rows, LANES)

    def put(self, ref, lo, hi, value):
        ref[lo:hi] = value.reshape(hi - lo, self.rows, LANES)

    def spread(self, ref, lo, hi):
        n = (hi - lo) * self.rows
        lane = lax.broadcasted_iota(jnp.int32, (n, LANES), 1)
        row = lax.broadcasted_iota(jnp.int32, (n, LANES), 0) % self.rows
        here = self.get(ref, lo, hi)
        beside = jnp.where(
            lane < self.width, self.get(ref, lo + 1, hi + 1), self.get(ref, lo - 1, hi - 1)
        )
        out = table_dot(jnp.concatenate([here, beside], axis=1), self.table[...])
        next_x = out[:, LANES:]
        return (
            out[:, :LANES]
            + jnp.where(row == self.rows - 1, 0.0, pltpu.roll(next_x, n - 1, 0))
            + jnp.where(row == 0, 0.0, pltpu.roll(next_x, 1, 0))
        )

    def operate(self, lo, hi, u, du):
        both = self.get(self.diff, lo, hi) * self.spread(u, lo, hi) + self.spread(du, lo, hi)
        return self.get(self.diag, lo, hi) * self.get(u, lo, hi) - (1.0 / 48.0) * both

    def set_diagonal(self, lo, hi, reaction):
        d = self.get(self.diff, lo, hi)
        diag = self.get(reaction, lo, hi) + (
            (0.5 * WEIGHT_SUM) * d + (1.0 / 48.0) * self.spread(self.diff, lo, hi)
        )
        self.put(self.diag, lo, hi, diag)
        self.put(self.inv, lo, hi, jnp.where(d > 0.0, 1.0 / diag, 0.0))

    def residual(self, lo, hi, out, u, du):
        self.put(out, lo, hi, self.get(self.side, lo, hi) - self.operate(lo, hi, u, du))

    def scale_x(self, lo, hi, out):
        self.put(out, lo, hi, self.get(self.diff, lo, hi) * self.get(self.x, lo, hi))

    def smooth(self, ranges, degree, lower, fresh, keep):
        middle = 0.5 * (UPPER_BOUND + lower)
        radius = 0.5 * (UPPER_BOUND - lower)
        ratio = middle / radius
        rho = 1.0 / ratio

        lo, hi = ranges[0]
        if fresh:
            r = self.get(self.side, lo, hi)
            self.put(self.r, lo, hi, r)
        else:
            r = self.get(self.r, lo, hi)
        q = self.get(self.inv, lo, hi) * r * (1.0 / middle)
        self.put(self.q[0], lo, hi, q)
        self.put(self.dq[0], lo, hi, self.get(self.diff, lo, hi) * q)
        self.put(self.x, lo, hi, q if fresh else self.get(self.x, lo, hi) + q)
        now = 0
        for turn in range(1, degree):
            rho_next = 1.0 / (2.0 * ratio - rho)
            a, b = rho_next * rho, 2.0 * rho_next / radius
            rho = rho_next
            u, du, v, dv = self.q[now], self.dq[now], self.q[1 - now], self.dq[1 - now]
            lo, hi = ranges[turn]
            r = self.get(self.r, lo, hi) - self.operate(lo, hi, u, du)
            q = a * self.get(u, lo, hi) + b * (self.get(self.inv, lo, hi) * r)
            x = self.get(self.x, lo, hi) + q
            self.put(self.x, lo, hi, x)
            if turn + 1 < degree:
                self.put(self.r, lo, hi, r)
                self.put(v, lo, hi, q)
                self.put(dv, lo, hi, self.get(self.diff, lo, hi) * q)
            elif keep:
                self.put(dv, lo, hi, self.get(self.diff, lo, hi) * x)
            now = 1 - now
        return self.dq[now]

    def row_pairs(self, ref, lo, hi):
        half = self.rows // 2
        return ref[lo:hi, pl.ds(0, half, 2), :] + ref[lo:hi, pl.ds(1, half, 2), :]

    def restricted(self, ref, lo, count, table):
        half = self.rows // 2
        pairs = self.row_pairs(ref, lo, lo + 4 * count).reshape(count, 4, half, LANES)
        wide = jnp.concatenate(
            [pairs[:, j].reshape(count * half, LANES) for j in range(4)], axis=1
        )
        return table_dot(wide, table[...]).reshape(count, half, LANES)

    def add_rows(self, k, fine):
        half = self.rows // 2
        for place in range(2):
            at = pl.ds(place, half, 2)
            self.x[k, at, :] = self.x[k, at, :] + fine


W0 = 22
W1 = 7
W2 = 14
W3 = 5
DMA = pltpu.SemaphoreType.DMA
STENCILS = pltpu.VMEM((4, 256, 256), BF16)
COARSE = pltpu.VMEM((3, 512, LANES), BF16)
BACK = pltpu.VMEM((3, LANES, 512), BF16)
SPACES = {"s": pltpu.SMEM, "v": pltpu.VMEM, "h": pltpu.HBM}


def call(kernel, outs, scratch, spaces, *args):
    made = []
    for space, shape in outs:
        if space == "v":
            made.append(pltpu.VMEM(shape, F32))
        else:
            made.append(jax.ShapeDtypeStruct(shape, F32))
    given = [
        pltpu.with_memory_space_constraint(a, pltpu.VMEM) if space == "v" else a
        for space, a in zip(spaces, args)
    ]
    return pl.pallas_call(
        kernel,
        out_shape=made,
        in_specs=[pl.BlockSpec(memory_space=SPACES[space]) for space in spaces],
        out_specs=[
            pl.BlockSpec(memory_space=pltpu.HBM if space == "h" else pltpu.VMEM) for space, _ in outs
        ],
        scratch_shapes=[pltpu.VMEM(s, F32) if isinstance(s, tuple) else s for s in scratch],
        compiler_params=pltpu.CompilerParams(vmem_limit_bytes=VMEM_LIMIT),
    )(*given)


def bring(sems, *pairs):
    copies = [pltpu.make_async_copy(a, b, sems.at[i]) for i, (a, b) in enumerate(pairs)]
    for copy in copies:
        copy.start()
    return copies


def wait(copies):
    for copy in copies:
        copy.wait()


def turn_eighths(x):
    row = lax.broadcasted_iota(jnp.int32, x.shape, 1)
    lane = lax.broadcasted_iota(jnp.int32, x.shape, 2) // 16
    total = jnp.where(lane == row, x, 0.0)
    for step in range(1, 8):
        moved = pltpu.roll(pltpu.roll(x, 16 * step, 2), 8 - step, 1)
        total = jnp.where((lane - row) % 8 == step, moved, total)
    return total


def holder(place, slab):
    odd = place[2]
    return jnp.where(odd == 1, HOLDERS[1][slab], HOLDERS[0][slab])


def pack_kernel(place, basis, diffusion, reaction, parts, fields, sems):
    copies = bring(
        sems, (basis.at[7], fields.at[0]), (diffusion, fields.at[1]), (reaction, fields.at[2])
    )
    for f in range(3):
        copies[f].wait()
        turned = fields[f].reshape(256, LANES).T
        for half in range(2):
            pieces = turn_eighths(
                turned[:, half * LANES : (half + 1) * LANES].reshape(16, 8, LANES)
            )
            for slab in range(16):
                parts[holder(place, slab), f, 8 * half : 8 * half + 8] = pieces[slab]


def to_blocks(place, received):
    wide = []
    for half in range(2):
        pieces = [
            received[holder(place, slab), 8 * half : 8 * half + 8][None] for slab in range(16)
        ]
        wide.append(turn_eighths(jnp.concatenate(pieces, axis=0)).reshape(LANES, LANES))
    return jnp.concatenate(wide, axis=1).T.reshape(16, 16, LANES)


def unpack_kernel(received, table, own):
    fields = own.shape[0]
    for f in range(fields):
        rows = []
        for gx in range(4):
            rows.append(jnp.concatenate([received[gx * 4 + gy, f] for gy in range(4)], axis=1))
        wide = table_dot(jnp.concatenate(rows, axis=0), table[...], 3)
        for k in range(4):
            own[f, k] = wide[:, k * LANES : (k + 1) * LANES]


def assemble(place, pieces, field, window):
    slab, core = place[0], place[1]
    sign = 1 - 2 * core
    clear(window.at[0], window.at[W0 - 1])
    for side, distance, ref, base in pieces:
        slot = 2 + side * sign * distance
        inside = jnp.logical_and(slab + slot - 2 >= 0, slab + slot - 2 < SLABS)
        window[pl.ds(1 + 4 * slot, 4)] = jnp.where(inside, ref[base + field], 0.0)


def clear(*refs):
    for ref in refs:
        ref[...] = jnp.zeros_like(ref)


def clear_ends(count, *refs):
    for ref in refs:
        size = ref.shape[0]
        clear(ref.at[0:count], ref.at[size - count : size])


def down_level0(level, level1, table):
    clear_ends(2, *level.q, *level.dq)
    dx = level.smooth([(1, 21), (2, 20), (2, 20), (3, 19)], DEGREE, SMOOTH_LOW, True, True)
    level.residual(4, 18, level.r, level.x, dx)
    clear_ends(1, level1.side)
    level1.side[1:6] = level.restricted(level.r, 1, 5, table)


def down_level1(level, table):
    clear(*level.q, *level.dq)
    dx = level.smooth([(1, 6), (2, 5), (2, 5), (2, 5)], DEGREE, SMOOTH_LOW, True, True)
    level.residual(3, 4, level.r, level.x, dx)
    return own_quarter(level, level.r, table)


def own_quarter(level, ref, table):
    return table_dot(level.row_pairs(ref, 3, 4)[0], table[0:LANES])


def turn_quarters(x):
    group = lax.broadcasted_iota(jnp.int32, (16, LANES), 0) // 4
    lane = lax.broadcasted_iota(jnp.int32, (16, LANES), 1) // 32
    total = jnp.where(lane == group, x, 0.0)
    for step in range(1, 4):
        moved = pltpu.roll(pltpu.roll(x, 32 * step, 1), 16 - 4 * step, 0)
        total = jnp.where((lane - group) % 4 == step, moved, total)
    return total


def to_all(packet, field, quarter):
    rows = turn_quarters(quarter)[0:4]
    packet[:, field] = jnp.broadcast_to(rows[None], (SLABS, 4, LANES))


def keep_early(sems, level, level1, centre, kept1):
    pairs = [
        (ref.at[7:15], centre.at[1 + i])
        for i, ref in enumerate((level.side, level.diff, level.diag, level.inv))
    ]
    pairs += [
        (ref, kept1.at[2 + i]) for i, ref in enumerate((level1.diff, level1.diag, level1.inv))
    ]
    return bring(sems, *pairs)


def keep_late(sems, level1, kept1, lent):
    pairs = [
        (level1.x, kept1.at[0]),
        (level1.side, kept1.at[1]),
        (level1.x.at[2:5], lent),
    ]
    return bring(sems, *pairs)


def make_levels(tables, full, side, work0, full1, work1):
    x, r, qa, qb, da, db = work0
    side1, x1, r1, q1a, q1b, d1a, d1b = work1
    level = Level(0, tables[0], full.at[1], full.at[2], full.at[3], side, x, r, [qa, qb], [da, db])
    level1 = Level(
        1, tables[1], full1.at[0], full1.at[1], full1.at[2], side1, x1, r1, [q1a, q1b], [d1a, d1b]
    )
    return level, level1


def down_first_kernel(
    place, own, near, near2, mate, far, stencils_in, coarse_in,
    full_out, full1, centre, kept1, lent, packet,
    full, stencils, coarse, sems, react, react1, *work
):
    work0, work1 = work[0:6], work[6:13]
    tables, coarse0, coarse1 = [stencils.at[0], stencils.at[1]], coarse.at[0], coarse.at[1]
    arriving = bring(
        sems, (stencils_in.at[0:2], stencils.at[0:2]), (coarse_in.at[0:2], coarse.at[0:2])
    )
    for i in (2, 3):
        clear_ends(1, full.at[i])
    clear(full1, work1[1], work1[2])
    pieces = [
        (-1, 0, own, 0), (-1, 1, near, 0), (-1, 2, near2, 0), (1, 1, mate, 0), (1, 2, far, 0)
    ]
    assemble(place, pieces, 0, full.at[0])
    assemble(place, pieces, 1, full.at[1])
    assemble(place, pieces, 2, react)
    level, level1 = make_levels(tables, full, full.at[0], work0, full1, work1)
    wait(arriving)
    level.set_diagonal(1, 21, react)
    leaving = bring(sems, (full, full_out))
    level1.diff[1:6] = 0.25 * level.restricted(level.diff, 1, 5, coarse0)
    react1[1:6] = level.restricted(react, 1, 5, coarse0)
    level1.set_diagonal(1, 6, react1)
    leaving += keep_early(sems.at[1:8], level, level1, centre, kept1)
    down_level0(level, level1, coarse0)
    leaving += bring(sems.at[11:12], (level.x.at[7:15], centre.at[0]))
    to_all(packet, 0, down_level1(level1, coarse1))
    to_all(packet, 1, 0.25 * own_quarter(level1, level1.diff, coarse1))
    to_all(packet, 2, own_quarter(level1, react1, coarse1))
    wait(leaving + keep_late(sems.at[8:11], level1, kept1, lent))


def down_second_kernel(
    place, own, near, near2, mate, far, full_in, full1_in, stencils_in, coarse_in,
    centre, kept1, lent, before, packet,
    full, full1, stencils, coarse, sems, window, dwin, side, *work
):
    work0, work1 = work[0:6], work[6:13]
    tables, coarse0, coarse1 = [stencils.at[0], stencils.at[1]], coarse.at[0], coarse.at[1]
    arriving = bring(
        sems,
        (full_in.at[1], full.at[1]),
        (stencils_in.at[0:2], stencils.at[0:2]),
        (full_in.at[2], full.at[2]),
        (full_in.at[0], full.at[0]),
        (full_in.at[3], full.at[3]),
        (coarse_in.at[0:2], coarse.at[0:2]),
        (full1_in, full1),
    )
    before[...] = own[0]
    clear(work1[1], work1[2])
    clear_ends(1, side)
    pieces = [
        (-1, 0, own, 0), (-1, 1, near, 0), (-1, 2, near2, 0), (1, 1, mate, 0), (1, 2, far, 0)
    ]
    assemble(place, pieces, 0, window)
    wait(arriving[0:1])
    dwin[...] = window[...] * full[1]
    wait(arriving[1:4])
    source, _ = make_levels(tables, full, full.at[0], work0, full1, work1)
    source.residual(1, 21, side, window, dwin)
    wait(arriving[4:])
    level, level1 = make_levels(tables, full, side, work0, full1, work1)
    down_level0(level, level1, coarse0)
    leaving = keep_early(sems.at[0:7], level, level1, centre, kept1)
    leaving += bring(sems.at[10:11], (level.x.at[7:15], centre.at[0]))
    to_all(packet, 0, down_level1(level1, coarse1))
    wait(leaving + keep_late(sems.at[7:10], level1, kept1, lent))


def gather_level2(place, order, packets, field, target):
    clear_ends(1, target)
    start = place[0] - place[0] % 16 - 16
    for pack in range(12):
        slab = start + 4 * pack
        inside = jnp.logical_and(slab >= 0, slab < SLABS)
        pieces = [packets[order[jnp.clip(slab + j, 0, SLABS - 1)], field] for j in range(4)]
        value = turn_quarters(jnp.concatenate(pieces, axis=0))
        target[1 + pack] = jnp.where(inside, value, 0.0)


def coarse_part(first, arriving, place, order, packets, tables, lv2, lv3, f2, f3, react2, react3, work2, work3, coarse2, back2):
    x2, r2, q2a, q2b, d2a, d2b = work2
    x3, r3, q3a, q3b, d3a, d3b = work3
    clear(*work2[2:])
    clear(*work3[2:])
    clear_ends(1, x2)
    level2 = Level(2, tables[2], lv2.at[0], lv2.at[1], lv2.at[2], f2, x2, r2, [q2a, q2b], [d2a, d2b])
    level3 = Level(3, tables[3], lv3.at[0], lv3.at[1], lv3.at[2], f3, x3, r3, [q3a, q3b], [d3a, d3b])
    gather_level2(place, order, packets, 0, f2)
    clear_ends(1, f3)
    if not first:
        wait(arriving)
    if first:
        clear_ends(1, lv2.at[1], lv2.at[2], lv3.at[0], lv3.at[1], lv3.at[2], react3)
        gather_level2(place, order, packets, 1, lv2.at[0])
        gather_level2(place, order, packets, 2, react2)
        wait(arriving)
        level2.set_diagonal(1, 13, react2)
        level3.diff[1:4] = 0.25 * level2.restricted(level2.diff, 1, 3, coarse2)
        react3[1:4] = level2.restricted(react2, 1, 3, coarse2)
        level3.set_diagonal(1, 4, react3)
    whole2 = [(1, 13)] * 4
    dx = level2.smooth(whole2, DEGREE, SMOOTH_LOW, True, True)
    level2.residual(1, 13, r2, x2, dx)
    f3[1:4] = level2.restricted(r2, 1, 3, coarse2)
    level3.smooth([(1, 4)] * 8, COARSE_DEGREE, COARSE_LOW, True, False)
    fine = table_dot(level3.get(x3, 1, 4), back2[...])
    for t in range(3):
        for j in range(4):
            level2.add_rows(1 + 4 * t + j, fine[t * 8 : t * 8 + 8, j * LANES : (j + 1) * LANES])
    level2.scale_x(1, 13, dx)
    level2.residual(1, 13, r2, x2, dx)
    level2.smooth(whole2, DEGREE, SMOOTH_LOW, False, False)
    return x2


def up_part(place, x2, spaced, tables, centre, kept1, swapped, mate, work0, work1, back0, back1):
    x, r, qa, qb, da, db = work0
    x1, r1, q1a, q1b, d1a, d1b = work1
    clear(*work0[2:])
    clear(*work1[2:])
    slab, core = place[0], place[1]
    for pack in range(3, 9):
        value = x2[1 + pack]
        for j in range(4):
            spaced[4 * pack + j - 12] = pltpu.roll(value, LANES - 32 * j, 1) if j else value
    level1 = Level(
        1, tables[1], kept1.at[2], kept1.at[3], kept1.at[4], kept1.at[1], x1, r1,
        [q1a, q1b], [d1a, d1b],
    )
    level = Level(
        0, tables[0], centre.at[2], centre.at[3], centre.at[4], centre.at[1], x, r,
        [qa, qb], [da, db],
    )
    x1[...] = kept1[0]
    x[...] = centre[0]
    half = lax.broadcasted_iota(jnp.int32, (32, LANES), 1) < 64
    below, above = slab > 0, slab < SLABS - 1
    first_core = core == 0

    def beside(pack, is_below):
        mine, others = (swapped, mate) if is_below else (mate, swapped)
        value = jnp.where(first_core, mine[pack], others[pack])
        return jnp.where(below if is_below else above, value, 0.0)

    x1[1] = beside(0, True)
    x1[2] = jnp.where(half, beside(1, True), x1[2])
    x1[4] = jnp.where(half, x1[4], beside(1, False))
    x1[5] = beside(2, False)
    start = slab % 16 + 2
    fine = table_dot(spaced[pl.ds(start, 5)].reshape(5 * 16, LANES), back1[:, 0:LANES])
    for t in range(5):
        level1.add_rows(1 + t, fine[t * 16 : t * 16 + 16])
    level1.scale_x(1, 6, d1b)
    level1.residual(1, 6, r1, x1, d1b)
    level1.smooth([(1, 6), (2, 5), (2, 5), (2, 5)], DEGREE, SMOOTH_LOW, False, False)
    fine = table_dot(level1.get(x1, 2, 5), back0[...])
    for k in range(8):
        t, j = divmod(2 + k, 4)
        level.add_rows(1 + k, fine[t * 32 : t * 32 + 32, j * LANES : (j + 1) * LANES])
    level.scale_x(1, 9, db)
    level.residual(1, 9, r, x, db)
    level.smooth([(1, 9), (2, 8), (2, 8), (3, 7)], DEGREE, SMOOTH_LOW, False, False)
    return x


def up_kernel(first, place, order, packets, centre_in, kept1_in, swapped_in, mate_in, *refs):
    if first:
        (stencils_in, coarse_in, back_in, applied, lv2, lv3), refs = refs[0:6], refs[6:]
        early, later = [], []
    else:
        (lv2_in, lv3_in, before_in, stencils_in, coarse_in, back_in), refs = refs[0:6], refs[6:]
        (to_block_in, out, lv2, lv3, before, to_block), refs = refs[0:6], refs[6:]
        early = [(lv2_in, lv2), (lv3_in, lv3)]
        later = [(before_in, before), (to_block_in, to_block)]
    (stencils, coarse, back, sems, centre, kept1, swapped, mate), refs = refs[0:8], refs[8:]
    early += [(stencils_in, stencils), (coarse_in.at[2], coarse.at[2]), (back_in, back)]
    later += [
        (kept1_in, kept1), (centre_in, centre.at[:, 1:9]), (swapped_in, swapped), (mate_in, mate)
    ]
    arriving = bring(sems.at[0:6], *early)
    arriving_later = bring(sems.at[6:12], *later)
    clear(centre.at[:, 0], centre.at[:, 9])
    tables = [stencils.at[i] for i in range(4)]
    coarse2, back0, back1, back2 = coarse.at[2], back.at[0], back.at[1], back.at[2]
    f2, f3, react2, react3 = refs[0:4]
    work2, work3, work0, work1, spaced = refs[4:10], refs[10:16], refs[16:22], refs[22:28], refs[28]
    x2 = coarse_part(
        first, arriving, place, order, packets, tables, lv2, lv3, f2, f3, react2, react3, work2, work3, coarse2, back2
    )
    wait(arriving_later)
    x = up_part(
        place, x2, spaced, tables, centre, kept1, swapped, mate, work0, work1, back0, back1
    )
    if first:
        applied[0] = x[3:7]
    else:
        wide = jnp.concatenate([before[k] + x[3 + k] for k in range(4)], axis=1)
        pieces = table_dot(wide, to_block[...], 3)
        for gx in range(4):
            for gy in range(4):
                out[gx * 4 + gy] = pieces[gx * 16 : (gx + 1) * 16, gy * LANES : (gy + 1) * LANES]


def up_first_kernel(*refs):
    up_kernel(True, *refs)


def up_second_kernel(*refs):
    up_kernel(False, *refs)


def row_of_sums(rows):
    stacked = jnp.concatenate(
        [jnp.sum(jnp.sum(a, axis=0), axis=0, keepdims=True) for _, a in rows], axis=0
    )
    totals = jnp.sum(stacked, axis=1, keepdims=True)
    lane = lax.broadcasted_iota(jnp.int32, (1, LANES), 1)
    out = jnp.zeros((1, LANES), F32)
    for i, (lanes, _) in enumerate(rows):
        for at in lanes:
            out = jnp.where(lane == at, totals[i : i + 1], out)
    return out


def sums_one_kernel(place, received, basis, applied, out):
    applied[...] = to_blocks(place, received)
    rows = [([8 * j + k, 8 * k + j], basis[j] * basis[k]) for j in range(8) for k in range(j, 8)]
    rows += [([64 + k], basis[k] * applied[...]) for k in range(8)]
    rows += [([72], applied[...] * applied[...])]
    out[...] = jnp.broadcast_to(row_of_sums(rows)[None], (SLABS, 1, LANES))


def read_sums(gathered):
    totals = jnp.sum(gathered[...], axis=0)
    row = lax.broadcasted_iota(jnp.int32, (8, LANES), 0)
    lane = lax.broadcasted_iota(jnp.int32, (8, LANES), 1)
    gram = jnp.zeros((8, LANES), F32)
    wide = jnp.broadcast_to(totals, (8, LANES))
    for j in range(8):
        gram = jnp.where(row == j, pltpu.roll(wide, (LANES - 8 * j) % LANES, 1), gram)
    gram = jnp.where(lane < 8, gram, 0.0)
    proj = jnp.where(lane < 8, pltpu.roll(wide, LANES - 64, 1), 0.0)[0:1]
    return gram, proj, totals[:, 72:73]


def column(row_vector):
    row = lax.broadcasted_iota(jnp.int32, (8, LANES), 0)
    lane = lax.broadcasted_iota(jnp.int32, (8, LANES), 1)
    return jnp.sum(jnp.where(row == lane, row_vector, 0.0), axis=1, keepdims=True)


def as_row(column_vector):
    row = lax.broadcasted_iota(jnp.int32, (8, LANES), 0)
    lane = lax.broadcasted_iota(jnp.int32, (8, LANES), 1)
    return jnp.sum(jnp.where(row == lane, column_vector, 0.0), axis=0, keepdims=True)


def times(gram, row_vector):
    return jnp.sum(gram * row_vector, axis=1, keepdims=True)


def dot8(a, b):
    return jnp.sum(a * b, axis=0, keepdims=True)


def finish(gram, proj_two, squares, coeff_one, base, basis, weights_of, out, coefficients, near):
    coeff_two = proj_two * (1.0 / CELLS)
    quadratic = dot8(coeff_two, times(gram, as_row(coeff_two)))
    mean_square = (squares - 2.0 * dot8(coeff_two, proj_two) + quadratic) * (1.0 / CELLS)
    length = jnp.sqrt(mean_square + 1e-06)
    value = base[...]
    subtract = weights_of(coeff_two)
    for k in range(8):
        value = value - subtract[k : k + 1].reshape(1, 1, 1) * basis[k]
    out[...] = value * (1.0 / length).reshape(1, 1, 1)
    lane = lax.broadcasted_iota(jnp.int32, (1, LANES), 1)
    row = as_row(coeff_one + coeff_two)
    coefficients[...] = jnp.where(lane == 8, length, jnp.where(lane == 9, near, row))


def finish_one_kernel(gathered, basis, applied, out, coefficients):
    gram, proj, square = read_sums(gathered)
    one_row = proj * (1.0 / CELLS)
    one, proj = column(one_row), column(proj)
    image = times(gram, one_row)
    proj_two = proj - image
    squares = square - 2.0 * dot8(one, proj) + dot8(one, image)
    near = jnp.where(squares > 0.02 * square, 0.0, 1.0)
    finish(
        gram, proj_two, squares, one, applied, basis, lambda two: one + two, out, coefficients, near
    )


def sums_two_kernel(gathered, basis, applied, first, out):
    _, proj, _ = read_sums(gathered)
    one = column(proj * (1.0 / CELLS))
    value = applied[...]
    for k in range(8):
        value = value - one[k : k + 1].reshape(1, 1, 1) * basis[k]
    first[...] = value
    sums = row_of_sums([([64 + k], basis[k] * value) for k in range(8)] + [([72], value * value)])
    out[...] = jnp.broadcast_to(sums[None], (SLABS, 1, LANES))


def finish_two_kernel(gathered, gathered_two, basis, first, out, coefficients):
    gram, proj, _ = read_sums(gathered)
    _, proj_two, squares = read_sums(gathered_two)
    one = column(proj * (1.0 / CELLS))
    near = jnp.zeros((1, 1), F32)
    finish(
        gram, column(proj_two), squares, one, first, basis, lambda two: two, out, coefficients, near
    )


def swap_all(x):
    return lax.all_to_all(x, AXES, 0, 0, tiled=True)


def halo(own):
    near = lax.ppermute(own, AXES, CHIP_SWAP)
    mate = lax.ppermute(own, AXES, CORE_SWAP)
    near2 = lax.ppermute(mate, AXES, CHIP_SWAP)
    far = lax.ppermute(near, AXES, CORE_SWAP)
    return near, near2, mate, far


def beside(lent):
    return lax.ppermute(lent, AXES, CHIP_SWAP), lax.ppermute(lent, AXES, CORE_SWAP)


def local(basis, diffusion, reaction):
    gx, gy, gz = (lax.axis_index(a) for a in AXES)
    odd = gz % 2
    core = gx % 2
    slab = 16 * gz + 2 * slab_in_group(gx // 2, gy, odd) + core
    place = jnp.stack([slab, core, odd]).astype(jnp.int32)
    order = jnp.asarray(ORDER, jnp.int32)
    stencils = jnp.asarray(np.stack(STENCIL), BF16)
    coarse = jnp.asarray(np.stack(RESTRICT), BF16)
    back = jnp.asarray(np.stack([t.T for t in RESTRICT]), BF16)
    to_slab = jnp.asarray(TO_SLAB, BF16)
    to_block = jnp.asarray(TO_SLAB.T, BF16)
    block = (16, 16, LANES)
    (parts,) = call(
        pack_kernel,
        [("v", (16, 3, 16, LANES))],
        [(3,) + block, DMA((3,))],
        "shhh", place, basis, diffusion, reaction,
    )
    received = lax.all_to_all(parts, ("gx", "gy"), 0, 0, tiled=True)
    (own,) = call(unpack_kernel, [("v", (3, 4, 64, LANES))], [], "vv", received, to_slab)

    big = (W0, 64, LANES)
    small = (W1, 32, LANES)
    two = (W2, 16, LANES)
    three = (W3, 8, LANES)
    mid = (10, 64, LANES)
    lending = ("h", (3, 32, LANES))
    kept = [("h", (5, 8, 64, LANES)), ("h", (5,) + small), lending]
    slab_shape = (4, 64, LANES)
    full, full1, centre, kept1, lent, packet = call(
        down_first_kernel,
        [("h", (4,) + big), ("o", (3,) + small), *kept, ("o", (SLABS, 3, 4, LANES))],
        [(4,) + big, STENCILS, COARSE, DMA((12,)), big, small] + [big] * 6 + [small] * 7,
        "svvvvvhh", place, own, *halo(own), stencils, coarse,
    )
    tables = [STENCILS, COARSE, BACK, DMA((12,))]
    tables += [pltpu.VMEM(s, F32) for s in ((5,) + mid, (5,) + small, (3, 32, LANES), (3, 32, LANES))]
    up_scratch = (
        [two, three, two, three]
        + [two] * 6
        + [three] * 6
        + [mid] * 6
        + [small] * 6
        + [(24, 16, LANES)]
    )
    applied, lv2, lv3 = call(
        up_first_kernel,
        [("v", (1,) + slab_shape), ("o", (3,) + two), ("o", (3,) + three)],
        tables + up_scratch,
        "ssvhhhhhhh",
        place, order, swap_all(packet), centre, kept1, *beside(lent), stencils, coarse, back,
    )
    centre, kept1, lent, before, packet = call(
        down_second_kernel,
        [*kept, ("o", slab_shape), ("o", (SLABS, 1, 4, LANES))],
        [(4,) + big, (3,) + small, STENCILS, COARSE, DMA((11,))] + [big] * 9 + [small] * 7,
        "svvvvvhhhh", place, applied, *halo(applied), full, full1, stencils, coarse,
    )
    (out,) = call(
        up_second_kernel,
        [("v", (16, 16, LANES))],
        [(3,) + two, (3,) + three, slab_shape, pltpu.VMEM((512, 512), BF16)] + tables + up_scratch,
        "ssvhhhhhhhhhhh",
        place, order, swap_all(packet), centre, kept1, *beside(lent), lv2, lv3, before,
        stencils, coarse, back, to_block,
    )
    back = lax.all_to_all(out, ("gx", "gy"), 0, 0, tiled=True)
    row = (1, LANES)
    applied, part = call(
        sums_one_kernel,
        [("v", block), ("v", (SLABS, 1, LANES))],
        [],
        "svv", place, back, basis,
    )
    gathered = swap_all(part)
    next_vector, coefficients = call(
        finish_one_kernel, [("o", block), ("o", row)], [], "vvv", gathered, basis, applied
    )

    def second_sum():
        first, part = call(
            sums_two_kernel, [("o", block), ("o", (SLABS, 1, LANES))], [], "vvv", gathered, basis, applied
        )
        return tuple(
            call(
                finish_two_kernel, [("o", block), ("o", row)], [], "vvvv",
                gathered, swap_all(part), basis, first,
            )
        )

    next_vector, coefficients = lax.cond(
        coefficients[0, 9] > 0.5, second_sum, lambda: (next_vector, coefficients)
    )
    return next_vector, coefficients[0, 0:9]


def solution(mesh):
    placed = (P(None, "gx", "gy", "gz"), P("gx", "gy", "gz"), P("gx", "gy", "gz"))
    return jax.shard_map(
        local, mesh=mesh, in_specs=placed, out_specs=(P("gx", "gy", "gz"), P()), check_vma=False
    )
```

```python
import numpy as np
import jax
import jax.numpy as jnp
from jax import lax
from jax.experimental import pallas as pl
from jax.experimental.pallas import tpu as pltpu
from jax.sharding import PartitionSpec as P

AXES = ("gx", "gy", "gz")
DEGREE = 4
COARSE_DEGREE = 8
UPPER_BOUND = 2.0
SMOOTH_LOW = 0.25
COARSE_LOW = 0.05
PULL = (1.0, 0.5, 2.0)
WX, WY, WZ = PULL
WXY = (WX + WY) / 8.0
WXZ = (WX + WZ) / 8.0
WYZ = (WY + WZ) / 8.0
WXYZ = (WX + WY + WZ) / 24.0
WEIGHT_SUM = 2.0 * (WX + WY + WZ) + 4.0 * (WXY + WXZ + WYZ) + 8.0 * WXYZ
LANES = 128
SLABS = 128
CELLS = 64.0 * 64.0 * 1024.0
F32 = jnp.float32
BF16 = jnp.bfloat16
VMEM_LIMIT = 56 * 1024 * 1024

WIDTHS = (64, 32, 16, 8)


def slab_in_group(x_lo, z, odd):
    turned = z + odd * (3 - 2 * z)
    return 2 * turned + (x_lo + z + 1) % 2


def device_order():
    order = [0] * SLABS
    for gx in range(4):
        for gy in range(4):
            for gz in range(8):
                slab = 16 * gz + 2 * slab_in_group(gx // 2, gy, gz % 2) + gx % 2
                order[slab] = (gx * 4 + gy) * 8 + gz
    return order


ORDER = device_order()
HOLDERS = [[0] * 16, [0] * 16]
for _a in range(4):
    for _b in range(4):
        for _odd in (0, 1):
            HOLDERS[_odd][2 * slab_in_group(_a // 2, _b, _odd) + _a % 2] = 4 * _a + _b
CORE_SWAP = [(ORDER[s], ORDER[s ^ 1]) for s in range(SLABS)]
CHIP_SWAP = [(ORDER[s], ORDER[(s + 1 if s % 2 else s - 1) % SLABS]) for s in range(SLABS)]


def fine_to_coarse(level):
    width = WIDTHS[level]
    planes = LANES // width
    table = np.zeros((4, LANES, LANES), np.float32)
    for pack in range(4):
        for lane in range(LANES):
            z, y = divmod(lane, width)
            table[pack, lane, ((pack * planes + z) // 2) * (width // 2) + y // 2] = 1.0
    return table.reshape(4 * LANES, LANES)


def block_to_slab():
    table = np.zeros((512, 512), np.float32)
    for gy in range(4):
        for z in range(8):
            for y in range(16):
                table[gy * 128 + z * 16 + y, (z // 2) * 128 + (z % 2) * 64 + gy * 16 + y] = 1.0
    return table


def stencil_table(level):
    width = WIDTHS[level]
    planes = LANES // width
    weights = {
        (0, 1, 0): WY, (0, 0, 1): WZ, (0, 1, 1): WYZ,
        (1, 0, 0): WX, (1, 1, 0): WXY, (1, 0, 1): WXZ, (1, 1, 1): WXYZ,
    }
    table = np.zeros((2 * LANES, 2 * LANES), np.float32)
    for lane in range(LANES):
        z, y = divmod(lane, width)
        for dz in (-1, 0, 1):
            for dy in (-1, 0, 1):
                if not 0 <= y + dy < width:
                    continue
                outside = not 0 <= z + dz < planes
                source = outside * LANES + (z + dz) % planes * width + y + dy
                for dx in (0, 1):
                    if (dx, abs(dy), abs(dz)) in weights:
                        weight = round(48.0 * weights[dx, abs(dy), abs(dz)]) / 2.0
                        table[source, dx * LANES + lane] += weight
    return table


RESTRICT = [fine_to_coarse(level) for level in range(3)]
TO_SLAB = block_to_slab()
STENCIL = [stencil_table(level) for level in range(4)]


def table_dot(a, table, parts=2):
    total = None
    rest = a
    for part_number in range(parts):
        part = rest.astype(BF16)
        if part_number + 1 < parts:
            rest = rest - part.astype(F32)
        term = jnp.dot(part, table, preferred_element_type=F32)
        total = term if total is None else total + term
    return total


class Level:
    def __init__(self, index, table, diff, diag, inv, side, x, r, q, dq):
        self.width = self.rows = WIDTHS[index]
        self.table = table
        self.diff, self.diag, self.inv, self.side = diff, diag, inv, side
        self.x, self.r, self.q, self.dq = x, r, q, dq

    def get(self, ref, lo, hi):
        return ref[lo:hi].reshape((hi - lo) * self.rows, LANES)

    def put(self, ref, lo, hi, value):
        ref[lo:hi] = value.reshape(hi - lo, self.rows, LANES)

    def spread(self, ref, lo, hi):
        n = (hi - lo) * self.rows
        lane = lax.broadcasted_iota(jnp.int32, (n, LANES), 1)
        row = lax.broadcasted_iota(jnp.int32, (n, LANES), 0) % self.rows
        here = self.get(ref, lo, hi)
        beside = jnp.where(
            lane < self.width, self.get(ref, lo + 1, hi + 1), self.get(ref, lo - 1, hi - 1)
        )
        out = table_dot(jnp.concatenate([here, beside], axis=1), self.table[...])
        next_x = out[:, LANES:]
        return (
            out[:, :LANES]
            + jnp.where(row == self.rows - 1, 0.0, pltpu.roll(next_x, n - 1, 0))
            + jnp.where(row == 0, 0.0, pltpu.roll(next_x, 1, 0))
        )

    def operate(self, lo, hi, u, du):
        both = self.get(self.diff, lo, hi) * self.spread(u, lo, hi) + self.spread(du, lo, hi)
        return self.get(self.diag, lo, hi) * self.get(u, lo, hi) - (1.0 / 48.0) * both

    def set_diagonal(self, lo, hi, reaction):
        d = self.get(self.diff, lo, hi)
        diag = self.get(reaction, lo, hi) + (
            (0.5 * WEIGHT_SUM) * d + (1.0 / 48.0) * self.spread(self.diff, lo, hi)
        )
        self.put(self.diag, lo, hi, diag)
        self.put(self.inv, lo, hi, jnp.where(d > 0.0, 1.0 / diag, 0.0))

    def residual(self, lo, hi, out, u, du):
        self.put(out, lo, hi, self.get(self.side, lo, hi) - self.operate(lo, hi, u, du))

    def scale_x(self, lo, hi, out):
        self.put(out, lo, hi, self.get(self.diff, lo, hi) * self.get(self.x, lo, hi))

    def smooth(self, ranges, degree, lower, fresh, keep):
        middle = 0.5 * (UPPER_BOUND + lower)
        radius = 0.5 * (UPPER_BOUND - lower)
        ratio = middle / radius
        rho = 1.0 / ratio

        lo, hi = ranges[0]
        if fresh:
            r = self.get(self.side, lo, hi)
            self.put(self.r, lo, hi, r)
        else:
            r = self.get(self.r, lo, hi)
        q = self.get(self.inv, lo, hi) * r * (1.0 / middle)
        self.put(self.q[0], lo, hi, q)
        self.put(self.dq[0], lo, hi, self.get(self.diff, lo, hi) * q)
        self.put(self.x, lo, hi, q if fresh else self.get(self.x, lo, hi) + q)
        now = 0
        for turn in range(1, degree):
            rho_next = 1.0 / (2.0 * ratio - rho)
            a, b = rho_next * rho, 2.0 * rho_next / radius
            rho = rho_next
            u, du, v, dv = self.q[now], self.dq[now], self.q[1 - now], self.dq[1 - now]
            lo, hi = ranges[turn]
            r = self.get(self.r, lo, hi) - self.operate(lo, hi, u, du)
            q = a * self.get(u, lo, hi) + b * (self.get(self.inv, lo, hi) * r)
            x = self.get(self.x, lo, hi) + q
            self.put(self.x, lo, hi, x)
            if turn + 1 < degree:
                self.put(self.r, lo, hi, r)
                self.put(v, lo, hi, q)
                self.put(dv, lo, hi, self.get(self.diff, lo, hi) * q)
            elif keep:
                self.put(dv, lo, hi, self.get(self.diff, lo, hi) * x)
            now = 1 - now
        return self.dq[now]

    def row_pairs(self, ref, lo, hi):
        half = self.rows // 2
        return ref[lo:hi, pl.ds(0, half, 2), :] + ref[lo:hi, pl.ds(1, half, 2), :]

    def restricted(self, ref, lo, count, table):
        half = self.rows // 2
        pairs = self.row_pairs(ref, lo, lo + 4 * count).reshape(count, 4, half, LANES)
        wide = jnp.concatenate(
            [pairs[:, j].reshape(count * half, LANES) for j in range(4)], axis=1
        )
        return table_dot(wide, table[...]).reshape(count, half, LANES)

    def add_rows(self, k, fine):
        half = self.rows // 2
        for place in range(2):
            at = pl.ds(place, half, 2)
            self.x[k, at, :] = self.x[k, at, :] + fine


W0 = 22
W1 = 7
W2 = 14
W3 = 5
DMA = pltpu.SemaphoreType.DMA
STENCILS = pltpu.VMEM((4, 256, 256), BF16)
COARSE = pltpu.VMEM((3, 512, LANES), BF16)
BACK = pltpu.VMEM((3, LANES, 512), BF16)
SPACES = {"s": pltpu.SMEM, "v": pltpu.VMEM, "h": pltpu.HBM}


def call(kernel, outs, scratch, spaces, *args):
    made = []
    for space, shape in outs:
        if space == "v":
            made.append(pltpu.VMEM(shape, F32))
        else:
            made.append(jax.ShapeDtypeStruct(shape, F32))
    given = [
        pltpu.with_memory_space_constraint(a, pltpu.VMEM) if space == "v" else a
        for space, a in zip(spaces, args)
    ]
    return pl.pallas_call(
        kernel,
        out_shape=made,
        in_specs=[pl.BlockSpec(memory_space=SPACES[space]) for space in spaces],
        out_specs=[
            pl.BlockSpec(memory_space=pltpu.HBM if space == "h" else pltpu.VMEM) for space, _ in outs
        ],
        scratch_shapes=[pltpu.VMEM(s, F32) if isinstance(s, tuple) else s for s in scratch],
        compiler_params=pltpu.CompilerParams(vmem_limit_bytes=VMEM_LIMIT),
    )(*given)


def bring(sems, *pairs):
    copies = [pltpu.make_async_copy(a, b, sems.at[i]) for i, (a, b) in enumerate(pairs)]
    for copy in copies:
        copy.start()
    return copies


def wait(copies):
    for copy in copies:
        copy.wait()


def turn_eighths(x):
    row = lax.broadcasted_iota(jnp.int32, x.shape, 1)
    lane = lax.broadcasted_iota(jnp.int32, x.shape, 2) // 16
    total = jnp.where(lane == row, x, 0.0)
    for step in range(1, 8):
        moved = pltpu.roll(pltpu.roll(x, 16 * step, 2), 8 - step, 1)
        total = jnp.where((lane - row) % 8 == step, moved, total)
    return total


def holder(place, slab):
    odd = place[2]
    return jnp.where(odd == 1, HOLDERS[1][slab], HOLDERS[0][slab])


def pack_kernel(place, basis, diffusion, reaction, parts, fields, sems):
    copies = bring(
        sems, (basis.at[7], fields.at[0]), (diffusion, fields.at[1]), (reaction, fields.at[2])
    )
    for f in range(3):
        copies[f].wait()
        turned = fields[f].reshape(256, LANES).T
        for half in range(2):
            pieces = turn_eighths(
                turned[:, half * LANES : (half + 1) * LANES].reshape(16, 8, LANES)
            )
            for slab in range(16):
                parts[holder(place, slab), f, 8 * half : 8 * half + 8] = pieces[slab]


def to_blocks(place, received):
    wide = []
    for half in range(2):
        pieces = [
            received[holder(place, slab), 8 * half : 8 * half + 8][None] for slab in range(16)
        ]
        wide.append(turn_eighths(jnp.concatenate(pieces, axis=0)).reshape(LANES, LANES))
    return jnp.concatenate(wide, axis=1).T.reshape(16, 16, LANES)


def unpack_kernel(received, table, own):
    fields = own.shape[0]
    for f in range(fields):
        rows = []
        for gx in range(4):
            rows.append(jnp.concatenate([received[gx * 4 + gy, f] for gy in range(4)], axis=1))
        wide = table_dot(jnp.concatenate(rows, axis=0), table[...], 3)
        for k in range(4):
            own[f, k] = wide[:, k * LANES : (k + 1) * LANES]


def assemble(place, pieces, field, window):
    slab, core = place[0], place[1]
    sign = 1 - 2 * core
    clear(window.at[0], window.at[W0 - 1])
    for side, distance, ref, base in pieces:
        slot = 2 + side * sign * distance
        inside = jnp.logical_and(slab + slot - 2 >= 0, slab + slot - 2 < SLABS)
        window[pl.ds(1 + 4 * slot, 4)] = jnp.where(inside, ref[base + field], 0.0)


def clear(*refs):
    for ref in refs:
        ref[...] = jnp.zeros_like(ref)


def clear_ends(count, *refs):
    for ref in refs:
        size = ref.shape[0]
        clear(ref.at[0:count], ref.at[size - count : size])


def down_level0(level, level1, table):
    clear_ends(2, *level.q, *level.dq)
    dx = level.smooth([(1, 21), (2, 20), (2, 20), (3, 19)], DEGREE, SMOOTH_LOW, True, True)
    level.residual(4, 18, level.r, level.x, dx)
    clear_ends(1, level1.side)
    level1.side[1:6] = level.restricted(level.r, 1, 5, table)


def down_level1(level, table):
    clear(*level.q, *level.dq)
    dx = level.smooth([(1, 6), (2, 5), (2, 5), (2, 5)], DEGREE, SMOOTH_LOW, True, True)
    level.residual(3, 4, level.r, level.x, dx)
    return own_quarter(level, level.r, table)


def own_quarter(level, ref, table):
    return table_dot(level.row_pairs(ref, 3, 4)[0], table[0:LANES])


def turn_quarters(x):
    group = lax.broadcasted_iota(jnp.int32, (16, LANES), 0) // 4
    lane = lax.broadcasted_iota(jnp.int32, (16, LANES), 1) // 32
    total = jnp.where(lane == group, x, 0.0)
    for step in range(1, 4):
        moved = pltpu.roll(pltpu.roll(x, 32 * step, 1), 16 - 4 * step, 0)
        total = jnp.where((lane - group) % 4 == step, moved, total)
    return total


def to_all(packet, field, quarter):
    rows = turn_quarters(quarter)[0:4]
    packet[:, field] = jnp.broadcast_to(rows[None], (SLABS, 4, LANES))


def keep_early(sems, level, level1, centre, kept1):
    pairs = [
        (ref.at[7:15], centre.at[1 + i])
        for i, ref in enumerate((level.side, level.diff, level.diag, level.inv))
    ]
    pairs += [
        (ref, kept1.at[2 + i]) for i, ref in enumerate((level1.diff, level1.diag, level1.inv))
    ]
    return bring(sems, *pairs)


def keep_late(sems, level1, kept1, lent):
    pairs = [
        (level1.x, kept1.at[0]),
        (level1.side, kept1.at[1]),
        (level1.x.at[2:5], lent),
    ]
    return bring(sems, *pairs)


def make_levels(tables, full, side, work0, full1, work1):
    x, r, qa, qb, da, db = work0
    side1, x1, r1, q1a, q1b, d1a, d1b = work1
    level = Level(0, tables[0], full.at[1], full.at[2], full.at[3], side, x, r, [qa, qb], [da, db])
    level1 = Level(
        1, tables[1], full1.at[0], full1.at[1], full1.at[2], side1, x1, r1, [q1a, q1b], [d1a, d1b]
    )
    return level, level1


def down_first_kernel(
    place, own, near, near2, mate, far, stencils_in, coarse_in,
    full_out, full1, centre, kept1, lent, packet,
    full, stencils, coarse, sems, react, react1, *work
):
    work0, work1 = work[0:6], work[6:13]
    tables, coarse0, coarse1 = [stencils.at[0], stencils.at[1]], coarse.at[0], coarse.at[1]
    arriving = bring(
        sems, (stencils_in.at[0:2], stencils.at[0:2]), (coarse_in.at[0:2], coarse.at[0:2])
    )
    for i in (2, 3):
        clear_ends(1, full.at[i])
    clear(full1, work1[1], work1[2])
    pieces = [
        (-1, 0, own, 0), (-1, 1, near, 0), (-1, 2, near2, 0), (1, 1, mate, 0), (1, 2, far, 0)
    ]
    assemble(place, pieces, 0, full.at[0])
    assemble(place, pieces, 1, full.at[1])
    assemble(place, pieces, 2, react)
    level, level1 = make_levels(tables, full, full.at[0], work0, full1, work1)
    wait(arriving)
    level.set_diagonal(1, 21, react)
    leaving = bring(sems, (full, full_out))
    level1.diff[1:6] = 0.25 * level.restricted(level.diff, 1, 5, coarse0)
    react1[1:6] = level.restricted(react, 1, 5, coarse0)
    level1.set_diagonal(1, 6, react1)
    leaving += keep_early(sems.at[1:8], level, level1, centre, kept1)
    down_level0(level, level1, coarse0)
    leaving += bring(sems.at[11:12], (level.x.at[7:15], centre.at[0]))
    to_all(packet, 0, down_level1(level1, coarse1))
    to_all(packet, 1, 0.25 * own_quarter(level1, level1.diff, coarse1))
    to_all(packet, 2, own_quarter(level1, react1, coarse1))
    wait(leaving + keep_late(sems.at[8:11], level1, kept1, lent))


def down_second_kernel(
    place, own, near, near2, mate, far, full_in, full1_in, stencils_in, coarse_in,
    centre, kept1, lent, before, packet,
    full, full1, stencils, coarse, sems, window, dwin, side, *work
):
    work0, work1 = work[0:6], work[6:13]
    tables, coarse0, coarse1 = [stencils.at[0], stencils.at[1]], coarse.at[0], coarse.at[1]
    arriving = bring(
        sems,
        (full_in.at[1], full.at[1]),
        (stencils_in.at[0:2], stencils.at[0:2]),
        (full_in.at[2], full.at[2]),
        (full_in.at[0], full.at[0]),
        (full_in.at[3], full.at[3]),
        (coarse_in.at[0:2], coarse.at[0:2]),
        (full1_in, full1),
    )
    before[...] = own[0]
    clear(work1[1], work1[2])
    clear_ends(1, side)
    pieces = [
        (-1, 0, own, 0), (-1, 1, near, 0), (-1, 2, near2, 0), (1, 1, mate, 0), (1, 2, far, 0)
    ]
    assemble(place, pieces, 0, window)
    wait(arriving[0:1])
    dwin[...] = window[...] * full[1]
    wait(arriving[1:4])
    source, _ = make_levels(tables, full, full.at[0], work0, full1, work1)
    source.residual(1, 21, side, window, dwin)
    wait(arriving[4:])
    level, level1 = make_levels(tables, full, side, work0, full1, work1)
    down_level0(level, level1, coarse0)
    leaving = keep_early(sems.at[0:7], level, level1, centre, kept1)
    leaving += bring(sems.at[10:11], (level.x.at[7:15], centre.at[0]))
    to_all(packet, 0, down_level1(level1, coarse1))
    wait(leaving + keep_late(sems.at[7:10], level1, kept1, lent))


def gather_level2(place, order, packets, field, target):
    clear_ends(1, target)
    start = place[0] - place[0] % 16 - 16
    for pack in range(12):
        slab = start + 4 * pack
        inside = jnp.logical_and(slab >= 0, slab < SLABS)
        pieces = [packets[order[jnp.clip(slab + j, 0, SLABS - 1)], field] for j in range(4)]
        value = turn_quarters(jnp.concatenate(pieces, axis=0))
        target[1 + pack] = jnp.where(inside, value, 0.0)


def coarse_part(first, arriving, place, order, packets, tables, lv2, lv3, f2, f3, react2, react3, work2, work3, coarse2, back2):
    x2, r2, q2a, q2b, d2a, d2b = work2
    x3, r3, q3a, q3b, d3a, d3b = work3
    clear(*work2[2:])
    clear(*work3[2:])
    clear_ends(1, x2)
    level2 = Level(2, tables[2], lv2.at[0], lv2.at[1], lv2.at[2], f2, x2, r2, [q2a, q2b], [d2a, d2b])
    level3 = Level(3, tables[3], lv3.at[0], lv3.at[1], lv3.at[2], f3, x3, r3, [q3a, q3b], [d3a, d3b])
    gather_level2(place, order, packets, 0, f2)
    clear_ends(1, f3)
    if not first:
        wait(arriving)
    if first:
        clear_ends(1, lv2.at[1], lv2.at[2], lv3.at[0], lv3.at[1], lv3.at[2], react3)
        gather_level2(place, order, packets, 1, lv2.at[0])
        gather_level2(place, order, packets, 2, react2)
        wait(arriving)
        level2.set_diagonal(1, 13, react2)
        level3.diff[1:4] = 0.25 * level2.restricted(level2.diff, 1, 3, coarse2)
        react3[1:4] = level2.restricted(react2, 1, 3, coarse2)
        level3.set_diagonal(1, 4, react3)
    whole2 = [(1, 13)] * 4
    dx = level2.smooth(whole2, DEGREE, SMOOTH_LOW, True, True)
    level2.residual(1, 13, r2, x2, dx)
    f3[1:4] = level2.restricted(r2, 1, 3, coarse2)
    level3.smooth([(1, 4)] * 8, COARSE_DEGREE, COARSE_LOW, True, False)
    fine = table_dot(level3.get(x3, 1, 4), back2[...])
    for t in range(3):
        for j in range(4):
            level2.add_rows(1 + 4 * t + j, fine[t * 8 : t * 8 + 8, j * LANES : (j + 1) * LANES])
    level2.scale_x(1, 13, dx)
    level2.residual(1, 13, r2, x2, dx)
    level2.smooth(whole2, DEGREE, SMOOTH_LOW, False, False)
    return x2


def up_part(place, x2, spaced, tables, centre, kept1, swapped, mate, work0, work1, back0, back1):
    x, r, qa, qb, da, db = work0
    x1, r1, q1a, q1b, d1a, d1b = work1
    clear(*work0[2:])
    clear(*work1[2:])
    slab, core = place[0], place[1]
    for pack in range(3, 9):
        value = x2[1 + pack]
        for j in range(4):
            spaced[4 * pack + j - 12] = pltpu.roll(value, LANES - 32 * j, 1) if j else value
    level1 = Level(
        1, tables[1], kept1.at[2], kept1.at[3], kept1.at[4], kept1.at[1], x1, r1,
        [q1a, q1b], [d1a, d1b],
    )
    level = Level(
        0, tables[0], centre.at[2], centre.at[3], centre.at[4], centre.at[1], x, r,
        [qa, qb], [da, db],
    )
    x1[...] = kept1[0]
    x[...] = centre[0]
    half = lax.broadcasted_iota(jnp.int32, (32, LANES), 1) < 64
    below, above = slab > 0, slab < SLABS - 1
    first_core = core == 0

    def beside(pack, is_below):
        mine, others = (swapped, mate) if is_below else (mate, swapped)
        value = jnp.where(first_core, mine[pack], others[pack])
        return jnp.where(below if is_below else above, value, 0.0)

    x1[1] = beside(0, True)
    x1[2] = jnp.where(half, beside(1, True), x1[2])
    x1[4] = jnp.where(half, x1[4], beside(1, False))
    x1[5] = beside(2, False)
    start = slab % 16 + 2
    fine = table_dot(spaced[pl.ds(start, 5)].reshape(5 * 16, LANES), back1[:, 0:LANES])
    for t in range(5):
        level1.add_rows(1 + t, fine[t * 16 : t * 16 + 16])
    level1.scale_x(1, 6, d1b)
    level1.residual(1, 6, r1, x1, d1b)
    level1.smooth([(1, 6), (2, 5), (2, 5), (2, 5)], DEGREE, SMOOTH_LOW, False, False)
    fine = table_dot(level1.get(x1, 2, 5), back0[...])
    for k in range(8):
        t, j = divmod(2 + k, 4)
        level.add_rows(1 + k, fine[t * 32 : t * 32 + 32, j * LANES : (j + 1) * LANES])
    level.scale_x(1, 9, db)
    level.residual(1, 9, r, x, db)
    level.smooth([(1, 9), (2, 8), (2, 8), (3, 7)], DEGREE, SMOOTH_LOW, False, False)
    return x


def up_kernel(first, place, order, packets, centre_in, kept1_in, swapped_in, mate_in, *refs):
    if first:
        (stencils_in, coarse_in, back_in, applied, lv2, lv3), refs = refs[0:6], refs[6:]
        early, later = [], []
    else:
        (lv2_in, lv3_in, before_in, stencils_in, coarse_in, back_in), refs = refs[0:6], refs[6:]
        (to_block_in, out, lv2, lv3, before, to_block), refs = refs[0:6], refs[6:]
        early = [(lv2_in, lv2), (lv3_in, lv3)]
        later = [(before_in, before), (to_block_in, to_block)]
    (stencils, coarse, back, sems, centre, kept1, swapped, mate), refs = refs[0:8], refs[8:]
    early += [(stencils_in, stencils), (coarse_in.at[2], coarse.at[2]), (back_in, back)]
    later += [
        (kept1_in, kept1), (centre_in, centre.at[:, 1:9]), (swapped_in, swapped), (mate_in, mate)
    ]
    arriving = bring(sems.at[0:6], *early)
    arriving_later = bring(sems.at[6:12], *later)
    clear(centre.at[:, 0], centre.at[:, 9])
    tables = [stencils.at[i] for i in range(4)]
    coarse2, back0, back1, back2 = coarse.at[2], back.at[0], back.at[1], back.at[2]
    f2, f3, react2, react3 = refs[0:4]
    work2, work3, work0, work1, spaced = refs[4:10], refs[10:16], refs[16:22], refs[22:28], refs[28]
    x2 = coarse_part(
        first, arriving, place, order, packets, tables, lv2, lv3, f2, f3, react2, react3, work2, work3, coarse2, back2
    )
    wait(arriving_later)
    x = up_part(
        place, x2, spaced, tables, centre, kept1, swapped, mate, work0, work1, back0, back1
    )
    if first:
        applied[0] = x[3:7]
    else:
        wide = jnp.concatenate([before[k] + x[3 + k] for k in range(4)], axis=1)
        pieces = table_dot(wide, to_block[...], 3)
        for gx in range(4):
            for gy in range(4):
                out[gx * 4 + gy] = pieces[gx * 16 : (gx + 1) * 16, gy * LANES : (gy + 1) * LANES]


def up_first_kernel(*refs):
    up_kernel(True, *refs)


def up_second_kernel(*refs):
    up_kernel(False, *refs)


def row_of_sums(rows):
    stacked = jnp.concatenate(
        [jnp.sum(jnp.sum(a, axis=0), axis=0, keepdims=True) for _, a in rows], axis=0
    )
    totals = jnp.sum(stacked, axis=1, keepdims=True)
    lane = lax.broadcasted_iota(jnp.int32, (1, LANES), 1)
    out = jnp.zeros((1, LANES), F32)
    for i, (lanes, _) in enumerate(rows):
        for at in lanes:
            out = jnp.where(lane == at, totals[i : i + 1], out)
    return out


def gram_kernel(basis, out):
    out[...] = row_of_sums(
        [([8 * j + k, 8 * k + j], basis[j] * basis[k]) for j in range(8) for k in range(j, 8)]
    )


def sums_one_kernel(place, received, basis, gram, applied, out):
    applied[...] = to_blocks(place, received)
    rows = [([64 + k], basis[k] * applied[...]) for k in range(8)]
    rows += [([72], applied[...] * applied[...])]
    out[...] = jnp.broadcast_to((row_of_sums(rows) + gram[...])[None], (SLABS, 1, LANES))


def read_sums(gathered):
    totals = jnp.sum(gathered[...], axis=0)
    row = lax.broadcasted_iota(jnp.int32, (8, LANES), 0)
    lane = lax.broadcasted_iota(jnp.int32, (8, LANES), 1)
    gram = jnp.zeros((8, LANES), F32)
    wide = jnp.broadcast_to(totals, (8, LANES))
    for j in range(8):
        gram = jnp.where(row == j, pltpu.roll(wide, (LANES - 8 * j) % LANES, 1), gram)
    gram = jnp.where(lane < 8, gram, 0.0)
    proj = jnp.where(lane < 8, pltpu.roll(wide, LANES - 64, 1), 0.0)[0:1]
    return gram, proj, totals[:, 72:73]


def column(row_vector):
    row = lax.broadcasted_iota(jnp.int32, (8, LANES), 0)
    lane = lax.broadcasted_iota(jnp.int32, (8, LANES), 1)
    return jnp.sum(jnp.where(row == lane, row_vector, 0.0), axis=1, keepdims=True)


def as_row(column_vector):
    row = lax.broadcasted_iota(jnp.int32, (8, LANES), 0)
    lane = lax.broadcasted_iota(jnp.int32, (8, LANES), 1)
    return jnp.sum(jnp.where(row == lane, column_vector, 0.0), axis=0, keepdims=True)


def times(gram, row_vector):
    return jnp.sum(gram * row_vector, axis=1, keepdims=True)


def dot8(a, b):
    return jnp.sum(a * b, axis=0, keepdims=True)


def finish(gram, proj_two, squares, coeff_one, base, basis, weights_of, out, coefficients):
    coeff_two = proj_two * (1.0 / CELLS)
    quadratic = dot8(coeff_two, times(gram, as_row(coeff_two)))
    mean_square = (squares - 2.0 * dot8(coeff_two, proj_two) + quadratic) * (1.0 / CELLS)
    length = jnp.sqrt(mean_square + 1e-06)
    value = base[...]
    subtract = weights_of(coeff_two)
    for k in range(8):
        value = value - subtract[k : k + 1].reshape(1, 1, 1) * basis[k]
    out[...] = value * (1.0 / length).reshape(1, 1, 1)
    lane = lax.broadcasted_iota(jnp.int32, (1, LANES), 1)
    row = as_row(coeff_one + coeff_two)
    coefficients[...] = jnp.where(lane == 8, length, row)[:, 0:9]


def finish_one_kernel(gathered, basis, applied, out, coefficients, near):
    gram, proj, square = read_sums(gathered)
    one_row = proj * (1.0 / CELLS)
    one, proj = column(one_row), column(proj)
    image = times(gram, one_row)
    proj_two = proj - image
    squares = square - 2.0 * dot8(one, proj) + dot8(one, image)
    near[...] = jnp.where(squares > 0.02 * square, 0.0, 1.0)
    finish(
        gram, proj_two, squares, one, applied, basis, lambda two: one + two, out, coefficients
    )


def sums_two_kernel(gathered, basis, applied, first, out):
    _, proj, _ = read_sums(gathered)
    one = column(proj * (1.0 / CELLS))
    value = applied[...]
    for k in range(8):
        value = value - one[k : k + 1].reshape(1, 1, 1) * basis[k]
    first[...] = value
    sums = row_of_sums([([64 + k], basis[k] * value) for k in range(8)] + [([72], value * value)])
    out[...] = jnp.broadcast_to(sums[None], (SLABS, 1, LANES))


def finish_two_kernel(gathered, gathered_two, basis, first, out, coefficients):
    gram, proj, _ = read_sums(gathered)
    _, proj_two, squares = read_sums(gathered_two)
    one = column(proj * (1.0 / CELLS))
    finish(
        gram, column(proj_two), squares, one, first, basis, lambda two: two, out, coefficients
    )


def swap_all(x):
    return lax.all_to_all(x, AXES, 0, 0, tiled=True)


def halo(own):
    near = lax.ppermute(own, AXES, CHIP_SWAP)
    mate = lax.ppermute(own, AXES, CORE_SWAP)
    near2 = lax.ppermute(mate, AXES, CHIP_SWAP)
    far = lax.ppermute(near, AXES, CORE_SWAP)
    return near, near2, mate, far


def beside(lent):
    return lax.ppermute(lent, AXES, CHIP_SWAP), lax.ppermute(lent, AXES, CORE_SWAP)


def local(basis, diffusion, reaction):
    gx, gy, gz = (lax.axis_index(a) for a in AXES)
    odd = gz % 2
    core = gx % 2
    slab = 16 * gz + 2 * slab_in_group(gx // 2, gy, odd) + core
    place = jnp.stack([slab, core, odd]).astype(jnp.int32)
    order = jnp.asarray(ORDER, jnp.int32)
    stencils = jnp.asarray(np.stack(STENCIL), BF16)
    coarse = jnp.asarray(np.stack(RESTRICT), BF16)
    back = jnp.asarray(np.stack([t.T for t in RESTRICT]), BF16)
    to_slab = jnp.asarray(TO_SLAB, BF16)
    to_block = jnp.asarray(TO_SLAB.T, BF16)
    block = (16, 16, LANES)
    (parts,) = call(
        pack_kernel,
        [("v", (16, 3, 16, LANES))],
        [(3,) + block, DMA((3,))],
        "shhh", place, basis, diffusion, reaction,
    )
    received = lax.all_to_all(parts, ("gx", "gy"), 0, 0, tiled=True)
    (own,) = call(unpack_kernel, [("v", (3, 4, 64, LANES))], [], "vv", received, to_slab)

    big = (W0, 64, LANES)
    small = (W1, 32, LANES)
    two = (W2, 16, LANES)
    three = (W3, 8, LANES)
    mid = (10, 64, LANES)
    lending = ("h", (3, 32, LANES))
    kept = [("h", (5, 8, 64, LANES)), ("h", (5,) + small), lending]
    slab_shape = (4, 64, LANES)
    full, full1, centre, kept1, lent, packet = call(
        down_first_kernel,
        [("h", (4,) + big), ("o", (3,) + small), *kept, ("o", (SLABS, 3, 4, LANES))],
        [(4,) + big, STENCILS, COARSE, DMA((12,)), big, small] + [big] * 6 + [small] * 7,
        "svvvvvhh", place, own, *halo(own), stencils, coarse,
    )
    tables = [STENCILS, COARSE, BACK, DMA((12,))]
    tables += [pltpu.VMEM(s, F32) for s in ((5,) + mid, (5,) + small, (3, 32, LANES), (3, 32, LANES))]
    up_scratch = (
        [two, three, two, three]
        + [two] * 6
        + [three] * 6
        + [mid] * 6
        + [small] * 6
        + [(24, 16, LANES)]
    )
    applied, lv2, lv3 = call(
        up_first_kernel,
        [("v", (1,) + slab_shape), ("o", (3,) + two), ("o", (3,) + three)],
        tables + up_scratch,
        "ssvhhhhhhh",
        place, order, swap_all(packet), centre, kept1, *beside(lent), stencils, coarse, back,
    )
    centre, kept1, lent, before, packet = call(
        down_second_kernel,
        [*kept, ("o", slab_shape), ("o", (SLABS, 1, 4, LANES))],
        [(4,) + big, (3,) + small, STENCILS, COARSE, DMA((11,))] + [big] * 9 + [small] * 7,
        "svvvvvhhhh", place, applied, *halo(applied), full, full1, stencils, coarse,
    )
    (out,) = call(
        up_second_kernel,
        [("v", (16, 16, LANES))],
        [(3,) + two, (3,) + three, slab_shape, pltpu.VMEM((512, 512), BF16)] + tables + up_scratch,
        "ssvhhhhhhhhhhh",
        place, order, swap_all(packet), centre, kept1, *beside(lent), lv2, lv3, before,
        stencils, coarse, back, to_block,
    )
    back = lax.all_to_all(out, ("gx", "gy"), 0, 0, tiled=True)
    row = (1, 9)
    (gram,) = call(gram_kernel, [("v", (1, LANES))], [], "v", basis)
    applied, part = call(
        sums_one_kernel,
        [("v", block), ("v", (SLABS, 1, LANES))],
        [],
        "svvv", place, back, basis, gram,
    )
    gathered = swap_all(part)
    next_vector, coefficients, near = call(
        finish_one_kernel, [("o", block), ("o", row), ("o", (1, 1))], [], "vvv", gathered, basis, applied
    )

    def second_sum():
        first, part = call(
            sums_two_kernel, [("o", block), ("o", (SLABS, 1, LANES))], [], "vvv", gathered, basis, applied
        )
        return tuple(
            call(
                finish_two_kernel, [("o", block), ("o", row)], [], "vvvv",
                gathered, swap_all(part), basis, first,
            )
        )

    next_vector, coefficients = lax.cond(
        near[0, 0] > 0.5, second_sum, lambda: (next_vector, coefficients)
    )
    return next_vector, coefficients.reshape(9)


def solution(mesh):
    placed = (P(None, "gx", "gy", "gz"), P("gx", "gy", "gz"), P("gx", "gy", "gz"))
    return jax.shard_map(
        local, mesh=mesh, in_specs=placed, out_specs=(P("gx", "gy", "gz"), P()), check_vma=False
    )
```

```python
import numpy as np
import jax
import jax.numpy as jnp
from jax import lax
from jax.experimental import pallas as pl
from jax.experimental.pallas import tpu as pltpu
from jax.sharding import PartitionSpec as P

AXES = ("gx", "gy", "gz")
DEGREE = 4
COARSE_DEGREE = 8
UPPER_BOUND = 2.0
SMOOTH_LOW = 0.25
COARSE_LOW = 0.05
PULL = (1.0, 0.5, 2.0)
WX, WY, WZ = PULL
WXY = (WX + WY) / 8.0
WXZ = (WX + WZ) / 8.0
WYZ = (WY + WZ) / 8.0
WXYZ = (WX + WY + WZ) / 24.0
WEIGHT_SUM = 2.0 * (WX + WY + WZ) + 4.0 * (WXY + WXZ + WYZ) + 8.0 * WXYZ
LANES = 128
SLABS = 128
CELLS = 64.0 * 64.0 * 1024.0
F32 = jnp.float32
BF16 = jnp.bfloat16
VMEM_LIMIT = 56 * 1024 * 1024

WIDTHS = (64, 32, 16, 8)


def slab_in_group(x_lo, z, odd):
    turned = z + odd * (3 - 2 * z)
    return 2 * turned + (x_lo + z + 1) % 2


def device_order():
    order = [0] * SLABS
    for gx in range(4):
        for gy in range(4):
            for gz in range(8):
                slab = 16 * gz + 2 * slab_in_group(gx // 2, gy, gz % 2) + gx % 2
                order[slab] = (gx * 4 + gy) * 8 + gz
    return order


ORDER = device_order()
HOLDERS = [[0] * 16, [0] * 16]
for _a in range(4):
    for _b in range(4):
        for _odd in (0, 1):
            HOLDERS[_odd][2 * slab_in_group(_a // 2, _b, _odd) + _a % 2] = 4 * _a + _b
CORE_SWAP = [(ORDER[s], ORDER[s ^ 1]) for s in range(SLABS)]
CHIP_SWAP = [(ORDER[s], ORDER[(s + 1 if s % 2 else s - 1) % SLABS]) for s in range(SLABS)]


def fine_to_coarse(level):
    width = WIDTHS[level]
    planes = LANES // width
    table = np.zeros((4, LANES, LANES), np.float32)
    for pack in range(4):
        for lane in range(LANES):
            z, y = divmod(lane, width)
            table[pack, lane, ((pack * planes + z) // 2) * (width // 2) + y // 2] = 1.0
    return table.reshape(4 * LANES, LANES)


def block_to_slab():
    table = np.zeros((512, 512), np.float32)
    for gy in range(4):
        for z in range(8):
            for y in range(16):
                table[gy * 128 + z * 16 + y, (z // 2) * 128 + (z % 2) * 64 + gy * 16 + y] = 1.0
    return table


def stencil_table(level):
    width = WIDTHS[level]
    planes = LANES // width
    weights = {
        (0, 1, 0): WY, (0, 0, 1): WZ, (0, 1, 1): WYZ,
        (1, 0, 0): WX, (1, 1, 0): WXY, (1, 0, 1): WXZ, (1, 1, 1): WXYZ,
    }
    table = np.zeros((2 * LANES, 2 * LANES), np.float32)
    for lane in range(LANES):
        z, y = divmod(lane, width)
        for dz in (-1, 0, 1):
            for dy in (-1, 0, 1):
                if not 0 <= y + dy < width:
                    continue
                outside = not 0 <= z + dz < planes
                source = outside * LANES + (z + dz) % planes * width + y + dy
                for dx in (0, 1):
                    if (dx, abs(dy), abs(dz)) in weights:
                        weight = round(48.0 * weights[dx, abs(dy), abs(dz)]) / 2.0
                        table[source, dx * LANES + lane] += weight
    return table


RESTRICT = [fine_to_coarse(level) for level in range(3)]
TO_SLAB = block_to_slab()
STENCIL = [stencil_table(level) for level in range(4)]


def stacked_dot(a, table):
    high = a.astype(BF16)
    low = (a - high.astype(F32)).astype(BF16)
    out = jnp.dot(jnp.concatenate([high, low], axis=0), table, preferred_element_type=F32)
    n = a.shape[0]
    return out[:n] + out[n:]


def table_dot(a, table, parts=2):
    total = None
    rest = a
    for part_number in range(parts):
        part = rest.astype(BF16)
        if part_number + 1 < parts:
            rest = rest - part.astype(F32)
        term = jnp.dot(part, table, preferred_element_type=F32)
        total = term if total is None else total + term
    return total


class Level:
    def __init__(self, index, table, diff, diag, inv, side, x, r, q, dq):
        self.width = self.rows = WIDTHS[index]
        self.table = table
        self.diff, self.diag, self.inv, self.side = diff, diag, inv, side
        self.x, self.r, self.q, self.dq = x, r, q, dq

    def get(self, ref, lo, hi):
        return ref[lo:hi].reshape((hi - lo) * self.rows, LANES)

    def put(self, ref, lo, hi, value):
        ref[lo:hi] = value.reshape(hi - lo, self.rows, LANES)

    def spread(self, ref, lo, hi):
        n = (hi - lo) * self.rows
        lane = lax.broadcasted_iota(jnp.int32, (n, LANES), 1)
        row = lax.broadcasted_iota(jnp.int32, (n, LANES), 0) % self.rows
        here = self.get(ref, lo, hi)
        beside = jnp.where(
            lane < self.width, self.get(ref, lo + 1, hi + 1), self.get(ref, lo - 1, hi - 1)
        )
        product = stacked_dot if self.rows == 8 else table_dot
        out = product(jnp.concatenate([here, beside], axis=1), self.table[...])
        next_x = out[:, LANES:]
        return (
            out[:, :LANES]
            + jnp.where(row == self.rows - 1, 0.0, pltpu.roll(next_x, n - 1, 0))
            + jnp.where(row == 0, 0.0, pltpu.roll(next_x, 1, 0))
        )

    def operate(self, lo, hi, u, du):
        both = self.get(self.diff, lo, hi) * self.spread(u, lo, hi) + self.spread(du, lo, hi)
        return self.get(self.diag, lo, hi) * self.get(u, lo, hi) - (1.0 / 48.0) * both

    def set_diagonal(self, lo, hi, reaction):
        d = self.get(self.diff, lo, hi)
        diag = self.get(reaction, lo, hi) + (
            (0.5 * WEIGHT_SUM) * d + (1.0 / 48.0) * self.spread(self.diff, lo, hi)
        )
        self.put(self.diag, lo, hi, diag)
        self.put(self.inv, lo, hi, jnp.where(d > 0.0, 1.0 / diag, 0.0))

    def residual(self, lo, hi, out, u, du):
        self.put(out, lo, hi, self.get(self.side, lo, hi) - self.operate(lo, hi, u, du))

    def scale_x(self, lo, hi, out):
        self.put(out, lo, hi, self.get(self.diff, lo, hi) * self.get(self.x, lo, hi))

    def smooth(self, ranges, degree, lower, fresh, keep):
        middle = 0.5 * (UPPER_BOUND + lower)
        radius = 0.5 * (UPPER_BOUND - lower)
        ratio = middle / radius
        rho = 1.0 / ratio

        lo, hi = ranges[0]
        if fresh:
            r = self.get(self.side, lo, hi)
            self.put(self.r, lo, hi, r)
        else:
            r = self.get(self.r, lo, hi)
        q = self.get(self.inv, lo, hi) * r * (1.0 / middle)
        self.put(self.q[0], lo, hi, q)
        self.put(self.dq[0], lo, hi, self.get(self.diff, lo, hi) * q)
        self.put(self.x, lo, hi, q if fresh else self.get(self.x, lo, hi) + q)
        now = 0
        for turn in range(1, degree):
            rho_next = 1.0 / (2.0 * ratio - rho)
            a, b = rho_next * rho, 2.0 * rho_next / radius
            rho = rho_next
            u, du, v, dv = self.q[now], self.dq[now], self.q[1 - now], self.dq[1 - now]
            lo, hi = ranges[turn]
            r = self.get(self.r, lo, hi) - self.operate(lo, hi, u, du)
            q = a * self.get(u, lo, hi) + b * (self.get(self.inv, lo, hi) * r)
            x = self.get(self.x, lo, hi) + q
            self.put(self.x, lo, hi, x)
            if turn + 1 < degree:
                self.put(self.r, lo, hi, r)
                self.put(v, lo, hi, q)
                self.put(dv, lo, hi, self.get(self.diff, lo, hi) * q)
            elif keep:
                self.put(dv, lo, hi, self.get(self.diff, lo, hi) * x)
            now = 1 - now
        return self.dq[now]

    def row_pairs(self, ref, lo, hi):
        half = self.rows // 2
        return ref[lo:hi, pl.ds(0, half, 2), :] + ref[lo:hi, pl.ds(1, half, 2), :]

    def restricted(self, ref, lo, count, table):
        half = self.rows // 2
        pairs = self.row_pairs(ref, lo, lo + 4 * count).reshape(count, 4, half, LANES)
        wide = jnp.concatenate(
            [pairs[:, j].reshape(count * half, LANES) for j in range(4)], axis=1
        )
        return table_dot(wide, table[...]).reshape(count, half, LANES)

    def add_rows(self, k, fine):
        half = self.rows // 2
        for place in range(2):
            at = pl.ds(place, half, 2)
            self.x[k, at, :] = self.x[k, at, :] + fine


W0 = 22
W1 = 7
W2 = 14
W3 = 5
DMA = pltpu.SemaphoreType.DMA
STENCILS = pltpu.VMEM((4, 256, 256), BF16)
COARSE = pltpu.VMEM((3, 512, LANES), BF16)
BACK = pltpu.VMEM((3, LANES, 512), BF16)
SPACES = {"s": pltpu.SMEM, "v": pltpu.VMEM, "h": pltpu.HBM}


def call(kernel, outs, scratch, spaces, *args):
    made = []
    for space, shape in outs:
        if space == "v":
            made.append(pltpu.VMEM(shape, F32))
        else:
            made.append(jax.ShapeDtypeStruct(shape, F32))
    given = [
        pltpu.with_memory_space_constraint(a, pltpu.VMEM) if space == "v" else a
        for space, a in zip(spaces, args)
    ]
    return pl.pallas_call(
        kernel,
        out_shape=made,
        in_specs=[pl.BlockSpec(memory_space=SPACES[space]) for space in spaces],
        out_specs=[
            pl.BlockSpec(memory_space=pltpu.HBM if space == "h" else pltpu.VMEM) for space, _ in outs
        ],
        scratch_shapes=[pltpu.VMEM(s, F32) if isinstance(s, tuple) else s for s in scratch],
        compiler_params=pltpu.CompilerParams(vmem_limit_bytes=VMEM_LIMIT),
    )(*given)


def bring(sems, *pairs):
    copies = [pltpu.make_async_copy(a, b, sems.at[i]) for i, (a, b) in enumerate(pairs)]
    for copy in copies:
        copy.start()
    return copies


def wait(copies):
    for copy in copies:
        copy.wait()


def turn_eighths(x):
    row = lax.broadcasted_iota(jnp.int32, x.shape, 1)
    lane = lax.broadcasted_iota(jnp.int32, x.shape, 2) // 16
    total = jnp.where(lane == row, x, 0.0)
    for step in range(1, 8):
        moved = pltpu.roll(pltpu.roll(x, 16 * step, 2), 8 - step, 1)
        total = jnp.where((lane - row) % 8 == step, moved, total)
    return total


def holder(place, slab):
    odd = place[2]
    return jnp.where(odd == 1, HOLDERS[1][slab], HOLDERS[0][slab])


def pack_kernel(place, basis, diffusion, reaction, parts, fields, sems):
    copies = bring(
        sems, (basis.at[7], fields.at[0]), (diffusion, fields.at[1]), (reaction, fields.at[2])
    )
    for f in range(3):
        copies[f].wait()
        turned = fields[f].reshape(256, LANES).T
        for half in range(2):
            pieces = turn_eighths(
                turned[:, half * LANES : (half + 1) * LANES].reshape(16, 8, LANES)
            )
            for slab in range(16):
                parts[holder(place, slab), f, 8 * half : 8 * half + 8] = pieces[slab]


def to_blocks(place, received):
    wide = []
    for half in range(2):
        pieces = [
            received[holder(place, slab), 8 * half : 8 * half + 8][None] for slab in range(16)
        ]
        wide.append(turn_eighths(jnp.concatenate(pieces, axis=0)).reshape(LANES, LANES))
    return jnp.concatenate(wide, axis=1).T.reshape(16, 16, LANES)


def unpack_kernel(received, table, own):
    fields = own.shape[0]
    for f in range(fields):
        rows = []
        for gx in range(4):
            rows.append(jnp.concatenate([received[gx * 4 + gy, f] for gy in range(4)], axis=1))
        wide = table_dot(jnp.concatenate(rows, axis=0), table[...], 3)
        for k in range(4):
            own[f, k] = wide[:, k * LANES : (k + 1) * LANES]


def assemble(place, pieces, field, window):
    slab, core = place[0], place[1]
    sign = 1 - 2 * core
    clear(window.at[0], window.at[W0 - 1])
    for side, distance, ref, base in pieces:
        slot = 2 + side * sign * distance
        inside = jnp.logical_and(slab + slot - 2 >= 0, slab + slot - 2 < SLABS)
        window[pl.ds(1 + 4 * slot, 4)] = jnp.where(inside, ref[base + field], 0.0)


def clear(*refs):
    for ref in refs:
        ref[...] = jnp.zeros_like(ref)


def clear_ends(count, *refs):
    for ref in refs:
        size = ref.shape[0]
        clear(ref.at[0:count], ref.at[size - count : size])


def down_level0(level, level1, table):
    clear_ends(2, *level.q, *level.dq)
    dx = level.smooth([(1, 21), (2, 20), (2, 20), (3, 19)], DEGREE, SMOOTH_LOW, True, True)
    level.residual(4, 18, level.r, level.x, dx)
    clear_ends(1, level1.side)
    level1.side[1:6] = level.restricted(level.r, 1, 5, table)


def down_level1(level, table):
    clear(*level.q, *level.dq)
    dx = level.smooth([(1, 6), (2, 5), (2, 5), (2, 5)], DEGREE, SMOOTH_LOW, True, True)
    level.residual(3, 4, level.r, level.x, dx)
    return own_quarter(level, level.r, table)


def own_quarter(level, ref, table):
    return table_dot(level.row_pairs(ref, 3, 4)[0], table[0:LANES])


def turn_quarters(x):
    group = lax.broadcasted_iota(jnp.int32, (16, LANES), 0) // 4
    lane = lax.broadcasted_iota(jnp.int32, (16, LANES), 1) // 32
    total = jnp.where(lane == group, x, 0.0)
    for step in range(1, 4):
        moved = pltpu.roll(pltpu.roll(x, 32 * step, 1), 16 - 4 * step, 0)
        total = jnp.where((lane - group) % 4 == step, moved, total)
    return total


def to_all(packet, field, quarter):
    rows = turn_quarters(quarter)[0:4]
    packet[:, field] = jnp.broadcast_to(rows[None], (SLABS, 4, LANES))


def keep_early(sems, level, level1, centre, kept1):
    pairs = [
        (ref.at[7:15], centre.at[1 + i])
        for i, ref in enumerate((level.side, level.diff, level.diag, level.inv))
    ]
    pairs += [
        (ref, kept1.at[2 + i]) for i, ref in enumerate((level1.diff, level1.diag, level1.inv))
    ]
    return bring(sems, *pairs)


def keep_late(sems, level1, kept1, lent):
    pairs = [
        (level1.x, kept1.at[0]),
        (level1.side, kept1.at[1]),
        (level1.x.at[2:5], lent),
    ]
    return bring(sems, *pairs)


def make_levels(tables, full, side, work0, full1, work1):
    x, r, qa, qb, da, db = work0
    side1, x1, r1, q1a, q1b, d1a, d1b = work1
    level = Level(0, tables[0], full.at[1], full.at[2], full.at[3], side, x, r, [qa, qb], [da, db])
    level1 = Level(
        1, tables[1], full1.at[0], full1.at[1], full1.at[2], side1, x1, r1, [q1a, q1b], [d1a, d1b]
    )
    return level, level1


def down_first_kernel(
    place, own, near, near2, mate, far, stencils_in, coarse_in,
    full_out, full1, centre, kept1, lent, packet,
    full, stencils, coarse, sems, react, react1, *work
):
    work0, work1 = work[0:6], work[6:13]
    tables, coarse0, coarse1 = [stencils.at[0], stencils.at[1]], coarse.at[0], coarse.at[1]
    arriving = bring(
        sems, (stencils_in.at[0:2], stencils.at[0:2]), (coarse_in.at[0:2], coarse.at[0:2])
    )
    for i in (2, 3):
        clear_ends(1, full.at[i])
    clear(full1, work1[1], work1[2])
    pieces = [
        (-1, 0, own, 0), (-1, 1, near, 0), (-1, 2, near2, 0), (1, 1, mate, 0), (1, 2, far, 0)
    ]
    assemble(place, pieces, 0, full.at[0])
    assemble(place, pieces, 1, full.at[1])
    assemble(place, pieces, 2, react)
    level, level1 = make_levels(tables, full, full.at[0], work0, full1, work1)
    wait(arriving)
    level.set_diagonal(1, 21, react)
    leaving = bring(sems, (full, full_out))
    level1.diff[1:6] = 0.25 * level.restricted(level.diff, 1, 5, coarse0)
    react1[1:6] = level.restricted(react, 1, 5, coarse0)
    level1.set_diagonal(1, 6, react1)
    leaving += keep_early(sems.at[1:8], level, level1, centre, kept1)
    down_level0(level, level1, coarse0)
    leaving += bring(sems.at[11:12], (level.x.at[7:15], centre.at[0]))
    to_all(packet, 0, down_level1(level1, coarse1))
    to_all(packet, 1, 0.25 * own_quarter(level1, level1.diff, coarse1))
    to_all(packet, 2, own_quarter(level1, react1, coarse1))
    wait(leaving + keep_late(sems.at[8:11], level1, kept1, lent))


def down_second_kernel(
    place, own, near, near2, mate, far, full_in, full1_in, stencils_in, coarse_in,
    centre, kept1, lent, before, packet,
    full, full1, stencils, coarse, sems, window, dwin, side, *work
):
    work0, work1 = work[0:6], work[6:13]
    tables, coarse0, coarse1 = [stencils.at[0], stencils.at[1]], coarse.at[0], coarse.at[1]
    arriving = bring(
        sems,
        (full_in.at[1], full.at[1]),
        (stencils_in.at[0:2], stencils.at[0:2]),
        (full_in.at[2], full.at[2]),
        (full_in.at[0], full.at[0]),
        (full_in.at[3], full.at[3]),
        (coarse_in.at[0:2], coarse.at[0:2]),
        (full1_in, full1),
    )
    before[...] = own[0]
    clear(work1[1], work1[2])
    clear_ends(1, side)
    pieces = [
        (-1, 0, own, 0), (-1, 1, near, 0), (-1, 2, near2, 0), (1, 1, mate, 0), (1, 2, far, 0)
    ]
    assemble(place, pieces, 0, window)
    wait(arriving[0:1])
    dwin[...] = window[...] * full[1]
    wait(arriving[1:4])
    source, _ = make_levels(tables, full, full.at[0], work0, full1, work1)
    source.residual(1, 21, side, window, dwin)
    wait(arriving[4:])
    level, level1 = make_levels(tables, full, side, work0, full1, work1)
    down_level0(level, level1, coarse0)
    leaving = keep_early(sems.at[0:7], level, level1, centre, kept1)
    leaving += bring(sems.at[10:11], (level.x.at[7:15], centre.at[0]))
    to_all(packet, 0, down_level1(level1, coarse1))
    wait(leaving + keep_late(sems.at[7:10], level1, kept1, lent))


def gather_level2(place, order, packets, field, target):
    clear_ends(1, target)
    start = place[0] - place[0] % 16 - 16
    for pack in range(12):
        slab = start + 4 * pack
        inside = jnp.logical_and(slab >= 0, slab < SLABS)
        pieces = [packets[order[jnp.clip(slab + j, 0, SLABS - 1)], field] for j in range(4)]
        value = turn_quarters(jnp.concatenate(pieces, axis=0))
        target[1 + pack] = jnp.where(inside, value, 0.0)


def coarse_part(first, arriving, place, order, packets, tables, lv2, lv3, f2, f3, react2, react3, work2, work3, coarse2, back2):
    x2, r2, q2a, q2b, d2a, d2b = work2
    x3, r3, q3a, q3b, d3a, d3b = work3
    clear(*work2[2:])
    clear(*work3[2:])
    clear_ends(1, x2)
    level2 = Level(2, tables[2], lv2.at[0], lv2.at[1], lv2.at[2], f2, x2, r2, [q2a, q2b], [d2a, d2b])
    level3 = Level(3, tables[3], lv3.at[0], lv3.at[1], lv3.at[2], f3, x3, r3, [q3a, q3b], [d3a, d3b])
    gather_level2(place, order, packets, 0, f2)
    clear_ends(1, f3)
    if not first:
        wait(arriving)
    if first:
        clear_ends(1, lv2.at[1], lv2.at[2], lv3.at[0], lv3.at[1], lv3.at[2], react3)
        gather_level2(place, order, packets, 1, lv2.at[0])
        gather_level2(place, order, packets, 2, react2)
        wait(arriving)
        level2.set_diagonal(1, 13, react2)
        level3.diff[1:4] = 0.25 * level2.restricted(level2.diff, 1, 3, coarse2)
        react3[1:4] = level2.restricted(react2, 1, 3, coarse2)
        level3.set_diagonal(1, 4, react3)
    whole2 = [(1, 13)] * 4
    dx = level2.smooth(whole2, DEGREE, SMOOTH_LOW, True, True)
    level2.residual(1, 13, r2, x2, dx)
    f3[1:4] = level2.restricted(r2, 1, 3, coarse2)
    level3.smooth([(1, 4)] * 8, COARSE_DEGREE, COARSE_LOW, True, False)
    fine = table_dot(level3.get(x3, 1, 4), back2[...])
    for t in range(3):
        for j in range(4):
            level2.add_rows(1 + 4 * t + j, fine[t * 8 : t * 8 + 8, j * LANES : (j + 1) * LANES])
    level2.scale_x(1, 13, dx)
    level2.residual(1, 13, r2, x2, dx)
    level2.smooth(whole2, DEGREE, SMOOTH_LOW, False, False)
    return x2


def up_part(place, x2, spaced, tables, centre, kept1, swapped, mate, work0, work1, back0, back1):
    x, r, qa, qb, da, db = work0
    x1, r1, q1a, q1b, d1a, d1b = work1
    clear(*work0[2:])
    clear(*work1[2:])
    slab, core = place[0], place[1]
    for pack in range(3, 9):
        value = x2[1 + pack]
        for j in range(4):
            spaced[4 * pack + j - 12] = pltpu.roll(value, LANES - 32 * j, 1) if j else value
    level1 = Level(
        1, tables[1], kept1.at[2], kept1.at[3], kept1.at[4], kept1.at[1], x1, r1,
        [q1a, q1b], [d1a, d1b],
    )
    level = Level(
        0, tables[0], centre.at[2], centre.at[3], centre.at[4], centre.at[1], x, r,
        [qa, qb], [da, db],
    )
    x1[...] = kept1[0]
    x[...] = centre[0]
    half = lax.broadcasted_iota(jnp.int32, (32, LANES), 1) < 64
    below, above = slab > 0, slab < SLABS - 1
    first_core = core == 0

    def beside(pack, is_below):
        mine, others = (swapped, mate) if is_below else (mate, swapped)
        value = jnp.where(first_core, mine[pack], others[pack])
        return jnp.where(below if is_below else above, value, 0.0)

    x1[1] = beside(0, True)
    x1[2] = jnp.where(half, beside(1, True), x1[2])
    x1[4] = jnp.where(half, x1[4], beside(1, False))
    x1[5] = beside(2, False)
    start = slab % 16 + 2
    fine = table_dot(spaced[pl.ds(start, 5)].reshape(5 * 16, LANES), back1[:, 0:LANES])
    for t in range(5):
        level1.add_rows(1 + t, fine[t * 16 : t * 16 + 16])
    level1.scale_x(1, 6, d1b)
    level1.residual(1, 6, r1, x1, d1b)
    level1.smooth([(1, 6), (2, 5), (2, 5), (2, 5)], DEGREE, SMOOTH_LOW, False, False)
    fine = table_dot(level1.get(x1, 2, 5), back0[...])
    for k in range(8):
        t, j = divmod(2 + k, 4)
        level.add_rows(1 + k, fine[t * 32 : t * 32 + 32, j * LANES : (j + 1) * LANES])
    level.scale_x(1, 9, db)
    level.residual(1, 9, r, x, db)
    level.smooth([(1, 9), (2, 8), (2, 8), (3, 7)], DEGREE, SMOOTH_LOW, False, False)
    return x


def up_kernel(first, place, order, packets, centre_in, kept1_in, swapped_in, mate_in, *refs):
    if first:
        (stencils_in, coarse_in, back_in, applied, lv2, lv3), refs = refs[0:6], refs[6:]
        early, later = [], []
    else:
        (lv2_in, lv3_in, before_in, stencils_in, coarse_in, back_in), refs = refs[0:6], refs[6:]
        (to_block_in, out, lv2, lv3, before, to_block), refs = refs[0:6], refs[6:]
        early = [(lv2_in, lv2), (lv3_in, lv3)]
        later = [(before_in, before), (to_block_in, to_block)]
    (stencils, coarse, back, sems, centre, kept1, swapped, mate), refs = refs[0:8], refs[8:]
    early += [(stencils_in, stencils), (coarse_in.at[2], coarse.at[2]), (back_in, back)]
    later += [
        (kept1_in, kept1), (centre_in, centre.at[:, 1:9]), (swapped_in, swapped), (mate_in, mate)
    ]
    arriving = bring(sems.at[0:6], *early)
    arriving_later = bring(sems.at[6:12], *later)
    clear(centre.at[:, 0], centre.at[:, 9])
    tables = [stencils.at[i] for i in range(4)]
    coarse2, back0, back1, back2 = coarse.at[2], back.at[0], back.at[1], back.at[2]
    f2, f3, react2, react3 = refs[0:4]
    work2, work3, work0, work1, spaced = refs[4:10], refs[10:16], refs[16:22], refs[22:28], refs[28]
    x2 = coarse_part(
        first, arriving, place, order, packets, tables, lv2, lv3, f2, f3, react2, react3, work2, work3, coarse2, back2
    )
    wait(arriving_later)
    x = up_part(
        place, x2, spaced, tables, centre, kept1, swapped, mate, work0, work1, back0, back1
    )
    if first:
        applied[0] = x[3:7]
    else:
        wide = jnp.concatenate([before[k] + x[3 + k] for k in range(4)], axis=1)
        pieces = table_dot(wide, to_block[...], 3)
        for gx in range(4):
            for gy in range(4):
                out[gx * 4 + gy] = pieces[gx * 16 : (gx + 1) * 16, gy * LANES : (gy + 1) * LANES]


def up_first_kernel(*refs):
    up_kernel(True, *refs)


def up_second_kernel(*refs):
    up_kernel(False, *refs)


def row_of_sums(rows):
    stacked = jnp.concatenate(
        [jnp.sum(jnp.sum(a, axis=0), axis=0, keepdims=True) for _, a in rows], axis=0
    )
    totals = jnp.sum(stacked, axis=1, keepdims=True)
    lane = lax.broadcasted_iota(jnp.int32, (1, LANES), 1)
    out = jnp.zeros((1, LANES), F32)
    for i, (lanes, _) in enumerate(rows):
        for at in lanes:
            out = jnp.where(lane == at, totals[i : i + 1], out)
    return out


def gram_kernel(basis, out):
    out[...] = row_of_sums(
        [([8 * j + k, 8 * k + j], basis[j] * basis[k]) for j in range(8) for k in range(j, 8)]
    )


def sums_one_kernel(place, received, basis, gram, applied, out):
    applied[...] = to_blocks(place, received)
    rows = [([64 + k], basis[k] * applied[...]) for k in range(8)]
    rows += [([72], applied[...] * applied[...])]
    out[...] = jnp.broadcast_to((row_of_sums(rows) + gram[...])[None], (SLABS, 1, LANES))


def read_sums(gathered):
    totals = jnp.sum(gathered[...], axis=0)
    row = lax.broadcasted_iota(jnp.int32, (8, LANES), 0)
    lane = lax.broadcasted_iota(jnp.int32, (8, LANES), 1)
    gram = jnp.zeros((8, LANES), F32)
    wide = jnp.broadcast_to(totals, (8, LANES))
    for j in range(8):
        gram = jnp.where(row == j, pltpu.roll(wide, (LANES - 8 * j) % LANES, 1), gram)
    gram = jnp.where(lane < 8, gram, 0.0)
    proj = jnp.where(lane < 8, pltpu.roll(wide, LANES - 64, 1), 0.0)[0:1]
    return gram, proj, totals[:, 72:73]


def column(row_vector):
    row = lax.broadcasted_iota(jnp.int32, (8, LANES), 0)
    lane = lax.broadcasted_iota(jnp.int32, (8, LANES), 1)
    return jnp.sum(jnp.where(row == lane, row_vector, 0.0), axis=1, keepdims=True)


def as_row(column_vector):
    row = lax.broadcasted_iota(jnp.int32, (8, LANES), 0)
    lane = lax.broadcasted_iota(jnp.int32, (8, LANES), 1)
    return jnp.sum(jnp.where(row == lane, column_vector, 0.0), axis=0, keepdims=True)


def times(gram, row_vector):
    return jnp.sum(gram * row_vector, axis=1, keepdims=True)


def dot8(a, b):
    return jnp.sum(a * b, axis=0, keepdims=True)


def finish(gram, proj_two, squares, coeff_one, base, basis, weights_of, out, coefficients):
    coeff_two = proj_two * (1.0 / CELLS)
    quadratic = dot8(coeff_two, times(gram, as_row(coeff_two)))
    mean_square = (squares - 2.0 * dot8(coeff_two, proj_two) + quadratic) * (1.0 / CELLS)
    length = jnp.sqrt(mean_square + 1e-06)
    value = base[...]
    subtract = weights_of(coeff_two)
    for k in range(8):
        value = value - subtract[k : k + 1].reshape(1, 1, 1) * basis[k]
    out[...] = value * (1.0 / length).reshape(1, 1, 1)
    lane = lax.broadcasted_iota(jnp.int32, (1, LANES), 1)
    row = as_row(coeff_one + coeff_two)
    coefficients[...] = jnp.where(lane == 8, length, row)[:, 0:9]


def finish_one_kernel(gathered, basis, applied, out, coefficients, near):
    gram, proj, square = read_sums(gathered)
    one_row = proj * (1.0 / CELLS)
    one, proj = column(one_row), column(proj)
    image = times(gram, one_row)
    proj_two = proj - image
    squares = square - 2.0 * dot8(one, proj) + dot8(one, image)
    near[...] = jnp.where(squares > 0.02 * square, 0.0, 1.0)
    finish(
        gram, proj_two, squares, one, applied, basis, lambda two: one + two, out, coefficients
    )


def sums_two_kernel(gathered, basis, applied, first, out):
    _, proj, _ = read_sums(gathered)
    one = column(proj * (1.0 / CELLS))
    value = applied[...]
    for k in range(8):
        value = value - one[k : k + 1].reshape(1, 1, 1) * basis[k]
    first[...] = value
    sums = row_of_sums([([64 + k], basis[k] * value) for k in range(8)] + [([72], value * value)])
    out[...] = jnp.broadcast_to(sums[None], (SLABS, 1, LANES))


def finish_two_kernel(gathered, gathered_two, basis, first, out, coefficients):
    gram, proj, _ = read_sums(gathered)
    _, proj_two, squares = read_sums(gathered_two)
    one = column(proj * (1.0 / CELLS))
    finish(
        gram, column(proj_two), squares, one, first, basis, lambda two: two, out, coefficients
    )


def swap_all(x):
    return lax.all_to_all(x, AXES, 0, 0, tiled=True)


def halo(own):
    near = lax.ppermute(own, AXES, CHIP_SWAP)
    mate = lax.ppermute(own, AXES, CORE_SWAP)
    near2 = lax.ppermute(mate, AXES, CHIP_SWAP)
    far = lax.ppermute(near, AXES, CORE_SWAP)
    return near, near2, mate, far


def beside(lent):
    return lax.ppermute(lent, AXES, CHIP_SWAP), lax.ppermute(lent, AXES, CORE_SWAP)


def local(basis, diffusion, reaction):
    gx, gy, gz = (lax.axis_index(a) for a in AXES)
    odd = gz % 2
    core = gx % 2
    slab = 16 * gz + 2 * slab_in_group(gx // 2, gy, odd) + core
    place = jnp.stack([slab, core, odd]).astype(jnp.int32)
    order = jnp.asarray(ORDER, jnp.int32)
    stencils = jnp.asarray(np.stack(STENCIL), BF16)
    coarse = jnp.asarray(np.stack(RESTRICT), BF16)
    back = jnp.asarray(np.stack([t.T for t in RESTRICT]), BF16)
    to_slab = jnp.asarray(TO_SLAB, BF16)
    to_block = jnp.asarray(TO_SLAB.T, BF16)
    block = (16, 16, LANES)
    (parts,) = call(
        pack_kernel,
        [("v", (16, 3, 16, LANES))],
        [(3,) + block, DMA((3,))],
        "shhh", place, basis, diffusion, reaction,
    )
    received = lax.all_to_all(parts, ("gx", "gy"), 0, 0, tiled=True)
    (own,) = call(unpack_kernel, [("v", (3, 4, 64, LANES))], [], "vv", received, to_slab)

    big = (W0, 64, LANES)
    small = (W1, 32, LANES)
    two = (W2, 16, LANES)
    three = (W3, 8, LANES)
    mid = (10, 64, LANES)
    lending = ("h", (3, 32, LANES))
    kept = [("h", (5, 8, 64, LANES)), ("h", (5,) + small), lending]
    slab_shape = (4, 64, LANES)
    full, full1, centre, kept1, lent, packet = call(
        down_first_kernel,
        [("h", (4,) + big), ("o", (3,) + small), *kept, ("o", (SLABS, 3, 4, LANES))],
        [(4,) + big, STENCILS, COARSE, DMA((12,)), big, small] + [big] * 6 + [small] * 7,
        "svvvvvhh", place, own, *halo(own), stencils, coarse,
    )
    tables = [STENCILS, COARSE, BACK, DMA((12,))]
    tables += [pltpu.VMEM(s, F32) for s in ((5,) + mid, (5,) + small, (3, 32, LANES), (3, 32, LANES))]
    up_scratch = (
        [two, three, two, three]
        + [two] * 6
        + [three] * 6
        + [mid] * 6
        + [small] * 6
        + [(24, 16, LANES)]
    )
    applied, lv2, lv3 = call(
        up_first_kernel,
        [("v", (1,) + slab_shape), ("o", (3,) + two), ("o", (3,) + three)],
        tables + up_scratch,
        "ssvhhhhhhh",
        place, order, swap_all(packet), centre, kept1, *beside(lent), stencils, coarse, back,
    )
    centre, kept1, lent, before, packet = call(
        down_second_kernel,
        [*kept, ("o", slab_shape), ("o", (SLABS, 1, 4, LANES))],
        [(4,) + big, (3,) + small, STENCILS, COARSE, DMA((11,))] + [big] * 9 + [small] * 7,
        "svvvvvhhhh", place, applied, *halo(applied), full, full1, stencils, coarse,
    )
    (out,) = call(
        up_second_kernel,
        [("v", (16, 16, LANES))],
        [(3,) + two, (3,) + three, slab_shape, pltpu.VMEM((512, 512), BF16)] + tables + up_scratch,
        "ssvhhhhhhhhhhh",
        place, order, swap_all(packet), centre, kept1, *beside(lent), lv2, lv3, before,
        stencils, coarse, back, to_block,
    )
    back = lax.all_to_all(out, ("gx", "gy"), 0, 0, tiled=True)
    row = (1, 9)
    (gram,) = call(gram_kernel, [("v", (1, LANES))], [], "v", basis)
    applied, part = call(
        sums_one_kernel,
        [("v", block), ("v", (SLABS, 1, LANES))],
        [],
        "svvv", place, back, basis, gram,
    )
    gathered = swap_all(part)
    next_vector, coefficients, near = call(
        finish_one_kernel, [("o", block), ("o", row), ("o", (1, 1))], [], "vvv", gathered, basis, applied
    )

    def second_sum():
        first, part = call(
            sums_two_kernel, [("o", block), ("o", (SLABS, 1, LANES))], [], "vvv", gathered, basis, applied
        )
        return tuple(
            call(
                finish_two_kernel, [("o", block), ("o", row)], [], "vvvv",
                gathered, swap_all(part), basis, first,
            )
        )

    next_vector, coefficients = lax.cond(
        near[0, 0] > 0.5, second_sum, lambda: (next_vector, coefficients)
    )
    return next_vector, coefficients.reshape(9)


def solution(mesh):
    placed = (P(None, "gx", "gy", "gz"), P("gx", "gy", "gz"), P("gx", "gy", "gz"))
    return jax.shard_map(
        local, mesh=mesh, in_specs=placed, out_specs=(P("gx", "gy", "gz"), P()), check_vma=False
    )
```
